128 devices in a mesh: shard: 2 (over core), rep: 64 (over x, z, y).
Axes of the slice: x: 4, y: 4, z: 4, core: 2. Of those that a mesh axis runs over, the one named last changes fastest.
Arguments:
- tokens: bfloat16 [16384, 576], P(('shard', 'rep')), may hold values from -6 to 6
- seq_lengths: int32 [2, 4], P('shard'), may hold values from 1 to 8096, as said below
- attn_gain: bfloat16 [2, 576], P(None, 'shard'), may hold values from 0.5 to 1.5
- w_query: bfloat16 [2, 576, 576], P(None, 'shard'), may hold values from -0.25 to 0.25
- key_weight: bfloat16 [2, 576, 192], P(None, 'shard'), may hold values from -0.25 to 0.25
- value_weight: bfloat16 [2, 576, 192], P(None, 'shard'), may hold values from -0.25 to 0.25
- w_out: bfloat16 [2, 576, 576], P(None, 'shard'), may hold values from -6 to 6
- mlp_gain: bfloat16 [2, 576], P(None, 'shard'), may hold values from 0.5 to 1.5
- w_gate: bfloat16 [2, 576, 1536], P(None, 'shard'), may hold values from -0.25 to 0.25
- w_up: bfloat16 [2, 576, 1536], P(None, 'shard'), may hold values from -0.25 to 0.25
- w_down: bfloat16 [2, 1536, 576], P(None, 'shard'), may hold values from -0.15625 to 0.15625
- cotangent: bfloat16 [16384, 576], P(('shard', 'rep')), may hold values from -6 to 6
Outputs:
- activations: bfloat16 [16384, 576], P(('shard', 'rep'))
- grad_tokens: float32 [16384, 576], P(('shard', 'rep'))
- grad_attn_gain: float32 [2, 576], P(None, 'shard')
- grad_w_query: float32 [2, 576, 576], P(None, 'shard')
- grad_w_key: float32 [2, 576, 192], P(None, 'shard')
- grad_w_value: float32 [2, 576, 192], P(None, 'shard')
- grad_w_out: float32 [2, 576, 576], P(None, 'shard')
- grad_mlp_gain: float32 [2, 576], P(None, 'shard')
- grad_w_gate: float32 [2, 576, 1536], P(None, 'shard')
- grad_w_up: float32 [2, 576, 1536], P(None, 'shard')
- grad_w_down: float32 [2, 1536, 576], P(None, 'shard')
The draws below stay inside these ranges and needn't reach their ends.
Inputs may be any that keep to these rules, and one draw needn't show every extreme that they name: `seq_lengths`: each pack holds 4 sequences whose lengths sum to 8192; one of them, at a place drawn from the seed, is exactly 8192 - 3 * (32) long, and the others together hold 3 * (32) tokens.
All inputs are finite; a program needn't handle non-finite values.
Results may differ from the reference program's by a relative error of at most 0.03.
Values may be sent and summed in bfloat16 or wider, within the bound.
A program may use at most 256 MiB of HBM per device.

```python
import math
import jax
import jax.numpy as jnp
from jax import lax

MODEL_WIDTH = 576
QUERY_HEADS = 9
KEY_VALUE_HEADS = 3
HEAD_SIZE = 64
FF = 1536
DECODER_LAYERS = 2
SEQS = 4
TOK_DEV = 128
PACK_TOKENS = 8192
TOKENS = 16384
N_SHARD = 2
N_REP = 64


def draw_seq_lengths(key, part):
    key = jax.random.fold_in(key, 7)
    pack_rows = TOK_DEV * N_REP
    short_total = 3 * (TOK_DEV // 4)
    spare = short_total - 3
    longest = pack_rows - short_total
    first_key, second_key = jax.random.split(key, 2)
    cuts = jax.random.randint(first_key, (N_SHARD, 2), 0, spare + 1)
    lower_cut = jnp.min(cuts, axis=1)
    upper_cut = jnp.max(cuts, axis=1)
    others = jnp.stack([1 + lower_cut, 1 + upper_cut - lower_cut, 1 + spare - upper_cut], axis=1)
    long_place = jax.random.randint(second_key, (N_SHARD, 1), 0, SEQS)
    places = jnp.arange(SEQS, dtype=jnp.int32)[None, :]
    source = jnp.clip(places - (places > long_place).astype(jnp.int32), 0, SEQS - 2)
    picked = jnp.take_along_axis(others, jnp.broadcast_to(source, (N_SHARD, SEQS)), axis=1)
    return jnp.where(places == long_place, longest, picked).astype(jnp.int32)


def level_of(own_key, dims, shards, low, top_value):
    gain, own = 1.0, jax.random.fold_in(own_key, 6)
    for axis_at, shards_of in shards:
        steps = jnp.exp(jax.random.uniform(jax.random.fold_in(own, axis_at), (shards_of,), jnp.float32, low / len(shards), top_value / len(shards)))
        gain = gain * jnp.repeat(steps, dims[axis_at] // shards_of).reshape([-1 if axis == axis_at else 1 for axis in range(len(dims))])
    return gain


def gaussian(rng, extent, scale, bound, cuts=(), kind=jnp.bfloat16):
    drawn = scale * jax.random.normal(rng, extent, jnp.float32)
    if cuts:
        drawn = drawn * level_of(rng, extent, cuts, -0.22, 0.18)
    return jnp.clip(drawn, -bound, bound).astype(kind)


def setup_inputs(seed: int = 0) -> dict:
    key_of = jax.random.split(jax.random.key(seed), 13)
    tokens = gaussian(key_of[0], (TOKENS, MODEL_WIDTH), 1.0, 6.0, ((0, 128),))
    seq_lengths = draw_seq_lengths(jax.random.fold_in(key_of[12], 71), 0)
    attn_gain = jnp.clip(1.0 + 0.1 * jax.random.normal(key_of[2], (DECODER_LAYERS, MODEL_WIDTH), jnp.float32), 0.5, 1.5).astype(jnp.bfloat16)
    w_query = gaussian(key_of[3], (DECODER_LAYERS, MODEL_WIDTH, QUERY_HEADS * HEAD_SIZE), MODEL_WIDTH ** -0.5, 0.25, ((1, 2),))
    key_weight = gaussian(key_of[4], (DECODER_LAYERS, MODEL_WIDTH, KEY_VALUE_HEADS * HEAD_SIZE), MODEL_WIDTH ** -0.5, 0.25, ((1, 2),))
    value_weight = gaussian(key_of[5], (DECODER_LAYERS, MODEL_WIDTH, KEY_VALUE_HEADS * HEAD_SIZE), MODEL_WIDTH ** -0.5, 0.25, ((1, 2),))
    w_out = gaussian(key_of[6], (DECODER_LAYERS, QUERY_HEADS * HEAD_SIZE, MODEL_WIDTH), (max(1, MODEL_WIDTH * 8 // PACK_TOKENS)) ** -0.5, 6.0, ((1, 2),))
    mlp_gain = jnp.clip(1.0 + 0.1 * jax.random.normal(key_of[7], (DECODER_LAYERS, MODEL_WIDTH), jnp.float32), 0.5, 1.5).astype(jnp.bfloat16)
    w_gate = gaussian(key_of[8], (DECODER_LAYERS, MODEL_WIDTH, FF), MODEL_WIDTH ** -0.5, 0.25, ((1, 2),))
    w_up = gaussian(key_of[9], (DECODER_LAYERS, MODEL_WIDTH, FF), MODEL_WIDTH ** -0.5, 0.25, ((1, 2),))
    w_down = gaussian(key_of[10], (DECODER_LAYERS, FF, MODEL_WIDTH), FF ** -0.5, 0.15625, ((1, 2),))
    cotangent = gaussian(key_of[11], (TOKENS, MODEL_WIDTH), 1.0, 6.0, ((0, 128),))
    return dict(tokens=tokens, seq_lengths=seq_lengths, attn_gain=attn_gain, w_query=w_query, key_weight=key_weight, value_weight=value_weight, w_out=w_out, mlp_gain=mlp_gain, w_gate=w_gate, w_up=w_up, w_down=w_down, cotangent=cotangent)


@jax.custom_vjp
def low(v):
    return lax.optimization_barrier(v.astype(jnp.bfloat16)).astype(jnp.float32)

@jax.custom_vjp
def low_back(v):
    return v

def low_keep(v):
    return (low(v), None)

def low_pass(kept, grad):
    return (grad,)

def back_keep(v):
    return (v, None)

def back_low(kept, grad):
    return (low(grad),)
low.defvjp(low_keep, low_pass)
low_back.defvjp(back_keep, back_low)
EPSILON = 1e-05
HIGHEST = lax.Precision.HIGHEST

def matmul(left, right):
    return jnp.dot(left, right, precision=HIGHEST, preferred_element_type=jnp.float32)

def segment_info(lengths, position_index):
    ends = jnp.cumsum(lengths)
    segment_ids = lax.optimization_barrier(jnp.sum((position_index[:, None] >= ends[None, :]).astype(jnp.int32), axis=1))
    starts = ends - lengths
    labels = jnp.arange(lengths.shape[0], dtype=jnp.int32)
    first = lax.optimization_barrier(jnp.sum(jnp.where(segment_ids[:, None] == labels[None, :], starts[None, :], 0), axis=1))
    return (segment_ids, position_index - first)

def rope_tables(position, head_size):
    half = head_size // 2
    freqs = jnp.exp(jnp.arange(half, dtype=jnp.float32) * (-2.0 * math.log(10000.0) / head_size))
    angles = position.astype(jnp.float32)[:, None] * freqs[None, :]
    return (jnp.cos(angles), jnp.sin(angles))

def apply_rotary(value_rows, cosine_table, sine_table):
    half = value_rows.shape[-1] // 2
    first_half = value_rows[..., :half]
    second_half = value_rows[..., half:]
    cosine_table = cosine_table[:, None, :]
    sine_table = sine_table[:, None, :]
    return jnp.concatenate([first_half * cosine_table - second_half * sine_table, second_half * cosine_table + first_half * sine_table], axis=-1)

def rms_norm(hidden, scales):
    inverse = lax.rsqrt(lax.optimization_barrier(jnp.mean(hidden * hidden, axis=-1, keepdims=True)) + EPSILON)
    return hidden * inverse * scales

def packed_attention(arguments):
    query_rows, keys_pack, values_pack, segment_ids, position_index = arguments
    token_rows = query_rows.shape[0]
    block_rows = math.gcd(token_rows, 512)
    blocks = token_rows // block_rows
    scale = 1.0 / math.sqrt(HEAD_SIZE)

    def one_block(inputs):
        query_block, segment_block, index_block = inputs
        scores = low_back(jnp.einsum('tkgd,rkd->tkgr', query_block, keys_pack, precision=HIGHEST)) * scale
        allowed = (segment_ids[None, :] == segment_block[:, None]) & (position_index[None, :] <= index_block[:, None])
        scores = jnp.where(allowed[:, None, None, :], scores, -1e+30)
        largest = lax.optimization_barrier(jnp.max(scores, axis=-1, keepdims=True))
        expon = jnp.exp(scores - largest)
        weights = expon / lax.optimization_barrier(jnp.sum(expon, axis=-1, keepdims=True))
        return jnp.einsum('tkgr,rkd->tkgd', low(weights), values_pack, precision=HIGHEST)
    shaped = query_rows.reshape((blocks, block_rows) + query_rows.shape[1:])
    result = lax.map(jax.checkpoint(one_block), (shaped, segment_ids.reshape(blocks, block_rows), position_index.reshape(blocks, block_rows)))
    return result.reshape(query_rows.shape)

def layer(hidden, attn_scale, w_query, key_weight, value_weight, w_out, mlp_scale, w_gate, w_up, w_down, cosine_table, sine_table, segment_ids, position_index):
    total_sum = hidden.shape[0]
    query_groups = QUERY_HEADS // KEY_VALUE_HEADS
    normed = low(rms_norm(hidden, attn_scale))
    query_proj = low_back(matmul(normed, w_query))
    projected_keys = low_back(matmul(normed, key_weight))
    value_rows = low(low_back(matmul(normed, value_weight)))
    query_rows = low(apply_rotary(query_proj.reshape(total_sum, QUERY_HEADS, HEAD_SIZE), cosine_table, sine_table))
    gathered_keys = low(apply_rotary(projected_keys.reshape(total_sum, KEY_VALUE_HEADS, HEAD_SIZE), cosine_table, sine_table))
    sequence_packs = segment_ids.shape[0]
    attention_output = lax.map(packed_attention, (query_rows.reshape(sequence_packs, PACK_TOKENS, KEY_VALUE_HEADS, query_groups, HEAD_SIZE), gathered_keys.reshape(sequence_packs, PACK_TOKENS, KEY_VALUE_HEADS, HEAD_SIZE), value_rows.reshape(sequence_packs, PACK_TOKENS, KEY_VALUE_HEADS, HEAD_SIZE), segment_ids, position_index))
    attention_output = low(low_back(attention_output.reshape(total_sum, QUERY_HEADS * HEAD_SIZE)))
    middle = hidden + low_back(matmul(attention_output, w_out))
    normed_two = low(rms_norm(middle, mlp_scale))
    gate = low_back(matmul(normed_two, w_gate))
    upward = low_back(matmul(normed_two, w_up))
    inner = low(jax.nn.silu(gate) * upward)
    return middle + low_back(matmul(inner, w_down))

def reference(tokens, seq_lengths, attn_gain, w_query, key_weight, value_weight, w_out, mlp_gain, w_gate, w_up, w_down, cotangent):
    position_index = jnp.arange(PACK_TOKENS, dtype=jnp.int32)
    segment_ids, position = jax.vmap(lambda lengths: segment_info(lengths, position_index))(seq_lengths)
    cosine_table, sine_table = rope_tables(position.reshape(-1), HEAD_SIZE)
    index_all = jnp.broadcast_to(position_index[None, :], segment_ids.shape)
    params = (attn_gain, w_query, key_weight, value_weight, w_out, mlp_gain, w_gate, w_up, w_down)
    params = tuple((item.astype(jnp.float32) for item in params))

    def forward(inputs, *weights):
        hidden = inputs
        for layer_no in range(DECODER_LAYERS):
            picked = tuple((item[layer_no] for item in weights))
            hidden = layer(hidden, *picked, cosine_table, sine_table, segment_ids, index_all)
        return hidden
    output, pullback = jax.vjp(forward, tokens.astype(jnp.float32), *params)
    grads = pullback(cotangent.astype(jnp.float32))
    return (output.astype(jnp.bfloat16), grads[0], grads[1], grads[2], grads[3], grads[4], grads[5], grads[6], grads[7], grads[8], grads[9])
```

```python
import functools
import math

import jax
import jax.numpy as jnp
from jax import lax
from jax.experimental import pallas as pl
from jax.experimental.pallas import tpu as pltpu
from jax.sharding import PartitionSpec as P

QUERY_HEADS = 9
KEY_VALUE_HEADS = 3
HEAD_SIZE = 64
DECODER_LAYERS = 2
MODEL_WIDTH = 576
HALF = 64
EPSILON = 1e-05
LOWEST = -1e30
FLOOR = -1e20

MESH = pl.DeviceIdType.MESH
ANY = pl.BlockSpec(memory_space=pl.ANY)
VMEM = pl.BlockSpec(memory_space=pltpu.VMEM)


def coords():
    rep = lax.axis_index("rep")
    return lax.axis_index("shard"), rep // 16, (rep // 4) % 4, rep % 4


def device(core, x, z, y):
    return (core, x * 16 + z * 4 + y)


def line_peer(axis, step):
    core, x, z, y = coords()
    if axis == "x":
        return device(core, (x + step) % 4, z, y)
    if axis == "z":
        return device(core, x, (z + step) % 4, y)
    return device(core, x, z, (y + step) % 4)


def core_peer():
    core, x, z, y = coords()
    return device(1 - core, x, z, y)


def mirror_peer():
    core, x, z, y = coords()
    return device(core, 3 - x, 3 - z, 3 - y)


def greet(peers):
    barrier = pltpu.get_barrier_semaphore()
    for peer in peers:
        pl.semaphore_signal(barrier, inc=1, device_id=peer, device_id_type=MESH)
    pl.semaphore_wait(barrier, len(peers))


def line_peers(axes):
    return [line_peer(axis, step) for axis in axes for step in (1, 2, 3)]


class Copies:
    def __init__(self, send, recv, local):
        self.send, self.recv, self.local = send, recv, local
        self.remotes, self.locals = 0, 0

    def remote(self, src, dst, peer):
        copy = pltpu.make_async_remote_copy(
            src_ref=src,
            dst_ref=dst,
            send_sem=self.send.at[self.remotes],
            recv_sem=self.recv.at[self.remotes],
            device_id=peer,
            device_id_type=MESH,
        )
        self.remotes += 1
        copy.start()
        return copy

    def here(self, src, dst):
        copy = pltpu.make_async_copy(src, dst, self.local.at[self.locals])
        self.locals += 1
        copy.start()
        return copy


def comm_call(kernel, name, cid, args, outs, in_specs, out_specs, remotes, locals_, scratch=()):
    return pl.pallas_call(
        kernel,
        out_shape=outs,
        in_specs=in_specs,
        out_specs=out_specs,
        scratch_shapes=[
            pltpu.SemaphoreType.DMA((remotes,)),
            pltpu.SemaphoreType.DMA((remotes,)),
            pltpu.SemaphoreType.DMA((max(locals_, 1),)),
            *scratch,
        ],
        compiler_params=pltpu.CompilerParams(
            collective_id=cid, has_side_effects=True, vmem_limit_bytes=56 << 20
        ),
        name=name,
    )(*args)


def shape_of(shape, dtype):
    return jax.ShapeDtypeStruct(shape, dtype)


def start_kernel(weights, *refs):
    tokens, cotangent, gains = refs[:3]
    mine = refs[3 : 3 + weights]
    tokens_out, cotangent_out, gains_out = refs[3 + weights : 6 + weights]
    both = refs[6 + weights : 6 + 2 * weights]
    copies = Copies(*refs[6 + 2 * weights :])
    core = lax.axis_index("shard")
    other, mirror = core_peer(), mirror_peer()
    greet([other, mirror])
    low, high = pl.ds(0, HALF), pl.ds(HALF, HALF)
    started = [copies.remote(tokens.at[high], tokens_out.at[high], mirror)]
    started.append(copies.remote(gains, gains_out.at[core], other))
    for own, all_ in zip(mine, both):
        started.append(copies.remote(own.at[0], all_.at[core], other))
    started.append(copies.remote(cotangent.at[high], cotangent_out.at[high], mirror))
    started.append(copies.here(tokens.at[low], tokens_out.at[low]))
    started.append(copies.here(cotangent.at[low], cotangent_out.at[low]))
    started.append(copies.here(gains, gains_out.at[core]))
    for own, all_ in zip(mine, both):
        started.append(copies.here(own.at[0], all_.at[core]))
    for copy in started:
        copy.wait()


def start(tokens, cotangent, gains, weights):
    outs = [
        shape_of(tokens.shape, tokens.dtype),
        shape_of(cotangent.shape, cotangent.dtype),
        shape_of((2,) + gains.shape, gains.dtype),
        *[shape_of((2,) + w.shape[1:], w.dtype) for w in weights],
    ]
    count = len(weights)
    return comm_call(
        functools.partial(start_kernel, count),
        "start_rows",
        0,
        (tokens, cotangent, gains, *weights),
        outs,
        [ANY] * (3 + count),
        [ANY] * (3 + count),
        3 + count,
        3 + count,
    )


def gather_kernel(layers, *refs):
    weights = len(layers)
    queries, even, odd = refs[:3]
    mine = refs[3 : 3 + weights]
    queries_all, even_all, odd_all = refs[3 + weights : 6 + weights]
    both = refs[6 + weights : 6 + 2 * weights]
    copies = Copies(*refs[6 + 2 * weights :])
    core, x, z, y = coords()
    other = core_peer()
    greet([other, *line_peers("xzy")])
    first_even = [copies.remote(even, even_all.at[z, y], line_peer("y", d)) for d in (1, 2, 3)]
    first_odd = [copies.remote(odd, odd_all.at[y, z], line_peer("z", d)) for d in (1, 2, 3)]
    first_even.append(copies.here(even, even_all.at[z, y]))
    first_odd.append(copies.here(odd, odd_all.at[y, z]))
    rest = [copies.remote(queries, queries_all.at[x], line_peer("x", d)) for d in (1, 2, 3)]
    rest.append(copies.here(queries, queries_all.at[x]))
    for layer, own, all_ in zip(layers, mine, both):
        rest.append(copies.remote(own.at[layer], all_.at[core], other))
        rest.append(copies.here(own.at[layer], all_.at[core]))
    for copy in first_even:
        copy.wait()
    for d in (1, 2, 3):
        rest.append(copies.remote(even_all.at[z], even_all.at[z], line_peer("z", d)))
    for copy in first_odd:
        copy.wait()
    for d in (1, 2, 3):
        rest.append(copies.remote(odd_all.at[y], odd_all.at[y], line_peer("y", d)))
    for copy in rest:
        copy.wait()


def gather(queries, even, odd, weights, layers, cid):
    kv = even.shape[1]
    outs = [
        shape_of((4,) + queries.shape, queries.dtype),
        shape_of((4, 4, HALF, kv), even.dtype),
        shape_of((4, 4, HALF, kv), odd.dtype),
        *[shape_of((2,) + w.shape[1:], w.dtype) for w in weights],
    ]
    count = len(weights)
    return comm_call(
        functools.partial(gather_kernel, tuple(layers)),
        f"gather_qkv_{cid}",
        cid,
        (queries, even, odd, *weights),
        outs,
        [ANY] * (3 + count),
        [ANY] * (3 + count),
        15 + count,
        3 + count,
    )


def unit_places(step):
    x = lax.axis_index("rep") // 16
    in_odd = step >= 4 - x
    section = jnp.where(in_odd, 1, 0)
    quarter = jnp.where(in_odd, step - 1, x + step)
    return section, quarter


def unit_bias(section, quarter, starts_ref):
    rep = lax.axis_index("rep")
    x, line = rep // 16, rep % 16
    row = lax.broadcasted_iota(jnp.int32, (1024, 128), 0)
    block, inside = row // HALF, row % HALF
    even_key = (16 * x + block) * 128 + inside
    odd_key = (127 - 2 * (16 * x + (block % 4) * 4 + block // 4)) * HALF + inside
    key = jnp.where(section == 1, odd_key, even_key)
    lane = lax.broadcasted_iota(jnp.int32, (1, 128), 1)
    even_query = (16 * quarter + line) * 128 + lane
    odd_query = (127 - 2 * (16 * (3 - quarter) + line)) * HALF + lane - HALF
    query = jnp.where(lane < HALF, even_query, odd_query)
    begin = jnp.where(
        lane < HALF, starts_ref[pl.ds(quarter, 1), :], starts_ref[pl.ds(3 - quarter, 1), :]
    )
    return jnp.where((key <= query) & (key >= begin), 0.0, LOWEST)


def head_rows(ref, quarter, group):
    parts = []
    for head in range(3 * group, 3 * group + 3):
        columns = slice(head * HEAD_SIZE, (head + 1) * HEAD_SIZE)
        parts.append(ref[quarter, 0:HALF, columns])
        parts.append(ref[3 - quarter, HALF : 2 * HALF, columns])
    return jnp.concatenate(parts, axis=0)


def contract(left, right, left_dim, right_dim):
    return lax.dot_general(
        left, right, (((left_dim,), (right_dim,)), ((), ())), preferred_element_type=jnp.float32
    )


def attend_kernel(q_ref, even_ref, odd_ref, starts_ref, o_ref, lse_ref, bias, best, total, accum):
    best[...] = jnp.full(best.shape, FLOOR, jnp.float32)
    total[...] = jnp.zeros(total.shape, jnp.float32)
    accum[...] = jnp.zeros(accum.shape, jnp.float32)

    def unit(section, quarter, kv_ref):
        bias[...] = unit_bias(section, quarter, starts_ref)
        for group in range(3):
            queries = head_rows(q_ref, quarter, group)
            keys = kv_ref[:, group * 128 : group * 128 + 64]
            values = kv_ref[:, group * 128 + 64 : group * 128 + 128]
            scores = contract(keys, queries, 1, 1)
            tile = bias[...]
            scores = scores + jnp.concatenate([tile, tile, tile], axis=1)
            old = best[quarter, group]
            new = jnp.maximum(old, jnp.max(scores, axis=0, keepdims=True))
            expon = jnp.exp(scores - new)
            decay = jnp.exp(old - new)
            best[quarter, group] = new
            total[quarter, group] = total[quarter, group] * decay + jnp.sum(
                expon, axis=0, keepdims=True
            )
            accum[quarter, group] = accum[quarter, group] * decay + contract(
                values, expon.astype(jnp.bfloat16), 0, 0
            )

    def step_body(step, carry):
        section, quarter = unit_places(step)

        @pl.when(section == 0)
        def _():
            unit(section, quarter, even_ref)

        @pl.when(section == 1)
        def _():
            unit(section, quarter, odd_ref)

        return carry

    lax.fori_loop(0, 5, step_body, 0)
    lane = lax.broadcasted_iota(jnp.int32, (1, 128), 1)
    results, logs = {}, {}
    for quarter in range(4):
        for group in range(3):
            summed = total[quarter, group]
            safe = jnp.where(summed > 0.0, summed, 1.0)
            results[quarter, group] = accum[quarter, group] / safe
            logs[quarter, group] = best[quarter, group] + jnp.log(safe)
    for chunk in range(4):
        rows = []
        for head in range(QUERY_HEADS):
            group, part = head // 3, slice((head % 3) * 128, (head % 3) * 128 + 128)
            o_ref[chunk, head * 64 : head * 64 + 64, :] = jnp.where(
                lane < HALF, results[chunk, group][:, part], results[3 - chunk, group][:, part]
            ).astype(jnp.bfloat16)
            rows.append(
                jnp.where(lane < HALF, logs[chunk, group][:, part], logs[3 - chunk, group][:, part])
            )
        rows.append(jnp.zeros((7, 128), jnp.float32))
        lse_ref[chunk] = jnp.concatenate(rows, axis=0)


def attend(queries, even, odd, starts):
    return pl.pallas_call(
        attend_kernel,
        out_shape=[
            shape_of((4, MODEL_WIDTH, 128), jnp.bfloat16),
            shape_of((4, 16, 128), jnp.float32),
        ],
        in_specs=[VMEM] * 4,
        out_specs=[VMEM] * 2,
        scratch_shapes=[
            pltpu.VMEM((1024, 128), jnp.float32),
            pltpu.VMEM((4, 3, 1, 384), jnp.float32),
            pltpu.VMEM((4, 3, 1, 384), jnp.float32),
            pltpu.VMEM((4, 3, 64, 384), jnp.float32),
        ],
        compiler_params=pltpu.CompilerParams(vmem_limit_bytes=56 << 20),
        name="attend",
    )(queries, even.reshape(1024, 384), odd.reshape(1024, 384), starts)


def merge_kernel(o_ref, lse_ref, o_all, lse_all, send, recv, local):
    copies = Copies(send, recv, local)
    _, x, _, _ = coords()
    greet(line_peers("x"))
    started = []
    for d in (1, 2, 3):
        peer = (x + d) % 4
        started.append(copies.remote(o_ref.at[peer], o_all.at[x], line_peer("x", d)))
        started.append(copies.remote(lse_ref.at[peer], lse_all.at[x], line_peer("x", d)))
    started.append(copies.here(o_ref.at[x], o_all.at[x]))
    started.append(copies.here(lse_ref.at[x], lse_all.at[x]))
    for copy in started:
        copy.wait()


def exchange_partials(partial, logs, cid):
    return comm_call(
        merge_kernel,
        f"swap_partials_{cid}",
        cid,
        (partial, logs),
        [shape_of(partial.shape, partial.dtype), shape_of(logs.shape, logs.dtype)],
        [ANY] * 2,
        [ANY] * 2,
        6,
        2,
    )


def back_gather_kernel(halves, wholes, *refs):
    count = halves + wholes
    grads, stats = refs[:2]
    mine = refs[2 : 2 + count]
    grads_all, stats_all = refs[2 + count : 4 + count]
    both = refs[4 + count : 4 + 2 * count]
    copies = Copies(*refs[4 + 2 * count :])
    core, x, _, _ = coords()
    other = core_peer()
    greet([other, *line_peers("x")])
    started = []
    for d in (1, 2, 3):
        started.append(copies.remote(grads, grads_all.at[x], line_peer("x", d)))
        started.append(copies.remote(stats, stats_all.at[x], line_peer("x", d)))
    started.append(copies.here(grads, grads_all.at[x]))
    started.append(copies.here(stats, stats_all.at[x]))
    for at, (own, all_) in enumerate(zip(mine, both)):
        if at < halves:
            started.append(copies.remote(own.at[1 - core], all_.at[core], other))
            started.append(copies.here(own.at[core], all_.at[core]))
        else:
            started.append(copies.remote(own, all_.at[core], other))
            started.append(copies.here(own, all_.at[core]))
    for copy in started:
        copy.wait()


def back_gather(grads, stats, halves, wholes, cid):
    count = len(halves) + len(wholes)
    return comm_call(
        functools.partial(back_gather_kernel, len(halves), len(wholes)),
        f"gather_grads_{cid}",
        cid,
        (grads, stats, *halves, *wholes),
        [
            shape_of((4,) + grads.shape, grads.dtype),
            shape_of((4,) + stats.shape, stats.dtype),
            *[shape_of(item.shape, item.dtype) for item in halves],
            *[shape_of((2,) + item.shape, item.dtype) for item in wholes],
        ],
        [ANY] * (2 + count),
        [ANY] * (2 + count),
        6 + count,
        2 + count,
    )


def attend_back_kernel(
    q_ref, even_ref, odd_ref, do_ref, stats_ref, starts_ref, dq_ref, dkv_ref, bias, dq, dkv
):
    dq[...] = jnp.zeros(dq.shape, jnp.float32)
    dkv[...] = jnp.zeros(dkv.shape, jnp.float32)

    def unit(section, quarter, kv_ref):
        bias[...] = unit_bias(section, quarter, starts_ref)
        lane = lax.broadcasted_iota(jnp.int32, (1, 128), 1)
        stats = jnp.where(lane < HALF, stats_ref[quarter], stats_ref[3 - quarter])
        for group in range(3):
            queries = head_rows(q_ref, quarter, group)
            grads = head_rows(do_ref, quarter, group)
            keys = kv_ref[:, group * 128 : group * 128 + 64]
            values = kv_ref[:, group * 128 + 64 : group * 128 + 128]
            heads = range(3 * group, 3 * group + 3)
            logs = jnp.concatenate([stats[0, h : h + 1, :] for h in heads], axis=1)
            delta = jnp.concatenate([stats[1, h : h + 1, :] for h in heads], axis=1)
            scores = contract(keys, queries, 1, 1)
            tile = bias[...]
            scores = scores + jnp.concatenate([tile, tile, tile], axis=1)
            weights = jnp.exp(scores - logs)
            grad_weights = contract(values, grads, 1, 1)
            grad_scores = (weights * (grad_weights - delta)).astype(jnp.bfloat16)
            grad_values = contract(weights.astype(jnp.bfloat16), grads, 1, 0)
            grad_keys = contract(grad_scores, queries, 1, 0)
            dkv[section, group] += jnp.concatenate([grad_keys, grad_values], axis=1)
            dq[quarter, group] += contract(keys, grad_scores, 0, 0)

    def step_body(step, carry):
        section, quarter = unit_places(step)

        @pl.when(section == 0)
        def _():
            unit(section, quarter, even_ref)

        @pl.when(section == 1)
        def _():
            unit(section, quarter, odd_ref)

        return carry

    lax.fori_loop(0, 5, step_body, 0)
    lane = lax.broadcasted_iota(jnp.int32, (1, 128), 1)
    for chunk in range(4):
        for head in range(QUERY_HEADS):
            group, part = head // 3, slice((head % 3) * 128, (head % 3) * 128 + 128)
            picked = jnp.where(
                lane < HALF, dq[chunk, group][:, part], dq[3 - chunk, group][:, part]
            )
            dq_ref[chunk, head * 64 : head * 64 + 64, :] = (picked * 0.125).astype(jnp.bfloat16)
    for section in range(2):
        for group in range(3):
            dkv_ref[section, :, group * 128 : group * 128 + 128] = dkv[section, group].astype(
                jnp.bfloat16
            )


def attend_back(queries, even, odd, grads, stats, starts):
    return pl.pallas_call(
        attend_back_kernel,
        out_shape=[
            shape_of((4, MODEL_WIDTH, 128), jnp.bfloat16),
            shape_of((2, 1024, 384), jnp.bfloat16),
        ],
        in_specs=[VMEM] * 6,
        out_specs=[VMEM] * 2,
        scratch_shapes=[
            pltpu.VMEM((1024, 128), jnp.float32),
            pltpu.VMEM((4, 3, 64, 384), jnp.float32),
            pltpu.VMEM((2, 3, 1024, 128), jnp.float32),
        ],
        compiler_params=pltpu.CompilerParams(vmem_limit_bytes=56 << 20),
        name="attend_back",
    )(queries, even.reshape(1024, 384), odd.reshape(1024, 384), grads, stats, starts)


def back_sum_kernel(dq_ref, dkv_ref, dq_out, dkv_out, send, recv, local, dq_in, first, middle, second):
    copies = Copies(send, recv, local)
    _, x, z, y = coords()
    greet(line_peers("xzy"))
    stage_one = [[], []]
    dq_copies = []
    for d in (1, 2, 3):
        stage_one[0].append(
            copies.remote(dkv_ref.at[0, (z + d) % 4], first.at[0, d - 1], line_peer("z", d))
        )
        stage_one[1].append(
            copies.remote(dkv_ref.at[1, (y + d) % 4], first.at[1, d - 1], line_peer("y", d))
        )
    for d in (1, 2, 3):
        dq_copies.append(copies.remote(dq_ref.at[(x + d) % 4], dq_in.at[d - 1], line_peer("x", d)))
    stage_two = [[], []]
    for half, mine, axis, there in ((0, z, "y", y), (1, y, "z", z)):
        for copy in stage_one[half]:
            copy.wait()
        total = dkv_ref[half, mine].astype(jnp.float32)
        for d in range(3):
            total = total + first[half, d].astype(jnp.float32)
        middle[half] = total.astype(jnp.bfloat16)
        for d in (1, 2, 3):
            stage_two[half].append(
                copies.remote(
                    middle.at[half, (there + d) % 4], second.at[half, d - 1], line_peer(axis, d)
                )
            )
    for copy in dq_copies:
        copy.wait()
    total = dq_ref[x].astype(jnp.float32)
    for d in range(3):
        total = total + dq_in[d].astype(jnp.float32)
    dq_out[...] = total
    for half, there in ((0, y), (1, z)):
        for copy in stage_two[half]:
            copy.wait()
        total = middle[half, there].astype(jnp.float32)
        for d in range(3):
            total = total + second[half, d].astype(jnp.float32)
        dkv_out[half * HALF : (half + 1) * HALF, :] = total


def back_sum(dq, dkv, cid):
    return comm_call(
        back_sum_kernel,
        f"sum_dqkv_{cid}",
        cid,
        (dq, dkv.reshape(2, 4, 4, HALF, 384)),
        [shape_of((MODEL_WIDTH, 128), jnp.float32), shape_of((128, 384), jnp.float32)],
        [VMEM] * 2,
        [VMEM] * 2,
        15,
        1,
        [
            pltpu.VMEM((3, MODEL_WIDTH, 128), jnp.bfloat16),
            pltpu.VMEM((2, 3, 4, HALF, 384), jnp.bfloat16),
            pltpu.VMEM((2, 4, HALF, 384), jnp.bfloat16),
            pltpu.VMEM((2, 3, HALF, 384), jnp.bfloat16),
        ],
    )


def pair_kernel(qkv, gains, qkv_all, gains_all, send, recv, local):
    copies = Copies(send, recv, local)
    core = lax.axis_index("shard")
    other = core_peer()
    greet([other])
    started = [
        copies.remote(qkv, qkv_all.at[core], other),
        copies.remote(gains.at[1 - core], gains_all.at[core], other),
        copies.here(qkv, qkv_all.at[core]),
        copies.here(gains.at[core], gains_all.at[core]),
    ]
    for copy in started:
        copy.wait()


def pair_exchange(qkv, gains, cid):
    return comm_call(
        pair_kernel,
        f"swap_cores_{cid}",
        cid,
        (qkv, gains),
        [shape_of((2,) + qkv.shape, qkv.dtype), shape_of(gains.shape, gains.dtype)],
        [ANY] * 2,
        [ANY] * 2,
        2,
        2,
    )


GRAD_ROWS = 1216
PIECE = GRAD_ROWS // 4


def weight_grad_kernel(
    normed, attended, normed_two, inner, branch, gate, up, middle, qkv, gains, out
):
    def rows(ref):
        return ref[...].reshape(ref.shape[0] * ref.shape[1], ref.shape[2])

    grad_qkv = contract(rows(normed), rows(qkv), 0, 0)
    grad_out = contract(rows(attended), rows(middle), 0, 0)
    out[0:288, :] = jnp.concatenate([grad_qkv, grad_out], axis=1).astype(jnp.bfloat16)
    two = rows(normed_two)
    out[288:576, :] = contract(two, rows(gate), 0, 0).astype(jnp.bfloat16)
    out[576:864, :] = contract(two, rows(up), 0, 0).astype(jnp.bfloat16)
    down = contract(rows(branch), rows(inner), 0, 0).astype(jnp.bfloat16)
    out[864:1152, 0:768] = down[0:288]
    out[864:1152, 768:1536] = down[288:576]
    out[1152:GRAD_ROWS, :] = jnp.zeros((GRAD_ROWS - 1152, 1536), jnp.bfloat16)
    out[1152:1168, 0:384] = (gains[0] + gains[1]).astype(jnp.bfloat16)


def weight_grads(*args):
    return pl.pallas_call(
        weight_grad_kernel,
        out_shape=shape_of((GRAD_ROWS, 1536), jnp.bfloat16),
        in_specs=[VMEM] * len(args),
        out_specs=VMEM,
        compiler_params=pltpu.CompilerParams(vmem_limit_bytes=56 << 20),
        name="weight_grads",
    )(*args)


def reduce_kernel(g_ref, out_ref, send, recv, local, one, sum_one, two, three):
    copies = Copies(send, recv, local)
    _, x, z, y = coords()
    place = {"x": x, "z": z, "y": y}
    orders = ("xzy", "zyx", "yxz")
    greet(line_peers("xzy"))

    def columns(part, at):
        return pl.ds(pl.multiple_of(part * 512 + at * 128, 128), 128)

    def rows(at):
        return pl.ds(pl.multiple_of(at * PIECE, 16), PIECE)

    stages = [[], [], []]
    for part, order in enumerate(orders):
        axis = order[0]
        for d in (1, 2, 3):
            stages[part].append(
                copies.remote(
                    g_ref.at[:, columns(part, (place[axis] + d) % 4)],
                    one.at[part, d - 1],
                    line_peer(axis, d),
                )
            )
    for part, order in enumerate(orders):
        for copy in stages[part]:
            copy.wait()
        total = g_ref[:, columns(part, place[order[0]])].astype(jnp.float32)
        for d in range(3):
            total = total + one[part, d].astype(jnp.float32)
        sum_one[part] = total.astype(jnp.bfloat16)
        axis = order[1]
        stages[part] = [
            copies.remote(
                sum_one.at[part, rows((place[axis] + d) % 4)],
                two.at[part, d - 1],
                line_peer(axis, d),
            )
            for d in (1, 2, 3)
        ]
    for part, order in enumerate(orders):
        for copy in stages[part]:
            copy.wait()
        total = sum_one[part, rows(place[order[1]])].astype(jnp.float32)
        for d in range(3):
            total = total + two[part, d].astype(jnp.float32)
        axis = order[2]
        here = place[axis]
        three[part, here] = total.astype(jnp.bfloat16)
        stages[part] = [
            copies.remote(three.at[part, here], three.at[part, here], line_peer(axis, d))
            for d in (1, 2, 3)
        ]
    for part, order in enumerate(orders):
        for copy in stages[part]:
            copy.wait()
        total = three[part, 0].astype(jnp.float32)
        for at in (1, 2, 3):
            total = total + three[part, at].astype(jnp.float32)
        window = (rows(place[order[1]]), columns(part, place[order[0]]))
        out_ref[window] = total.astype(jnp.bfloat16)
        stages[part] = [
            copies.remote(out_ref.at[window], out_ref.at[window], line_peer(order[1], d))
            for d in (1, 2, 3)
        ]
    for part, order in enumerate(orders):
        for copy in stages[part]:
            copy.wait()
        window = (slice(None), columns(part, place[order[0]]))
        stages[part] = [
            copies.remote(out_ref.at[window], out_ref.at[window], line_peer(order[0], d))
            for d in (1, 2, 3)
        ]
    for part in range(3):
        for copy in stages[part]:
            copy.wait()


def reduce_grads(grads, cid):
    return comm_call(
        reduce_kernel,
        f"sum_weight_grads_{cid}",
        cid,
        (grads,),
        shape_of(grads.shape, grads.dtype),
        [VMEM],
        VMEM,
        45,
        1,
        [
            pltpu.VMEM((3, 3, GRAD_ROWS, 128), jnp.bfloat16),
            pltpu.VMEM((3, GRAD_ROWS, 128), jnp.bfloat16),
            pltpu.VMEM((3, 3, PIECE, 128), jnp.bfloat16),
            pltpu.VMEM((3, 4, PIECE, 128), jnp.bfloat16),
        ],
    )


def finish_kernel(acts, grads, acts_out, grads_out, send, recv, local):
    copies = Copies(send, recv, local)
    mirror = mirror_peer()
    greet([mirror])
    low, high = pl.ds(0, HALF), pl.ds(HALF, HALF)
    started = [
        copies.remote(grads.at[high], grads_out.at[high], mirror),
        copies.remote(acts.at[high], acts_out.at[high], mirror),
        copies.here(grads.at[low], grads_out.at[low]),
        copies.here(acts.at[low], acts_out.at[low]),
    ]
    for copy in started:
        copy.wait()


def finish(acts, grads, cid):
    return comm_call(
        finish_kernel,
        "return_rows",
        cid,
        (acts, grads),
        [shape_of(acts.shape, acts.dtype), shape_of(grads.shape, grads.dtype)],
        [ANY] * 2,
        [ANY] * 2,
        2,
        2,
    )


def sequence_starts(lengths, rows):
    ends = jnp.cumsum(lengths)
    begins = ends - lengths
    segment = jnp.sum((rows[..., None] >= ends).astype(jnp.int32), axis=-1)
    labels = jnp.arange(lengths.shape[0], dtype=jnp.int32)
    return jnp.sum(jnp.where(segment[..., None] == labels, begins, 0), axis=-1)


def rope_tables(position):
    half = HEAD_SIZE // 2
    freqs = jnp.exp(jnp.arange(half, dtype=jnp.float32) * (-2.0 * math.log(10000.0) / HEAD_SIZE))
    angles = position.astype(jnp.float32)[:, None] * freqs[None, :]
    return jnp.cos(angles), jnp.sin(angles)


def rope(rows, tables, sign):
    cosine, sine = tables
    half = HEAD_SIZE // 2
    shaped = rows.reshape(rows.shape[0], -1, HEAD_SIZE)
    one, two = shaped[..., :half], shaped[..., half:]
    cosine, sine = cosine[:, None, :], sign * sine[:, None, :]
    return jnp.concatenate(
        [one * cosine - two * sine, two * cosine + one * sine], axis=-1
    ).reshape(rows.shape)


def dot(left, right):
    return jnp.dot(left, right, preferred_element_type=jnp.float32)


def dot_t(left, right):
    return jnp.einsum("ta,ba->tb", left, right, preferred_element_type=jnp.float32)


def inverse_rms(rows):
    return lax.rsqrt(jnp.mean(rows * rows, axis=-1, keepdims=True) + EPSILON)


def norm_back(grad, rows, inverse, gain):
    scaled = grad * gain
    return inverse * scaled - rows * inverse**3 * jnp.mean(scaled * rows, axis=-1, keepdims=True)


def halves_of(rows):
    count, width = rows.shape
    return rows.reshape(count, 2, width // 2).transpose(1, 0, 2)


def whole(pair):
    return pair.reshape(pair.shape[0] * pair.shape[1], pair.shape[2])


def per_device(
    tokens,
    seq_lengths,
    attn_gain,
    w_query,
    key_weight,
    value_weight,
    w_out,
    mlp_gain,
    w_gate,
    w_up,
    w_down,
    cotangent,
):
    lengths = seq_lengths[0]
    rep = lax.axis_index("rep")
    x, line = rep // 16, rep % 16
    inside = jnp.arange(128, dtype=jnp.int32)
    chunk = jnp.arange(4, dtype=jnp.int32)[:, None] * 16 + line
    rows_all = jnp.where(
        inside[None, :] < HALF,
        chunk * 128 + inside[None, :],
        (127 - 2 * chunk) * HALF + inside[None, :] - HALF,
    )
    starts = sequence_starts(lengths, rows_all)
    position = jnp.where(
        inside < HALF, rep * 128 + inside, (127 - 2 * rep) * HALF + inside - HALF
    ) - sequence_starts(
        lengths,
        jnp.where(inside < HALF, rep * 128 + inside, (127 - 2 * rep) * HALF + inside - HALF),
    )
    tables = rope_tables(position)
    gains = jnp.pad(jnp.concatenate([attn_gain, mlp_gain]), ((0, 12), (0, 96)))
    tokens, cotangent, gains, *first = start(
        tokens, cotangent, gains, (w_query, key_weight, value_weight)
    )
    gains = jnp.concatenate([gains[0, :4, :288], gains[1, :4, :288]], axis=1).astype(jnp.float32)
    projections = [[whole(item) for item in first], None]
    later = [None, None]

    hidden = tokens.astype(jnp.float32)
    kept = []
    for layer in range(DECODER_LAYERS):
        wq, wk, wv = projections[layer]
        inv_one = inverse_rms(hidden)
        normed = (hidden * inv_one * gains[layer]).astype(jnp.bfloat16)
        queries = rope(dot(normed, wq), tables, 1.0).astype(jnp.bfloat16) * 0.125
        keys = rope(dot(normed, wk), tables, 1.0).astype(jnp.bfloat16)
        values = dot(normed, wv).astype(jnp.bfloat16)
        joined = jnp.concatenate(
            [keys.reshape(128, 3, 64), values.reshape(128, 3, 64)], axis=-1
        ).reshape(128, 384)
        weights = [w_out, w_gate, w_up, w_down]
        layers = [layer] * 4
        if layer == 0:
            weights += [w_query, key_weight, value_weight]
            layers += [1] * 3
        queries_all, even, odd, *got = gather(
            queries, joined[:HALF], joined[HALF:], weights, layers, 1 + layer
        )
        got = [whole(item) for item in got]
        later[layer] = got[:4]
        if layer == 0:
            projections[1] = got[4:]
        wo, wg, wu, wd = later[layer]
        partial, logs = attend(queries_all, even, odd, starts)
        partial, logs = exchange_partials(partial, logs, 3 + layer)
        largest = jnp.max(logs, axis=0)
        shares = jnp.exp(logs - largest)
        total = jnp.sum(shares, axis=0)
        lse = largest + jnp.log(total)
        shares = (shares / total)[:, :QUERY_HEADS, None, :]
        outcome = jnp.sum(
            shares * partial.reshape(4, QUERY_HEADS, HEAD_SIZE, 128).astype(jnp.float32), axis=0
        )
        attended = outcome.reshape(MODEL_WIDTH, 128).astype(jnp.bfloat16).T
        middle = hidden + dot(attended, wo)
        inv_two = inverse_rms(middle)
        normed_two = (middle * inv_two * gains[2 + layer]).astype(jnp.bfloat16)
        gate = dot(normed_two, wg)
        up = dot(normed_two, wu)
        inner = (jax.nn.silu(gate) * up).astype(jnp.bfloat16)
        kept.append(
            (
                hidden,
                inv_one,
                normed,
                queries_all,
                even,
                odd,
                lse,
                outcome,
                attended,
                middle,
                inv_two,
                normed_two,
                gate,
                up,
                inner,
            )
        )
        hidden = middle + dot(inner, wd)
    activations = hidden.astype(jnp.bfloat16)

    grad = cotangent.astype(jnp.float32)
    collected = [None, None]
    for layer in (1, 0):
        (
            hidden,
            inv_one,
            normed,
            queries_all,
            even,
            odd,
            lse,
            outcome,
            attended,
            middle,
            inv_two,
            normed_two,
            gate,
            up,
            inner,
        ) = kept[layer]
        wq, wk, wv = projections[layer]
        wo, wg, wu, wd = later[layer]
        branch = grad.astype(jnp.bfloat16)
        grad_inner = dot_t(branch, wd)
        sigma = jax.nn.sigmoid(gate)
        grad_gate = (grad_inner * up * sigma * (1.0 + gate * (1.0 - sigma))).astype(jnp.bfloat16)
        grad_up = (grad_inner * gate * sigma).astype(jnp.bfloat16)
        grad_normed_two = dot_t(grad_gate, wg) + dot_t(grad_up, wu)
        grad_mlp_gain = jnp.sum(middle * inv_two * grad_normed_two, axis=0)
        grad_middle = grad + norm_back(grad_normed_two, middle, inv_two, gains[2 + layer])
        attn_branch = grad_middle.astype(jnp.bfloat16)
        grad_attended = dot_t(attn_branch, wo).astype(jnp.bfloat16)
        delta = jnp.sum(
            grad_attended.astype(jnp.float32).T.reshape(QUERY_HEADS, HEAD_SIZE, 128) * outcome,
            axis=1,
        )
        stats = jnp.stack([lse, jnp.pad(delta, ((0, 7), (0, 0)))])
        grads_all, stats_all, *swapped = back_gather(
            grad_attended,
            stats,
            [halves_of(item) for item in (normed, attended, normed_two, inner)],
            [branch, grad_gate, grad_up, attn_branch],
            5 + layer,
        )
        dq, dkv = attend_back(queries_all, even, odd, grads_all, stats_all, starts)
        dq, dkv = back_sum(dq, dkv, 7 + layer)
        dkv = dkv.reshape(128, 3, 128)
        grad_qp = rope(dq.T, tables, -1.0).astype(jnp.bfloat16)
        grad_kp = rope(dkv[:, :, :64].reshape(128, 192), tables, -1.0).astype(jnp.bfloat16)
        grad_vp = dkv[:, :, 64:].reshape(128, 192).astype(jnp.bfloat16)
        grad_normed = dot_t(grad_qp, wq) + dot_t(grad_kp, wk) + dot_t(grad_vp, wv)
        grad_attn_gain = jnp.sum(hidden * inv_one * grad_normed, axis=0)
        grad = grad_middle + norm_back(grad_normed, hidden, inv_one, gains[layer])
        gain_grads = jnp.pad(
            jnp.stack([grad_attn_gain, grad_mlp_gain]).reshape(2, 2, 288).transpose(1, 0, 2),
            ((0, 0), (0, 14), (0, 96)),
        )
        grad_qkv, gain_grads = pair_exchange(
            jnp.concatenate([grad_qp, grad_kp, grad_vp], axis=1), gain_grads, 9 + layer
        )
        summed = weight_grads(*swapped, grad_qkv, gain_grads)
        collected[layer] = reduce_grads(summed, 11 + layer)

    activations, grad = finish(activations, grad, 13)
    both = [item.astype(jnp.float32) for item in collected]

    def stacked(pick):
        return jnp.stack([pick(item) for item in both])

    return (
        activations,
        grad,
        stacked(lambda g: g[1152, :288]),
        stacked(lambda g: g[0:288, 0:576]),
        stacked(lambda g: g[0:288, 576:768]),
        stacked(lambda g: g[0:288, 768:960]),
        stacked(lambda g: g[0:288, 960:1536]),
        stacked(lambda g: g[1153, :288]),
        stacked(lambda g: g[288:576]),
        stacked(lambda g: g[576:864]),
        stacked(lambda g: jnp.concatenate([g[864:1152, :768], g[864:1152, 768:]], axis=0).T),
    )


def solution(mesh):
    rows = P(("shard", "rep"), None)
    gain, weight = P(None, "shard"), P(None, "shard", None)
    return jax.shard_map(
        per_device,
        mesh=mesh,
        in_specs=(
            rows,
            P("shard", None),
            gain,
            weight,
            weight,
            weight,
            weight,
            gain,
            weight,
            weight,
            weight,
            rows,
        ),
        out_specs=(
            rows,
            rows,
            gain,
            weight,
            weight,
            weight,
            weight,
            gain,
            weight,
            weight,
            weight,
        ),
        check_vma=False,
    )
```

```python
import functools
import math
from types import SimpleNamespace

import jax
import jax.numpy as jnp
from jax import lax
from jax.experimental import pallas as pl
from jax.experimental.pallas import tpu as pltpu
from jax.sharding import PartitionSpec as P

QUERY_HEADS = 9
KEY_VALUE_HEADS = 3
HEAD_SIZE = 64
DECODER_LAYERS = 2
MODEL_WIDTH = 576
HALF = 64
EPSILON = 1e-05
LOWEST = -1e30
FLOOR = -1e20

MESH = pl.DeviceIdType.MESH
ANY = pl.BlockSpec(memory_space=pl.ANY)
VMEM = pl.BlockSpec(memory_space=pltpu.VMEM)


def coords():
    rep = lax.axis_index("rep")
    return lax.axis_index("shard"), rep // 16, (rep // 4) % 4, rep % 4


def device(core, x, z, y):
    return (core, x * 16 + z * 4 + y)


def line_peer(axis, step):
    core, x, z, y = coords()
    if axis == "x":
        return device(core, (x + step) % 4, z, y)
    if axis == "z":
        return device(core, x, (z + step) % 4, y)
    return device(core, x, z, (y + step) % 4)


def core_peer():
    core, x, z, y = coords()
    return device(1 - core, x, z, y)


def mirror_peer():
    core, x, z, y = coords()
    return device(core, 3 - x, 3 - z, 3 - y)


def greet(peers):
    barrier = pltpu.get_barrier_semaphore()
    for peer in peers:
        pl.semaphore_signal(barrier, inc=1, device_id=peer, device_id_type=MESH)
    pl.semaphore_wait(barrier, len(peers))


def line_peers(axes):
    return [line_peer(axis, step) for axis in axes for step in (1, 2, 3)]


def named_call(body, name, cid, ins, outs, scratch):
    keys = [*ins, *outs, *scratch]

    def kernel(*refs):
        sems = refs[len(keys) :]
        body(SimpleNamespace(**dict(zip(keys, refs))), Copies(*sems))

    results = pl.pallas_call(
        kernel,
        out_shape=[shape_of(shape, dtype) for shape, dtype, _ in outs.values()],
        in_specs=[spec for _, spec in ins.values()],
        out_specs=[spec for _, _, spec in outs.values()],
        scratch_shapes=[
            *[pltpu.VMEM(shape, dtype) for shape, dtype in scratch.values()],
            pltpu.SemaphoreType.DMA((112,)),
            pltpu.SemaphoreType.DMA((112,)),
            pltpu.SemaphoreType.DMA((40,)),
        ],
        compiler_params=pltpu.CompilerParams(
            collective_id=cid, has_side_effects=True, vmem_limit_bytes=60 << 20
        ),
        name=name,
    )(*[array for array, _ in ins.values()])
    return SimpleNamespace(**dict(zip(outs, results)))


class Copies:
    def __init__(self, send, recv, local):
        self.send, self.recv, self.local = send, recv, local
        self.remotes, self.locals = 0, 0

    def reserve(self, count):
        first = self.remotes
        self.remotes += count
        return first

    def describe(self, src, dst, peer, at):
        return pltpu.make_async_remote_copy(
            src_ref=src,
            dst_ref=dst,
            send_sem=self.send.at[at],
            recv_sem=self.recv.at[at],
            device_id=peer,
            device_id_type=MESH,
        )

    def remote(self, src, dst, peer):
        copy = self.describe(src, dst, peer, self.reserve(1))
        copy.start()
        return copy

    def here(self, src, dst):
        copy = pltpu.make_async_copy(src, dst, self.local.at[self.locals])
        self.locals += 1
        copy.start()
        return copy


def comm_call(kernel, name, cid, args, outs, in_specs, out_specs, remotes, locals_, scratch=()):
    return pl.pallas_call(
        kernel,
        out_shape=outs,
        in_specs=in_specs,
        out_specs=out_specs,
        scratch_shapes=[
            pltpu.SemaphoreType.DMA((remotes,)),
            pltpu.SemaphoreType.DMA((remotes,)),
            pltpu.SemaphoreType.DMA((max(locals_, 1),)),
            *scratch,
        ],
        compiler_params=pltpu.CompilerParams(
            collective_id=cid, has_side_effects=True, vmem_limit_bytes=56 << 20
        ),
        name=name,
    )(*args)


def shape_of(shape, dtype):
    return jax.ShapeDtypeStruct(shape, dtype)


def unit_places(step):
    x = lax.axis_index("rep") // 16
    in_odd = step >= 4 - x
    section = jnp.where(in_odd, 1, 0)
    quarter = jnp.where(in_odd, step - 1, x + step)
    return section, quarter


def unit_bias(section, quarter, starts_ref):
    rep = lax.axis_index("rep")
    x, line = rep // 16, rep % 16
    row = lax.broadcasted_iota(jnp.int32, (1024, 128), 0)
    block, inside = row // HALF, row % HALF
    even_key = (16 * x + block) * 128 + inside
    odd_key = (127 - 2 * (16 * x + (block % 4) * 4 + block // 4)) * HALF + inside
    key = jnp.where(section == 1, odd_key, even_key)
    lane = lax.broadcasted_iota(jnp.int32, (1, 128), 1)
    even_query = (16 * quarter + line) * 128 + lane
    odd_query = (127 - 2 * (16 * (3 - quarter) + line)) * HALF + lane - HALF
    query = jnp.where(lane < HALF, even_query, odd_query)
    begin = jnp.where(
        lane < HALF, starts_ref[pl.ds(quarter, 1), :], starts_ref[pl.ds(3 - quarter, 1), :]
    )
    return jnp.where((key <= query) & (key >= begin), 0.0, LOWEST)


def head_rows(ref, quarter, group):
    parts = []
    for head in range(3 * group, 3 * group + 3):
        columns = slice(head * HEAD_SIZE, (head + 1) * HEAD_SIZE)
        parts.append(ref[quarter, 0:HALF, columns])
        parts.append(ref[3 - quarter, HALF : 2 * HALF, columns])
    return jnp.concatenate(parts, axis=0)


def contract(left, right, left_dim, right_dim):
    return lax.dot_general(
        left, right, (((left_dim,), (right_dim,)), ((), ())), preferred_element_type=jnp.float32
    )


def attend_kernel(q_ref, kv_ref, starts_ref, o_ref, lse_ref, bias, best, total, accum):
    best[...] = jnp.full(best.shape, FLOOR, jnp.float32)
    total[...] = jnp.zeros(total.shape, jnp.float32)
    accum[...] = jnp.zeros(accum.shape, jnp.float32)

    def unit(section, quarter):
        bias[...] = unit_bias(section, quarter, starts_ref)
        for group in range(3):
            queries = head_rows(q_ref, quarter, group)
            keys = kv_ref[section, :, group * 128 : group * 128 + 64]
            values = kv_ref[section, :, group * 128 + 64 : group * 128 + 128]
            scores = contract(keys, queries, 1, 1)
            tile = bias[...]
            scores = scores + jnp.concatenate([tile, tile, tile], axis=1)
            old = best[quarter, group]
            new = jnp.maximum(old, jnp.max(scores, axis=0, keepdims=True))
            expon = jnp.exp(scores - new)
            decay = jnp.exp(old - new)
            best[quarter, group] = new
            total[quarter, group] = total[quarter, group] * decay + jnp.sum(
                expon, axis=0, keepdims=True
            )
            accum[quarter, group] = accum[quarter, group] * decay + contract(
                values, expon.astype(jnp.bfloat16), 0, 0
            )

    def step_body(step, carry):
        section, quarter = unit_places(step)

        @pl.when(section == 0)
        def _():
            unit(0, quarter)

        @pl.when(section == 1)
        def _():
            unit(1, quarter)

        return carry

    lax.fori_loop(0, 5, step_body, 0)
    lane = lax.broadcasted_iota(jnp.int32, (1, 128), 1)
    results, logs = {}, {}
    for quarter in range(4):
        for group in range(3):
            summed = total[quarter, group]
            safe = jnp.where(summed > 0.0, summed, 1.0)
            results[quarter, group] = accum[quarter, group] / safe
            logs[quarter, group] = best[quarter, group] + jnp.log(safe)
    for chunk in range(4):
        rows = []
        for head in range(QUERY_HEADS):
            group, part = head // 3, slice((head % 3) * 128, (head % 3) * 128 + 128)
            o_ref[chunk, head * 64 : head * 64 + 64, :] = jnp.where(
                lane < HALF, results[chunk, group][:, part], results[3 - chunk, group][:, part]
            ).astype(jnp.bfloat16)
            rows.append(
                jnp.where(lane < HALF, logs[chunk, group][:, part], logs[3 - chunk, group][:, part])
            )
        rows.append(jnp.zeros((7, 128), jnp.float32))
        lse_ref[chunk] = jnp.concatenate(rows, axis=0)


ATTEND = {
    "partial": ((4, MODEL_WIDTH, 128), jnp.bfloat16),
    "logs": ((4, 16, 128), jnp.float32),
    "bias": ((1024, 128), jnp.float32),
    "best": ((4, 3, 1, 384), jnp.float32),
    "total": ((4, 3, 1, 384), jnp.float32),
    "accum": ((4, 3, 64, 384), jnp.float32),
}


def attend(refs):
    attend_kernel(
        refs.queries_in,
        refs.kv_in,
        refs.starts,
        refs.partial,
        refs.logs,
        refs.bias,
        refs.best,
        refs.total,
        refs.accum,
    )


ORDERS = ("xzy", "zyx", "yxz")


def part_columns(part, at):
    return pl.ds(pl.multiple_of(part * 512 + at * 128, 128), 128)


def piece_rows(piece, at):
    return pl.ds(pl.multiple_of(at * piece, 16), piece)


def places():
    _, x, z, y = coords()
    return {"x": x, "z": z, "y": y}


def reduce_scratch(rows):
    return [
        pltpu.VMEM((3, 3, rows, 128), jnp.bfloat16),
        pltpu.VMEM((3, rows, 128), jnp.bfloat16),
        pltpu.VMEM((3, 3, rows // 4, 128), jnp.bfloat16),
        pltpu.VMEM((3, 4, rows // 4, 128), jnp.bfloat16),
    ]


class Reduce:
    def __init__(self, copies, source, one, sum_one, two, three, target):
        self.copies, self.source, self.target = copies, source, target
        self.one, self.sum_one, self.two, self.three = one, sum_one, two, three
        self.piece = source.shape[0] // 4
        self.place = places()
        self.first = copies.reserve(27)

    def legs(self, stage, part):
        axis = ORDERS[part][stage]
        here = self.place[axis]
        made = []
        for d in (1, 2, 3):
            there = (here + d) % 4
            if stage == 0:
                src = self.source.at[:, part_columns(part, there)]
                dst = self.one.at[part, d - 1]
            elif stage == 1:
                src = self.sum_one.at[part, piece_rows(self.piece, there)]
                dst = self.two.at[part, d - 1]
            else:
                src = dst = self.three.at[part, here]
            at = self.first + stage * 9 + part * 3 + d - 1
            made.append(self.copies.describe(src, dst, line_peer(axis, d), at))
        return made

    def go(self, stage, part):
        for copy in self.legs(stage, part):
            copy.start()

    def arrive(self, stage, part):
        for copy in self.legs(stage, part):
            copy.wait()

    def start(self):
        for part in range(3):
            self.go(0, part)

    def second(self):
        for part, order in enumerate(ORDERS):
            self.arrive(0, part)
            total = self.source[:, part_columns(part, self.place[order[0]])].astype(jnp.float32)
            for d in range(3):
                total = total + self.one[part, d].astype(jnp.float32)
            self.sum_one[part] = total.astype(jnp.bfloat16)
            self.go(1, part)

    def third(self):
        for part, order in enumerate(ORDERS):
            self.arrive(1, part)
            mine = piece_rows(self.piece, self.place[order[1]])
            total = self.sum_one[part, mine].astype(jnp.float32)
            for d in range(3):
                total = total + self.two[part, d].astype(jnp.float32)
            self.three[part, self.place[order[2]]] = total.astype(jnp.bfloat16)
            self.go(2, part)

    def finish(self):
        for part in range(3):
            self.arrive(2, part)
            total = self.three[part, 0].astype(jnp.float32)
            for at in (1, 2, 3):
                total = total + self.three[part, at].astype(jnp.float32)
            self.target[part] = total.astype(jnp.bfloat16)


class Spread:
    def __init__(self, copies, pieces, target):
        self.copies, self.pieces, self.target = copies, pieces, target
        self.piece = target.shape[0] // 4
        self.place = places()
        self.first = copies.reserve(18)

    def window(self, stage, part):
        order = ORDERS[part]
        columns = part_columns(part, self.place[order[0]])
        if stage == 0:
            return piece_rows(self.piece, self.place[order[1]]), columns
        return slice(None), columns

    def legs(self, stage, part):
        axis = ORDERS[part][1 - stage]
        block = self.target.at[self.window(stage, part)]
        at = self.first + stage * 9 + part * 3
        return [
            self.copies.describe(block, block, line_peer(axis, d), at + d - 1) for d in (1, 2, 3)
        ]

    def start(self):
        for part in range(3):
            self.target[self.window(0, part)] = self.pieces[part]
            for copy in self.legs(0, part):
                copy.start()

    def second(self):
        for part in range(3):
            for copy in self.legs(0, part):
                copy.wait()
            for copy in self.legs(1, part):
                copy.start()

    def finish(self):
        for part in range(3):
            for copy in self.legs(1, part):
                copy.wait()


ROWS_A, ROWS_B = 1024, 256


def split_wide(matrix):
    gap = jnp.zeros((144, 64), jnp.float32)
    tail = jnp.zeros((144, 320), jnp.float32)
    return jnp.concatenate([matrix[:144], gap, matrix[144:], tail], axis=1)


def rows_of(ref):
    return ref[...].reshape(ref.shape[0] * ref.shape[1], ref.shape[2])


def put_gain(out, row, gains):
    out[row : row + 16, :] = jnp.zeros((16, 1536), jnp.bfloat16)
    out[row : row + 16, 0:384] = (gains[0] + gains[1]).astype(jnp.bfloat16)


WEIGHTS = {"wq": 576, "wk": 192, "wv": 192, "wo": 576, "wg": 1536, "wu": 1536, "wd": 576}
WIDE = jnp.float32
LOW = jnp.bfloat16


def dot(left, right):
    return contract(left, right, 1, 0)


def dot_t(left, right):
    return contract(left, right, 1, 1)


def inverse_rms(rows):
    return lax.rsqrt(jnp.mean(rows * rows, axis=-1, keepdims=True) + EPSILON)


def norm_back(grad, rows, inverse, gain):
    scaled = grad * gain
    return inverse * scaled - rows * inverse**3 * jnp.mean(scaled * rows, axis=-1, keepdims=True)


def gain_row(gains, row):
    both = gains[...].astype(WIDE)
    return jnp.concatenate(
        [both[0, row : row + 1, 0:288], both[1, row : row + 1, 0:288]], axis=1
    )


def rotate(rows, cosine, sine):
    lane = lax.broadcasted_iota(jnp.int32, (128, 128), 1) % HEAD_SIZE
    tiles = []
    for at in range(0, rows.shape[1], 128):
        tile = rows[:, at : at + 128]
        swapped = jnp.where(lane < 32, pltpu.roll(tile, 96, 1), pltpu.roll(tile, 32, 1))
        tiles.append(tile * cosine + swapped * sine)
    return jnp.concatenate(tiles, axis=1)


def put_halves(ref, rows):
    width = rows.shape[1] // 2
    ref[0] = rows[:, :width].astype(ref.dtype)
    ref[1] = rows[:, width:].astype(ref.dtype)


def get_halves(ref):
    return jnp.concatenate([ref[0], ref[1]], axis=1)


def put_gain_halves(ref, gain):
    ref[...] = jnp.zeros(ref.shape, WIDE)
    ref[0, 0:1, 0:288] = gain[:, 0:288]
    ref[1, 0:1, 0:288] = gain[:, 288:576]


def project(refs, hidden, gain, weights):
    normed = (hidden * inverse_rms(hidden) * gain).astype(LOW)
    put_halves(refs.normed, normed)
    wq, wk, wv = [weight[...] for weight in weights]
    turned = rotate(
        jnp.concatenate([dot(normed, wq), dot(normed, wk)], axis=1), refs.cosine[...], refs.sine[...]
    )
    refs.queries[...] = (turned[:, 0:576] * 0.125).astype(LOW)
    values = dot(normed, wv)
    parts = []
    for group in range(3):
        parts.append(turned[:, 576 + 64 * group : 640 + 64 * group])
        parts.append(values[:, 64 * group : 64 * group + 64])
    refs.kv[...] = jnp.concatenate(parts, axis=1).astype(LOW)


def send_weights(refs, copies, layer, names):
    core = lax.axis_index("shard")
    started = {}
    for name in names:
        own = getattr(refs, name).at[layer]
        depth = own.shape[0]
        target = getattr(refs, name + "_all").at[pl.ds(pl.multiple_of(core * depth, 16), depth)]
        started[name] = [copies.remote(own, target, core_peer())]
    return started


def bring_weights(refs, copies, layer, names):
    return {
        name: copies.here(getattr(refs, name).at[layer], getattr(refs, name + "_stage"))
        for name in names
    }


def keep_weights(refs, copies, started, inward):
    core = lax.axis_index("shard")
    for name, copy in inward.items():
        copy.wait()
        stage = getattr(refs, name + "_stage")
        depth = stage.shape[0]
        target = getattr(refs, name + "_all").at[pl.ds(pl.multiple_of(core * depth, 16), depth)]
        started[name].append(copies.here(stage, target))


def load(copies, pairs):
    return [copies.here(source, target) for source, target in pairs]


def wait_all(started):
    for copy in started:
        copy.wait()


def gather_start(refs, copies):
    _, x, z, y = coords()
    even, odd = refs.kv.at[pl.ds(0, HALF)], refs.kv.at[pl.ds(HALF, HALF)]
    even_slot, odd_slot = refs.kv_all.at[0, z, y], refs.kv_all.at[1, y, z]
    first_even = [copies.remote(even, even_slot, line_peer("y", d)) for d in (1, 2, 3)]
    first_odd = [copies.remote(odd, odd_slot, line_peer("z", d)) for d in (1, 2, 3)]
    first_even.append(copies.here(even, even_slot))
    first_odd.append(copies.here(odd, odd_slot))
    slot = refs.queries_all.at[x]
    rest = [copies.remote(refs.queries, slot, line_peer("x", d)) for d in (1, 2, 3)]
    rest.append(copies.here(refs.queries, slot))
    return first_even, first_odd, rest


def gather_finish(refs, copies, flying):
    _, _, z, y = coords()
    first_even, first_odd, rest = flying
    wait_all(first_even)
    block = refs.kv_all.at[0, z]
    rest += [copies.remote(block, block, line_peer("z", d)) for d in (1, 2, 3)]
    wait_all(first_odd)
    block = refs.kv_all.at[1, y]
    rest += [copies.remote(block, block, line_peer("y", d)) for d in (1, 2, 3)]
    wait_all(rest)


def gather_outs():
    return {
        "queries_all": ((4, 128, 576), LOW, ANY),
        "kv_all": ((2, 4, 4, HALF, 384), LOW, ANY),
        "normed": ((2, 128, 288), LOW, VMEM),
    }


def weight_outs():
    return {
        name + "_all": ((1536 if name == "wd" else 576, width), LOW, ANY)
        for name, width in WEIGHTS.items()
    }


def weight_stages():
    return {
        name + "_stage": ((768 if name == "wd" else 288, width), LOW)
        for name, width in WEIGHTS.items()
    }


def weight_loads(names):
    return {
        name + "_here": ((1536 if name == "wd" else 576, WEIGHTS[name]), LOW) for name in names
    }


QKV, LATER = ("wq", "wk", "wv"), ("wo", "wg", "wu", "wd")


def start_body(refs, copies):
    other, mirror = core_peer(), mirror_peer()
    core = lax.axis_index("shard")
    inward = bring_weights(refs, copies, 0, [*QKV, *LATER])
    greet([other, mirror, *line_peers("xzy")])
    low, high = pl.ds(0, HALF), pl.ds(HALF, HALF)
    rows = [
        copies.remote(refs.tokens.at[high], refs.tokens_out.at[high], mirror),
        copies.remote(refs.gains, refs.gains_out.at[core], other),
    ]
    started = send_weights(refs, copies, 0, QKV)
    cotangent = copies.remote(refs.cotangent.at[high], refs.cotangent_out.at[high], mirror)
    refs.tokens_out[0:HALF] = refs.tokens[0:HALF]
    refs.cotangent_out[0:HALF] = refs.cotangent[0:HALF]
    refs.gains_out[core] = refs.gains[...]
    keep_weights(refs, copies, started, {name: inward[name] for name in QKV})
    loads = []
    for name in QKV:
        wait_all(started[name])
        loads += load(
            copies, [(getattr(refs, name + "_all"), getattr(refs, name + "_here"))]
        )
    later = send_weights(refs, copies, 0, LATER)
    wait_all(rows)
    wait_all(loads)
    project(
        refs,
        refs.tokens_out[...].astype(WIDE),
        gain_row(refs.gains_out, 0),
        (refs.wq_here, refs.wk_here, refs.wv_here),
    )
    flying = gather_start(refs, copies)
    keep_weights(refs, copies, later, {name: inward[name] for name in LATER})
    gather_finish(refs, copies, flying)
    cotangent.wait()
    for name in LATER:
        wait_all(later[name])


def swap_partials(refs, copies):
    _, x, _, _ = coords()
    started = []
    for d in (1, 2, 3):
        peer = (x + d) % 4
        there = line_peer("x", d)
        started.append(copies.remote(refs.partial.at[peer], refs.partials.at[x], there))
        started.append(copies.remote(refs.logs.at[peer], refs.logs_all.at[x], there))
    refs.partials[x] = refs.partial[x]
    refs.logs_all[x] = refs.logs[x]
    return started


def merge_and_feed(refs, hidden, gain):
    logs = refs.logs_all[...]
    largest = jnp.max(logs, axis=0)
    shares = jnp.exp(logs - largest)
    total = jnp.sum(shares, axis=0)
    refs.lse[...] = largest + jnp.log(total)
    shares = shares / total
    for head in range(QUERY_HEADS):
        rows = slice(head * HEAD_SIZE, (head + 1) * HEAD_SIZE)
        outcome = jnp.zeros((HEAD_SIZE, 128), WIDE)
        for at in range(4):
            outcome += shares[at, head : head + 1, :] * refs.partials[at, rows, :].astype(WIDE)
        refs.outcome[rows, :] = outcome
    attended = refs.outcome[...].T.astype(LOW)
    put_halves(refs.attended, attended)
    middle = hidden + dot(attended, refs.wo_here[...])
    refs.middle[...] = middle
    normed_two = (middle * inverse_rms(middle) * gain).astype(LOW)
    put_halves(refs.normed_two, normed_two)
    gate = dot(normed_two, refs.wg_here[...])
    up = dot(normed_two, refs.wu_here[...])
    refs.gate[...] = gate
    refs.up[...] = up
    inner = (gate * jax.nn.sigmoid(gate) * up).astype(LOW)
    put_halves(refs.inner, inner)
    return middle + dot(inner, refs.wd_here[...])


FEED = {
    "lse": ((16, 128), WIDE),
    "outcome": ((576, 128), WIDE),
    "attended": ((2, 128, 288), LOW),
    "middle": ((128, 576), WIDE),
    "normed_two": ((2, 128, 288), LOW),
    "gate": ((128, 1536), WIDE),
    "up": ((128, 1536), WIDE),
    "inner": ((2, 128, 768), LOW),
}
PARTIALS = {"partials": ((4, 576, 128), LOW), "logs_all": ((4, 16, 128), WIDE)}


def between_body(refs, copies):
    names = [*QKV, *LATER]
    loads = load(
        copies, [(getattr(refs, name + "_low"), getattr(refs, name + "_here")) for name in LATER]
    )
    inward = bring_weights(refs, copies, 1, names)
    greet([core_peer(), *line_peers("xzy")])
    started = send_weights(refs, copies, 1, names)
    attend(refs)
    swapped = swap_partials(refs, copies)
    keep_weights(refs, copies, started, inward)
    wait_all(loads)
    wait_all(swapped)
    hidden = merge_and_feed(refs, refs.tokens[...].astype(WIDE), gain_row(refs.gains, 2))
    refs.hidden[...] = hidden
    loads = []
    for name in QKV:
        wait_all(started[name])
        loads += load(
            copies, [(getattr(refs, name + "_all"), getattr(refs, name + "_here"))]
        )
    wait_all(loads)
    project(refs, hidden, gain_row(refs.gains, 1), (refs.wq_here, refs.wk_here, refs.wv_here))
    gather_finish(refs, copies, gather_start(refs, copies))
    for name in LATER:
        wait_all(started[name])


SWAPS = {
    "normed": (2, 128, 288),
    "attended": (2, 128, 288),
    "normed_two": (2, 128, 288),
    "inner": (2, 128, 768),
    "branch": (128, 576),
    "grad_gate": (128, 1536),
    "grad_up": (128, 1536),
    "grad_branch": (128, 576),
    "grad_qkv": (128, 960),
}


def swap_cores(refs, copies, name, whole_array):
    core = lax.axis_index("shard")
    own, pair = getattr(refs, name), getattr(refs, name + "_pair")
    if whole_array:
        pair[core] = own[...]
        return copies.remote(own, pair.at[core], core_peer())
    pair[core] = own[core]
    return copies.remote(own.at[1 - core], pair.at[core], core_peer())


def pair_scratch(names):
    shapes = {}
    for name in names:
        shape = SWAPS[name]
        shapes[name + "_pair"] = (shape if len(shape) == 3 else (2,) + shape, LOW)
    return shapes


def rows_of(ref):
    return ref[...].reshape(ref.shape[0] * ref.shape[1], ref.shape[2])


def split_wide(matrix):
    gap = jnp.zeros((144, 64), WIDE)
    tail = jnp.zeros((144, 320), WIDE)
    return jnp.concatenate([matrix[:144], gap, matrix[144:], tail], axis=1)


def put_gain(out, row, gains):
    out[row : row + 16, :] = jnp.zeros((16, 1536), LOW)
    out[row : row + 16, 0:384] = (gains[0] + gains[1]).astype(LOW)


def grads_b(out, normed, qkv, gains):
    grad = contract(rows_of(normed), rows_of(qkv), 0, 0)
    out[0:144, :] = split_wide(grad[:, 0:576]).astype(LOW)
    rest = grad[:, 576:960].astype(LOW)
    for at in range(3):
        out[144:240, at * 384 : (at + 1) * 384] = rest[at * 96 : (at + 1) * 96]
    out[144:240, 1152:1536] = jnp.zeros((96, 384), LOW)
    put_gain(out, 240, gains)


def feed_back(refs, copies, grad, gain):
    _, x, _, _ = coords()
    flying = {}
    flying["normed"] = swap_cores(refs, copies, "normed", False)
    flying["attended"] = swap_cores(refs, copies, "attended", False)
    flying["normed_two"] = swap_cores(refs, copies, "normed_two", False)
    flying["inner"] = swap_cores(refs, copies, "inner", False)
    branch = grad.astype(LOW)
    refs.branch[...] = branch
    flying["branch"] = swap_cores(refs, copies, "branch", True)
    grad_inner = dot_t(branch, refs.wd_here[...])
    gate = refs.gate[...]
    sigma = jax.nn.sigmoid(gate)
    refs.grad_gate[...] = (
        grad_inner * refs.up[...] * sigma * (1.0 + gate * (1.0 - sigma))
    ).astype(LOW)
    refs.grad_up[...] = (grad_inner * gate * sigma).astype(LOW)
    flying["grad_gate"] = swap_cores(refs, copies, "grad_gate", True)
    flying["grad_up"] = swap_cores(refs, copies, "grad_up", True)
    grad_normed = dot_t(refs.grad_gate[...], refs.wg_here[...]) + dot_t(
        refs.grad_up[...], refs.wu_here[...]
    )
    middle = refs.middle[...]
    inverse = inverse_rms(middle)
    put_gain_halves(refs.mlp_gain, jnp.sum(middle * inverse * grad_normed, axis=0, keepdims=True))
    flying["mlp_gain"] = swap_cores(refs, copies, "mlp_gain", False)
    grad_middle = grad + norm_back(grad_normed, middle, inverse, gain)
    refs.grad_middle[...] = grad_middle
    low = grad_middle.astype(LOW)
    refs.grad_branch[...] = low
    flying["grad_branch"] = swap_cores(refs, copies, "grad_branch", True)
    refs.grad_attended[...] = dot_t(low, refs.wo_here[...]).astype(LOW)
    slot = refs.grads_all.at[x]
    started = [copies.remote(refs.grad_attended, slot, line_peer("x", d)) for d in (1, 2, 3)]
    started.append(copies.here(refs.grad_attended, slot))
    turned = dot_t(refs.wo_here[...], low).astype(LOW).astype(WIDE) * refs.outcome[...]
    refs.stats[0] = refs.lse[...]
    refs.stats[1, 9:16] = jnp.zeros((7, 128), WIDE)
    for head in range(QUERY_HEADS):
        refs.stats[1, head : head + 1] = jnp.sum(
            turned[head * HEAD_SIZE : (head + 1) * HEAD_SIZE], axis=0, keepdims=True
        )
    slot = refs.stats_all.at[x]
    started += [copies.remote(refs.stats, slot, line_peer("x", d)) for d in (1, 2, 3)]
    started.append(copies.here(refs.stats, slot))
    for name in ("inner", "branch", "normed_two", "grad_gate", "grad_up"):
        flying[name].wait()
    out = refs.grads_a
    two = rows_of(refs.normed_two_pair)
    out[0:288, :] = contract(two, rows_of(refs.grad_gate_pair), 0, 0).astype(LOW)
    out[288:576, :] = contract(two, rows_of(refs.grad_up_pair), 0, 0).astype(LOW)
    down = contract(rows_of(refs.branch_pair), rows_of(refs.inner_pair), 0, 0).astype(LOW)
    out[576:864, 0:768] = down[0:288]
    out[576:864, 768:1536] = down[288:576]
    flying["attended"].wait()
    flying["grad_branch"].wait()
    grad_out = contract(rows_of(refs.attended_pair), rows_of(refs.grad_branch_pair), 0, 0)
    out[864:1008, :] = split_wide(grad_out).astype(LOW)
    flying["mlp_gain"].wait()
    put_gain(out, 1008, refs.mlp_gain_pair)
    flying["normed"].wait()
    wait_all(started)


BACK_OUTS = {
    "grads_all": ((4, 128, 576), LOW, ANY),
    "stats_all": ((4, 2, 16, 128), WIDE, ANY),
    "grads_a": ((1024, 1536), LOW, VMEM),
    "normed_pair": ((2, 128, 288), LOW, VMEM),
    "grad_middle": ((128, 576), WIDE, VMEM),
}
BACK_SCRATCH = {
    "branch": ((128, 576), LOW),
    "grad_gate": ((128, 1536), LOW),
    "grad_up": ((128, 1536), LOW),
    "grad_branch": ((128, 576), LOW),
    "grad_attended": ((128, 576), LOW),
    "stats": ((2, 16, 128), WIDE),
    "mlp_gain": ((2, 16, 384), WIDE),
    "mlp_gain_pair": ((2, 16, 384), WIDE),
    **pair_scratch(
        ("attended", "normed_two", "inner", "branch", "grad_gate", "grad_up", "grad_branch")
    ),
}


def turn_body(refs, copies):
    loads = load(
        copies, [(getattr(refs, name + "_low"), getattr(refs, name + "_here")) for name in LATER]
    )
    greet([core_peer(), *line_peers("x")])
    attend(refs)
    swapped = swap_partials(refs, copies)
    wait_all(loads)
    wait_all(swapped)
    gain = gain_row(refs.gains, 3)
    rows = merge_and_feed(refs, refs.hidden[...], gain)
    refs.activations[...] = rows.astype(LOW)
    feed_back(refs, copies, refs.cotangent[...].astype(WIDE), gain)


SUMS = {
    "dq_in": ((3, MODEL_WIDTH, 128), LOW),
    "first": ((2, 3, 4, HALF, 384), LOW),
    "midway": ((2, 4, HALF, 384), LOW),
    "second": ((2, 3, HALF, 384), LOW),
    "dkv_sum": ((128, 384), WIDE),
    "grad_qkv": ((128, 960), LOW),
    "grad_qkv_pair": ((2, 128, 960), LOW),
    "attn_gain": ((2, 16, 384), WIDE),
    "attn_gain_pair": ((2, 16, 384), WIDE),
}


def sum_and_project_back(refs, copies, hidden, gain, between):
    _, x, z, y = coords()
    one, turned = [[], []], []
    for d in (1, 2, 3):
        one[0].append(
            copies.remote(
                refs.dkv.at[0, (z + d) % 4], refs.first.at[0, d - 1], line_peer("z", d)
            )
        )
        one[1].append(
            copies.remote(
                refs.dkv.at[1, (y + d) % 4], refs.first.at[1, d - 1], line_peer("y", d)
            )
        )
    for d in (1, 2, 3):
        turned.append(
            copies.remote(refs.dq.at[(x + d) % 4], refs.dq_in.at[d - 1], line_peer("x", d))
        )
    between()
    two = [[], []]
    for half, mine, axis, there in ((0, z, "y", y), (1, y, "z", z)):
        wait_all(one[half])
        total = refs.dkv[half, mine].astype(WIDE)
        for d in range(3):
            total = total + refs.first[half, d].astype(WIDE)
        refs.midway[half] = total.astype(LOW)
        for d in (1, 2, 3):
            two[half].append(
                copies.remote(
                    refs.midway.at[half, (there + d) % 4],
                    refs.second.at[half, d - 1],
                    line_peer(axis, d),
                )
            )
    wait_all(turned)
    total = refs.dq[x].astype(WIDE)
    for d in range(3):
        total = total + refs.dq_in[d].astype(WIDE)
    grad_queries = total.T
    for half, there in ((0, y), (1, z)):
        wait_all(two[half])
        total = refs.midway[half, there].astype(WIDE)
        for d in range(3):
            total = total + refs.second[half, d].astype(WIDE)
        refs.dkv_sum[half * HALF : (half + 1) * HALF, :] = total
    summed = refs.dkv_sum[...]
    keys = [summed[:, 128 * group : 128 * group + 64] for group in range(3)]
    values = [summed[:, 128 * group + 64 : 128 * group + 128] for group in range(3)]
    back = rotate(
        jnp.concatenate([grad_queries, *keys], axis=1), refs.cosine[...], -refs.sine[...]
    )
    joined = jnp.concatenate([back, *values], axis=1).astype(LOW)
    refs.grad_qkv[...] = joined
    sent = swap_cores(refs, copies, "grad_qkv", True)
    grad_normed = (
        dot_t(joined[:, 0:576], refs.wq_here[...])
        + dot_t(joined[:, 576:768], refs.wk_here[...])
        + dot_t(joined[:, 768:960], refs.wv_here[...])
    )
    inverse = inverse_rms(hidden)
    put_gain_halves(refs.attn_gain, jnp.sum(hidden * inverse * grad_normed, axis=0, keepdims=True))
    more = swap_cores(refs, copies, "attn_gain", False)
    grad = refs.grad_before[...] + norm_back(grad_normed, hidden, inverse, gain)
    return grad, [sent, more]


def down_body(refs, copies):
    loads = load(
        copies,
        [
            (getattr(refs, name + "_low"), getattr(refs, name + "_here"))
            for name in (*QKV, *LATER)
        ],
    )
    greet([core_peer(), *line_peers("xzy")])
    grad, sent = sum_and_project_back(
        refs, copies, refs.hidden[...], gain_row(refs.gains, 1), lambda: wait_all(loads)
    )
    feed_back(refs, copies, grad, gain_row(refs.gains, 2))
    wait_all(sent)
    grads_b(refs.grads_b, refs.normed_above, refs.grad_qkv_pair, refs.attn_gain_pair)


def last_body(refs, copies):
    loads = load(
        copies, [(getattr(refs, name + "_low"), getattr(refs, name + "_here")) for name in QKV]
    )
    mirror = mirror_peer()
    greet([core_peer(), mirror, *line_peers("xzy")])
    high = pl.ds(HALF, HALF)
    spreads = [
        Spread(copies, refs.red_a, refs.sum_a0),
        Spread(copies, refs.red_b, refs.sum_b1),
    ]

    def between():
        for spread in spreads:
            spread.start()
        wait_all(loads)

    grad, sent = sum_and_project_back(
        refs, copies, refs.tokens[...].astype(WIDE), gain_row(refs.gains, 0), between
    )
    wait_all(sent)
    grads_b(refs.grads_low, refs.normed_pair, refs.grad_qkv_pair, refs.attn_gain_pair)
    reduce = Reduce(
        copies, refs.grads_low, refs.one, refs.sum_one, refs.two, refs.three, refs.red
    )
    reduce.start()
    refs.grad[...] = grad
    refs.grad_out[0:HALF] = grad[0:HALF]
    refs.acts_out[0:HALF] = refs.acts[0:HALF]
    rows = [
        copies.remote(refs.grad.at[high], refs.grad_out.at[high], mirror),
        copies.remote(refs.acts.at[high], refs.acts_out.at[high], mirror),
    ]
    for spread in spreads:
        spread.second()
    reduce.second()
    reduce.third()
    reduce.finish()
    last = Spread(copies, refs.red, refs.sum_b0)
    last.start()
    last.second()
    wait_all(rows)
    for spread in [*spreads, last]:
        spread.finish()


def results_kernel(a0, a1, b0, b1, ga, wq, wk, wv, wo, gm, wg, wu, wd):
    wide = jnp.float32
    for layer, (a, b) in enumerate(((a0, b0), (a1, b1))):
        wg[layer] = a[0:288, :].astype(wide)
        wu[layer] = a[288:576, :].astype(wide)
        wd[layer, 0:768, 0:288] = a[576:864, 0:768].astype(wide).T
        wd[layer, 0:768, 288:576] = a[576:864, 768:1536].astype(wide).T
        wo[layer, 0:144] = a[864:1008, 0:576].astype(wide)
        wo[layer, 144:288] = a[864:1008, 640:1216].astype(wide)
        gm[layer : layer + 1, :] = a[1008:1024, 0:288].astype(wide)[0:1]
        wq[layer, 0:144] = b[0:144, 0:576].astype(wide)
        wq[layer, 144:288] = b[0:144, 640:1216].astype(wide)
        for at in range(3):
            rows = slice(at * 96, at * 96 + 96)
            wk[layer, rows] = b[144:240, at * 384 : at * 384 + 192].astype(wide)
            wv[layer, rows] = b[144:240, at * 384 + 192 : at * 384 + 384].astype(wide)
        ga[layer : layer + 1, :] = b[240:256, 0:288].astype(wide)[0:1]


def results(a0, a1, b0, b1):
    shapes = [
        (2, 288),
        (2, 288, 576),
        (2, 288, 192),
        (2, 288, 192),
        (2, 288, 576),
        (2, 288),
        (2, 288, 1536),
        (2, 288, 1536),
        (2, 768, 576),
    ]
    return pl.pallas_call(
        results_kernel,
        out_shape=[shape_of(shape, jnp.float32) for shape in shapes],
        in_specs=[VMEM] * 4,
        out_specs=[VMEM] * 9,
        compiler_params=pltpu.CompilerParams(vmem_limit_bytes=56 << 20),
        name="results",
    )(a0, a1, b0, b1)


def attend_back_kernel(last, *refs):
    q_ref, kv_ref, do_ref, stats_ref, starts_ref = refs[:5]
    if last:
        grads_a, grads_b, pieces = refs[5:8]
        dq_ref, dkv_ref, red_a, red_b, spread_out = refs[8:13]
        rest = refs[13:]
    else:
        (grads_a,) = refs[5:6]
        dq_ref, dkv_ref, red_a = refs[6:9]
        rest = refs[9:]
    copies = Copies(*rest[:3])
    bias, dq, dkv = rest[3:6]
    greet(line_peers("xzy"))
    sums = [Reduce(copies, grads_a, *rest[6:10], red_a)]
    spread = None
    if last:
        sums.append(Reduce(copies, grads_b, *rest[10:14], red_b))
        spread = Spread(copies, pieces, spread_out)
    for item in sums:
        item.start()
    if last:
        spread.start()
    dq[...] = jnp.zeros(dq.shape, jnp.float32)
    dkv[...] = jnp.zeros(dkv.shape, jnp.float32)

    def step_body(step, carry):
        section, quarter = unit_places(step)
        bias[...] = unit_bias(section, quarter, starts_ref)
        lane = lax.broadcasted_iota(jnp.int32, (1, 128), 1)
        stats = jnp.where(lane < HALF, stats_ref[quarter], stats_ref[3 - quarter])
        for group in range(3):
            queries = head_rows(q_ref, quarter, group)
            grads = head_rows(do_ref, quarter, group)
            keys = kv_ref[section, :, group * 128 : group * 128 + 64]
            values = kv_ref[section, :, group * 128 + 64 : group * 128 + 128]
            heads = range(3 * group, 3 * group + 3)
            logs = jnp.concatenate([stats[0, h : h + 1, :] for h in heads], axis=1)
            delta = jnp.concatenate([stats[1, h : h + 1, :] for h in heads], axis=1)
            scores = contract(keys, queries, 1, 1)
            tile = bias[...]
            scores = scores + jnp.concatenate([tile, tile, tile], axis=1)
            weights = jnp.exp(scores - logs)
            grad_weights = contract(values, grads, 1, 1)
            grad_scores = (weights * (grad_weights - delta)).astype(jnp.bfloat16)
            grad_values = contract(weights.astype(jnp.bfloat16), grads, 1, 0)
            grad_keys = contract(grad_scores, queries, 1, 0)
            dkv[section, group] += jnp.concatenate([grad_keys, grad_values], axis=1)
            dq[quarter, group] += contract(keys, grad_scores, 0, 0)
        @pl.when(step == 2)
        def _():
            if last:
                spread.second()
            else:
                sums[0].second()

        @pl.when(step == 3)
        def _():
            if last:
                for item in sums:
                    item.second()
            else:
                sums[0].third()

        return carry

    lax.fori_loop(0, 5, step_body, 0)
    if last:
        for item in sums:
            item.third()
    lane = lax.broadcasted_iota(jnp.int32, (1, 128), 1)
    for chunk in range(4):
        for head in range(QUERY_HEADS):
            group, part = head // 3, slice((head % 3) * 128, (head % 3) * 128 + 128)
            picked = jnp.where(
                lane < HALF, dq[chunk, group][:, part], dq[3 - chunk, group][:, part]
            )
            dq_ref[chunk, head * 64 : head * 64 + 64, :] = (picked * 0.125).astype(jnp.bfloat16)
    for section in range(2):
        for group in range(3):
            dkv_ref[section, :, group * 128 : group * 128 + 128] = dkv[section, group].astype(
                jnp.bfloat16
            )
    for item in sums:
        item.finish()
    if last:
        spread.finish()


def attend_back(queries, kv, grads, stats, starts, jobs, cid):
    last = len(jobs) > 1
    outs = [
        shape_of((4, MODEL_WIDTH, 128), jnp.bfloat16),
        shape_of((2, 1024, 384), jnp.bfloat16),
        shape_of((3, ROWS_A // 4, 128), jnp.bfloat16),
    ]
    scratch = [
        pltpu.VMEM((1024, 128), jnp.float32),
        pltpu.VMEM((4, 3, 64, 384), jnp.float32),
        pltpu.VMEM((2, 3, 1024, 128), jnp.float32),
        *reduce_scratch(ROWS_A),
    ]
    if last:
        outs.append(shape_of((3, ROWS_B // 4, 128), jnp.bfloat16))
        outs.append(shape_of((ROWS_A, 1536), jnp.bfloat16))
        scratch += reduce_scratch(ROWS_B)
    return comm_call(
        functools.partial(attend_back_kernel, last),
        f"attend_back_{cid}",
        cid,
        (queries, kv.reshape(2, 1024, 384), grads, stats, starts, *jobs),
        outs,
        [VMEM] * (5 + len(jobs)),
        [VMEM] * len(outs),
        27 + 27 + 18 if last else 27,
        1,
        scratch,
    )


def sequence_starts(lengths, rows):
    ends = jnp.cumsum(lengths)
    begins = ends - lengths
    segment = jnp.sum((rows[..., None] >= ends).astype(jnp.int32), axis=-1)
    labels = jnp.arange(lengths.shape[0], dtype=jnp.int32)
    return jnp.sum(jnp.where(segment[..., None] == labels, begins, 0), axis=-1)


def rope_tables(position):
    half = HEAD_SIZE // 2
    freqs = jnp.exp(jnp.arange(half, dtype=jnp.float32) * (-2.0 * math.log(10000.0) / HEAD_SIZE))
    angles = position.astype(jnp.float32)[:, None] * freqs[None, :]
    return jnp.cos(angles), jnp.sin(angles)


def per_device(
    tokens,
    seq_lengths,
    attn_gain,
    w_query,
    key_weight,
    value_weight,
    w_out,
    mlp_gain,
    w_gate,
    w_up,
    w_down,
    cotangent,
):
    lengths = seq_lengths[0]
    rep = lax.axis_index("rep")
    x, line = rep // 16, rep % 16
    inside = jnp.arange(128, dtype=jnp.int32)
    chunk = jnp.arange(4, dtype=jnp.int32)[:, None] * 16 + line
    rows_all = jnp.where(
        inside[None, :] < HALF,
        chunk * 128 + inside[None, :],
        (127 - 2 * chunk) * HALF + inside[None, :] - HALF,
    )
    starts = sequence_starts(lengths, rows_all)
    position = jnp.where(
        inside < HALF, rep * 128 + inside, (127 - 2 * rep) * HALF + inside - HALF
    ) - sequence_starts(
        lengths,
        jnp.where(inside < HALF, rep * 128 + inside, (127 - 2 * rep) * HALF + inside - HALF),
    )
    cosine, sine = rope_tables(position)
    cosine = jnp.concatenate([cosine] * 4, axis=1)
    sine = jnp.concatenate([-sine, sine] * 2, axis=1)
    tables = {"cosine": (cosine, VMEM), "sine": (sine, VMEM)}
    gains = jnp.pad(jnp.concatenate([attn_gain, mlp_gain]), ((0, 12), (0, 96)))
    params = dict(zip(WEIGHTS, (w_query, key_weight, value_weight, w_out, w_gate, w_up, w_down)))
    raw = {name: (value, ANY) for name, value in params.items()}
    sources = {"queries": ((128, 576), LOW), "kv": ((128, 384), LOW)}

    def kept_weights(result, names):
        return {name + "_low": (getattr(result, name + "_all"), ANY) for name in names}

    def kept_rows(result, names):
        return {name: (getattr(result, name), VMEM) for name in names}

    zero = named_call(
        start_body,
        "start",
        0,
        {
            "tokens": (tokens, VMEM),
            "cotangent": (cotangent, VMEM),
            "gains": (gains, VMEM),
            **tables,
            **raw,
        },
        {
            "tokens_out": ((128, 576), LOW, VMEM),
            "cotangent_out": ((128, 576), LOW, VMEM),
            "gains_out": ((2, 16, 384), LOW, VMEM),
            **gather_outs(),
            **weight_outs(),
        },
        {**sources, **weight_stages(), **weight_loads(QKV)},
    )
    gains = (zero.gains_out, VMEM)
    tokens = (zero.tokens_out, VMEM)
    one = named_call(
        between_body,
        "between",
        1,
        {
            "queries_in": (zero.queries_all, VMEM),
            "kv_in": (zero.kv_all.reshape(2, 1024, 384), VMEM),
            "starts": (starts, VMEM),
            "tokens": tokens,
            "gains": gains,
            **tables,
            **raw,
            **kept_weights(zero, LATER),
        },
        {
            "hidden": ((128, 576), WIDE, VMEM),
            **{name: (*kind, VMEM) for name, kind in FEED.items()},
            **gather_outs(),
            **weight_outs(),
        },
        {**sources, **ATTEND, **PARTIALS, **weight_stages(), **weight_loads([*QKV, *LATER])},
    )
    back_one = named_call(
        turn_body,
        "turn",
        2,
        {
            "queries_in": (one.queries_all, VMEM),
            "kv_in": (one.kv_all.reshape(2, 1024, 384), VMEM),
            "starts": (starts, VMEM),
            "hidden": (one.hidden, VMEM),
            "cotangent": (zero.cotangent_out, VMEM),
            "gains": gains,
            "normed": (one.normed, VMEM),
            **kept_weights(one, LATER),
        },
        {"activations": ((128, 576), LOW, VMEM), **BACK_OUTS},
        {**FEED, **ATTEND, **PARTIALS, **BACK_SCRATCH, **weight_loads(LATER)},
    )
    dq, dkv, red_a1 = attend_back(
        one.queries_all,
        one.kv_all,
        back_one.grads_all,
        back_one.stats_all,
        starts,
        (back_one.grads_a,),
        3,
    )
    back_zero = named_call(
        down_body,
        "down",
        4,
        {
            "dq": (dq, VMEM),
            "dkv": (dkv.reshape(2, 4, 4, HALF, 384), VMEM),
            "hidden": (one.hidden, VMEM),
            "grad_before": (back_one.grad_middle, VMEM),
            "gains": gains,
            "normed": (zero.normed, VMEM),
            "normed_above": (back_one.normed_pair, VMEM),
            **tables,
            **kept_rows(one, FEED),
            **kept_weights(one, QKV),
            **kept_weights(zero, LATER),
        },
        {"grads_b": ((ROWS_B, 1536), LOW, VMEM), **BACK_OUTS},
        {**SUMS, **BACK_SCRATCH, **weight_loads([*QKV, *LATER])},
    )
    dq, dkv, red_a0, red_b1, sum_a1 = attend_back(
        zero.queries_all,
        zero.kv_all,
        back_zero.grads_all,
        back_zero.stats_all,
        starts,
        (back_zero.grads_a, back_zero.grads_b, red_a1),
        5,
    )
    end = named_call(
        last_body,
        "last",
        6,
        {
            "dq": (dq, VMEM),
            "dkv": (dkv.reshape(2, 4, 4, HALF, 384), VMEM),
            "tokens": tokens,
            "acts": (back_one.activations, VMEM),
            "grad_before": (back_zero.grad_middle, VMEM),
            "gains": gains,
            "normed_pair": (back_zero.normed_pair, VMEM),
            "red_a": (red_a0, VMEM),
            "red_b": (red_b1, VMEM),
            **tables,
            **kept_weights(zero, QKV),
        },
        {
            "acts_out": ((128, 576), LOW, VMEM),
            "grad_out": ((128, 576), WIDE, VMEM),
            "sum_a0": ((ROWS_A, 1536), LOW, VMEM),
            "sum_b1": ((ROWS_B, 1536), LOW, VMEM),
            "sum_b0": ((ROWS_B, 1536), LOW, VMEM),
        },
        {
            **SUMS,
            **weight_loads(QKV),
            "grad": ((128, 576), WIDE),
            "grads_low": ((ROWS_B, 1536), LOW),
            "one": ((3, 3, ROWS_B, 128), LOW),
            "sum_one": ((3, ROWS_B, 128), LOW),
            "two": ((3, 3, ROWS_B // 4, 128), LOW),
            "three": ((3, 4, ROWS_B // 4, 128), LOW),
            "red": ((3, ROWS_B // 4, 128), LOW),
        },
    )
    return (end.acts_out, end.grad_out, *results(end.sum_a0, sum_a1, end.sum_b0, end.sum_b1))


def solution(mesh):
    rows = P(("shard", "rep"), None)
    gain, weight = P(None, "shard"), P(None, "shard", None)
    return jax.shard_map(
        per_device,
        mesh=mesh,
        in_specs=(
            rows,
            P("shard", None),
            gain,
            weight,
            weight,
            weight,
            weight,
            gain,
            weight,
            weight,
            weight,
            rows,
        ),
        out_specs=(
            rows,
            rows,
            gain,
            weight,
            weight,
            weight,
            weight,
            gain,
            weight,
            weight,
            weight,
        ),
        check_vma=False,
    )
```

```python
import functools
import math
from types import SimpleNamespace

import jax
import jax.numpy as jnp
from jax import lax
from jax.experimental import pallas as pl
from jax.experimental.pallas import tpu as pltpu
from jax.sharding import PartitionSpec as P

QUERY_HEADS = 9
KEY_VALUE_HEADS = 3
HEAD_SIZE = 64
DECODER_LAYERS = 2
MODEL_WIDTH = 576
HALF = 64
EPSILON = 1e-05
LOWEST = -1e30
FLOOR = -1e20

MESH = pl.DeviceIdType.MESH
ANY = pl.BlockSpec(memory_space=pl.ANY)
VMEM = pl.BlockSpec(memory_space=pltpu.VMEM)


def coords():
    rep = lax.axis_index("rep")
    return lax.axis_index("shard"), rep // 16, (rep // 4) % 4, rep % 4


def device(core, x, z, y):
    return (core, x * 16 + z * 4 + y)


def line_peer(axis, step):
    core, x, z, y = coords()
    if axis == "x":
        return device(core, (x + step) % 4, z, y)
    if axis == "z":
        return device(core, x, (z + step) % 4, y)
    return device(core, x, z, (y + step) % 4)


def core_peer():
    core, x, z, y = coords()
    return device(1 - core, x, z, y)


def mirror_peer():
    core, x, z, y = coords()
    return device(core, 3 - x, 3 - z, 3 - y)


def greet(peers):
    barrier = pltpu.get_barrier_semaphore()
    for peer in peers:
        pl.semaphore_signal(barrier, inc=1, device_id=peer, device_id_type=MESH)
    pl.semaphore_wait(barrier, len(peers))


def line_peers(axes):
    return [line_peer(axis, step) for axis in axes for step in (1, 2, 3)]


def named_call(body, name, cid, ins, outs, scratch):
    keys = [*ins, *outs, *scratch]

    def kernel(*refs):
        sems = refs[len(keys) :]
        body(SimpleNamespace(**dict(zip(keys, refs))), Copies(*sems))

    results = pl.pallas_call(
        kernel,
        out_shape=[shape_of(shape, dtype) for shape, dtype, _ in outs.values()],
        in_specs=[spec for _, spec in ins.values()],
        out_specs=[spec for _, _, spec in outs.values()],
        scratch_shapes=[
            *[pltpu.VMEM(shape, dtype) for shape, dtype in scratch.values()],
            pltpu.SemaphoreType.DMA((112,)),
            pltpu.SemaphoreType.DMA((112,)),
            pltpu.SemaphoreType.DMA((40,)),
        ],
        compiler_params=pltpu.CompilerParams(
            collective_id=cid, has_side_effects=True, vmem_limit_bytes=60 << 20
        ),
        name=name,
    )(*[array for array, _ in ins.values()])
    return SimpleNamespace(**dict(zip(outs, results)))


class Copies:
    def __init__(self, send, recv, local):
        self.send, self.recv, self.local = send, recv, local
        self.remotes, self.locals = 0, 0

    def reserve(self, count):
        first = self.remotes
        self.remotes += count
        return first

    def describe(self, src, dst, peer, at):
        return pltpu.make_async_remote_copy(
            src_ref=src,
            dst_ref=dst,
            send_sem=self.send.at[at],
            recv_sem=self.recv.at[at],
            device_id=peer,
            device_id_type=MESH,
        )

    def remote(self, src, dst, peer):
        copy = self.describe(src, dst, peer, self.reserve(1))
        copy.start()
        return copy

    def here(self, src, dst):
        copy = pltpu.make_async_copy(src, dst, self.local.at[self.locals])
        self.locals += 1
        copy.start()
        return copy


def comm_call(kernel, name, cid, args, outs, in_specs, out_specs, remotes, locals_, scratch=()):
    return pl.pallas_call(
        kernel,
        out_shape=outs,
        in_specs=in_specs,
        out_specs=out_specs,
        scratch_shapes=[
            pltpu.SemaphoreType.DMA((remotes,)),
            pltpu.SemaphoreType.DMA((remotes,)),
            pltpu.SemaphoreType.DMA((max(locals_, 1),)),
            *scratch,
        ],
        compiler_params=pltpu.CompilerParams(
            collective_id=cid, has_side_effects=True, vmem_limit_bytes=56 << 20
        ),
        name=name,
    )(*args)


def shape_of(shape, dtype):
    return jax.ShapeDtypeStruct(shape, dtype)


def unit_places(step):
    x = lax.axis_index("rep") // 16
    in_odd = step >= 4 - x
    section = jnp.where(in_odd, 1, 0)
    quarter = jnp.where(in_odd, step - 1, x + step)
    return section, quarter


def unit_bias(section, quarter, starts_ref):
    rep = lax.axis_index("rep")
    x, line = rep // 16, rep % 16
    row = lax.broadcasted_iota(jnp.int32, (1024, 128), 0)
    block, inside = row // HALF, row % HALF
    even_key = (16 * x + block) * 128 + inside
    odd_key = (127 - 2 * (16 * x + (block % 4) * 4 + block // 4)) * HALF + inside
    key = jnp.where(section == 1, odd_key, even_key)
    lane = lax.broadcasted_iota(jnp.int32, (1, 128), 1)
    even_query = (16 * quarter + line) * 128 + lane
    odd_query = (127 - 2 * (16 * (3 - quarter) + line)) * HALF + lane - HALF
    query = jnp.where(lane < HALF, even_query, odd_query)
    begin = jnp.where(
        lane < HALF, starts_ref[pl.ds(quarter, 1), :], starts_ref[pl.ds(3 - quarter, 1), :]
    )
    return jnp.where((key <= query) & (key >= begin), 0.0, LOWEST)


def head_rows(ref, quarter, group):
    parts = []
    for head in range(3 * group, 3 * group + 3):
        columns = slice(head * HEAD_SIZE, (head + 1) * HEAD_SIZE)
        parts.append(ref[quarter, 0:HALF, columns])
        parts.append(ref[3 - quarter, HALF : 2 * HALF, columns])
    return jnp.concatenate(parts, axis=0)


def contract(left, right, left_dim, right_dim):
    return lax.dot_general(
        left, right, (((left_dim,), (right_dim,)), ((), ())), preferred_element_type=jnp.float32
    )


def attend_kernel(q_ref, kv_ref, starts_ref, o_ref, lse_ref, bias, best, total, accum):
    best[...] = jnp.full(best.shape, FLOOR, jnp.float32)
    total[...] = jnp.zeros(total.shape, jnp.float32)
    accum[...] = jnp.zeros(accum.shape, jnp.float32)

    def unit(section, quarter):
        bias[...] = unit_bias(section, quarter, starts_ref)
        for group in range(3):
            queries = head_rows(q_ref, quarter, group)
            keys = kv_ref[section, :, group * 128 : group * 128 + 64]
            values = kv_ref[section, :, group * 128 + 64 : group * 128 + 128]
            scores = contract(keys, queries, 1, 1)
            tile = bias[...]
            scores = scores + jnp.concatenate([tile, tile, tile], axis=1)
            old = best[quarter, group]
            new = jnp.maximum(old, jnp.max(scores, axis=0, keepdims=True))
            expon = jnp.exp(scores - new)
            decay = jnp.exp(old - new)
            best[quarter, group] = new
            total[quarter, group] = total[quarter, group] * decay + jnp.sum(
                expon, axis=0, keepdims=True
            )
            accum[quarter, group] = accum[quarter, group] * decay + contract(
                values, expon.astype(jnp.bfloat16), 0, 0
            )

    def step_body(step, carry):
        section, quarter = unit_places(step)

        @pl.when(section == 0)
        def _():
            unit(0, quarter)

        @pl.when(section == 1)
        def _():
            unit(1, quarter)

        return carry

    lax.fori_loop(0, 5, step_body, 0)
    lane = lax.broadcasted_iota(jnp.int32, (1, 128), 1)
    results, logs = {}, {}
    for quarter in range(4):
        for group in range(3):
            summed = total[quarter, group]
            safe = jnp.where(summed > 0.0, summed, 1.0)
            results[quarter, group] = accum[quarter, group] / safe
            logs[quarter, group] = best[quarter, group] + jnp.log(safe)
    for chunk in range(4):
        rows = []
        for head in range(QUERY_HEADS):
            group, part = head // 3, slice((head % 3) * 128, (head % 3) * 128 + 128)
            o_ref[chunk, head * 64 : head * 64 + 64, :] = jnp.where(
                lane < HALF, results[chunk, group][:, part], results[3 - chunk, group][:, part]
            ).astype(jnp.bfloat16)
            rows.append(
                jnp.where(lane < HALF, logs[chunk, group][:, part], logs[3 - chunk, group][:, part])
            )
        rows.append(jnp.zeros((7, 128), jnp.float32))
        lse_ref[chunk] = jnp.concatenate(rows, axis=0)


ATTEND = dict(
    partial=((4, MODEL_WIDTH, 128), jnp.bfloat16),
    logs=((4, 16, 128), jnp.float32),
    bias=((1024, 128), jnp.float32),
    best=((4, 3, 1, 384), jnp.float32),
    total=((4, 3, 1, 384), jnp.float32),
    accum=((4, 3, 64, 384), jnp.float32),
)


def attend(refs):
    attend_kernel(
        refs.queries_in,
        refs.kv_in,
        refs.starts,
        refs.partial,
        refs.logs,
        refs.bias,
        refs.best,
        refs.total,
        refs.accum,
    )


ORDERS = ("xzy", "zyx", "yxz")


def part_columns(part, at):
    return pl.ds(pl.multiple_of(part * 512 + at * 128, 128), 128)


def piece_rows(piece, at):
    return pl.ds(pl.multiple_of(at * piece, 16), piece)


def places():
    _, x, z, y = coords()
    return dict(x=x, z=z, y=y)


def reduce_scratch(rows):
    return [
        pltpu.VMEM((3, 3, rows, 128), jnp.bfloat16),
        pltpu.VMEM((3, rows, 128), jnp.bfloat16),
        pltpu.VMEM((3, 3, rows // 4, 128), jnp.bfloat16),
        pltpu.VMEM((3, 4, rows // 4, 128), jnp.bfloat16),
    ]


class Reduce:
    def __init__(self, copies, source, one, sum_one, two, three, target):
        self.copies, self.source, self.target = copies, source, target
        self.one, self.sum_one, self.two, self.three = one, sum_one, two, three
        self.piece = source.shape[0] // 4
        self.place = places()
        self.first = copies.reserve(27)

    def legs(self, stage, part):
        axis = ORDERS[part][stage]
        here = self.place[axis]
        made = []
        for d in (1, 2, 3):
            there = (here + d) % 4
            if stage == 0:
                src = self.source.at[:, part_columns(part, there)]
                dst = self.one.at[part, d - 1]
            elif stage == 1:
                src = self.sum_one.at[part, piece_rows(self.piece, there)]
                dst = self.two.at[part, d - 1]
            else:
                src = dst = self.three.at[part, here]
            at = self.first + stage * 9 + part * 3 + d - 1
            made.append(self.copies.describe(src, dst, line_peer(axis, d), at))
        return made

    def go(self, stage, part):
        for copy in self.legs(stage, part):
            copy.start()

    def arrive(self, stage, part):
        for copy in self.legs(stage, part):
            copy.wait()

    def start(self):
        for part in range(3):
            self.go(0, part)

    def second(self):
        for part, order in enumerate(ORDERS):
            self.arrive(0, part)
            total = self.source[:, part_columns(part, self.place[order[0]])].astype(jnp.float32)
            for d in range(3):
                total = total + self.one[part, d].astype(jnp.float32)
            self.sum_one[part] = total.astype(jnp.bfloat16)
            self.go(1, part)

    def third(self):
        for part, order in enumerate(ORDERS):
            self.arrive(1, part)
            mine = piece_rows(self.piece, self.place[order[1]])
            total = self.sum_one[part, mine].astype(jnp.float32)
            for d in range(3):
                total = total + self.two[part, d].astype(jnp.float32)
            self.three[part, self.place[order[2]]] = total.astype(jnp.bfloat16)
            self.go(2, part)

    def finish(self):
        for part in range(3):
            self.arrive(2, part)
            total = self.three[part, 0].astype(jnp.float32)
            for at in (1, 2, 3):
                total = total + self.three[part, at].astype(jnp.float32)
            self.target[part] = total.astype(jnp.bfloat16)


class Spread:
    def __init__(self, copies, pieces, target):
        self.copies, self.pieces, self.target = copies, pieces, target
        self.piece = target.shape[0] // 4
        self.place = places()
        self.first = copies.reserve(18)

    def window(self, stage, part):
        order = ORDERS[part]
        columns = part_columns(part, self.place[order[0]])
        if stage == 0:
            return piece_rows(self.piece, self.place[order[1]]), columns
        return slice(None), columns

    def legs(self, stage, part):
        axis = ORDERS[part][1 - stage]
        block = self.target.at[self.window(stage, part)]
        at = self.first + stage * 9 + part * 3
        return [
            self.copies.describe(block, block, line_peer(axis, d), at + d - 1) for d in (1, 2, 3)
        ]

    def start(self):
        for part in range(3):
            self.target[self.window(0, part)] = self.pieces[part]
            for copy in self.legs(0, part):
                copy.start()

    def second(self):
        for part in range(3):
            for copy in self.legs(0, part):
                copy.wait()
            for copy in self.legs(1, part):
                copy.start()

    def finish(self):
        for part in range(3):
            for copy in self.legs(1, part):
                copy.wait()


ROWS_A, ROWS_B = 1024, 256


def split_wide(matrix):
    gap = jnp.zeros((144, 64), jnp.float32)
    tail = jnp.zeros((144, 320), jnp.float32)
    return jnp.concatenate([matrix[:144], gap, matrix[144:], tail], axis=1)


def rows_of(ref):
    return ref[...].reshape(ref.shape[0] * ref.shape[1], ref.shape[2])


def put_gain(out, row, gains):
    out[row : row + 16, :] = jnp.zeros((16, 1536), jnp.bfloat16)
    out[row : row + 16, 0:384] = (gains[0] + gains[1]).astype(jnp.bfloat16)


WEIGHTS = dict(wq=576, wk=192, wv=192, wo=576, wg=1536, wu=1536, wd=1536)
ALL, STAGE, HERE, LOWER, PAIR = "_all", "_stage", "_here", "_low", "_pair"
WIDE = jnp.float32
LOW = jnp.bfloat16


def dot(left, right):
    return contract(left, right, 1, 0)


def dot_t(left, right):
    return contract(left, right, 1, 1)


def inverse_rms(rows):
    return lax.rsqrt(jnp.mean(rows * rows, axis=-1, keepdims=True) + EPSILON)


def norm_back(grad, rows, inverse, gain):
    scaled = grad * gain
    return inverse * scaled - rows * inverse**3 * jnp.mean(scaled * rows, axis=-1, keepdims=True)


def gain_row(gains, row):
    both = gains[...].astype(WIDE)
    return jnp.concatenate(
        [both[0, row : row + 1, 0:288], both[1, row : row + 1, 0:288]], axis=1
    )


def rotate(rows, cosine, sine):
    lane = lax.broadcasted_iota(jnp.int32, (128, 128), 1) % HEAD_SIZE
    tiles = []
    for at in range(0, rows.shape[1], 128):
        tile = rows[:, at : at + 128]
        swapped = jnp.where(lane < 32, pltpu.roll(tile, 96, 1), pltpu.roll(tile, 32, 1))
        tiles.append(tile * cosine + swapped * sine)
    return jnp.concatenate(tiles, axis=1)


def put_halves(ref, rows):
    width = rows.shape[1] // 2
    ref[0] = rows[:, :width].astype(ref.dtype)
    ref[1] = rows[:, width:].astype(ref.dtype)


def get_halves(ref):
    return jnp.concatenate([ref[0], ref[1]], axis=1)


def put_gain_halves(ref, gain):
    ref[...] = jnp.zeros(ref.shape, WIDE)
    ref[0, 0:1, 0:288] = gain[:, 0:288]
    ref[1, 0:1, 0:288] = gain[:, 288:576]


def project(refs, hidden, gain, weights):
    normed = (hidden * inverse_rms(hidden) * gain).astype(LOW)
    put_halves(refs.normed, normed)
    wq, wk, wv = [weight[...] for weight in weights]
    turned = rotate(
        jnp.concatenate([dot(normed, wq), dot(normed, wk)], axis=1), refs.cosine[...], refs.sine[...]
    )
    refs.queries[...] = (turned[:, 0:576] * 0.125).astype(LOW)
    values = dot(normed, wv)
    parts = []
    for group in range(3):
        parts.append(turned[:, 576 + 64 * group : 640 + 64 * group])
        parts.append(values[:, 64 * group : 64 * group + 64])
    refs.kv[...] = jnp.concatenate(parts, axis=1).astype(LOW)


def own_part(refs, name, core):
    whole = getattr(refs, name + ALL)
    if name == "wd":
        return whole.at[:, pl.ds(pl.multiple_of(core * 768, 128), 768)]
    return whole.at[pl.ds(pl.multiple_of(core * 288, 16), 288)]


def whole_shape(name):
    return (MODEL_WIDTH, WEIGHTS[name])


def half_shape(name):
    return (576, 768) if name == "wd" else (288, WEIGHTS[name])


def send_weights(refs, copies, layer, names):
    core = lax.axis_index("shard")
    started = {}
    for name in names:
        own = getattr(refs, name).at[layer]
        started[name] = [copies.remote(own, own_part(refs, name, core), core_peer())]
    return started


def bring_weights(refs, copies, layer, names):
    return {
        name: copies.here(getattr(refs, name).at[layer], getattr(refs, name + STAGE))
        for name in names
    }


def keep_weights(refs, copies, started, inward):
    core = lax.axis_index("shard")
    for name, copy in inward.items():
        copy.wait()
        stage = getattr(refs, name + STAGE)
        started[name].append(copies.here(stage, own_part(refs, name, core)))


def load(copies, pairs):
    return [copies.here(source, target) for source, target in pairs]


def wait_all(started):
    for copy in started:
        copy.wait()


def gather_start(refs, copies):
    _, x, z, y = coords()
    even, odd = refs.kv.at[pl.ds(0, HALF)], refs.kv.at[pl.ds(HALF, HALF)]
    even_slot, odd_slot = refs.kv_all.at[0, z, y], refs.kv_all.at[1, y, z]
    first_even = [copies.remote(even, even_slot, line_peer("y", d)) for d in (1, 2, 3)]
    first_odd = [copies.remote(odd, odd_slot, line_peer("z", d)) for d in (1, 2, 3)]
    first_even.append(copies.here(even, even_slot))
    first_odd.append(copies.here(odd, odd_slot))
    slot = refs.queries_all.at[x]
    rest = [copies.remote(refs.queries, slot, line_peer("x", d)) for d in (1, 2, 3)]
    rest.append(copies.here(refs.queries, slot))
    return first_even, first_odd, rest


def gather_finish(refs, copies, flying):
    _, _, z, y = coords()
    first_even, first_odd, rest = flying
    wait_all(first_even)
    block = refs.kv_all.at[0, z]
    rest += [copies.remote(block, block, line_peer("z", d)) for d in (1, 2, 3)]
    wait_all(first_odd)
    block = refs.kv_all.at[1, y]
    rest += [copies.remote(block, block, line_peer("y", d)) for d in (1, 2, 3)]
    wait_all(rest)


def gather_outs():
    return dict(
        queries_all=((4, 128, 576), LOW, ANY),
        kv_all=((2, 4, 4, HALF, 384), LOW, ANY),
        normed=((2, 128, 288), LOW, VMEM),
    )


def weight_outs():
    return {
        name + ALL: (whole_shape(name), LOW, ANY)
        for name in WEIGHTS
    }


def weight_stages():
    return {
        name + STAGE: (half_shape(name), LOW)
        for name in WEIGHTS
    }


def weight_loads(names):
    return {
        name + HERE: (whole_shape(name), LOW) for name in names
    }


QKV, LATER = ("wq", "wk", "wv"), ("wo", "wg", "wu", "wd")


def start_body(refs, copies):
    other, mirror = core_peer(), mirror_peer()
    core = lax.axis_index("shard")
    inward = bring_weights(refs, copies, 0, [*QKV, *LATER])
    refs.token_rows[...] = refs.tokens[...].astype(WIDE).T.astype(LOW)
    refs.cotangent_rows[...] = refs.cotangent[...].astype(WIDE).T.astype(LOW)
    greet([other, mirror, *line_peers("xzy")])
    high = pl.ds(HALF, HALF)
    rows = [
        copies.remote(refs.token_rows.at[high], refs.tokens_out.at[high], mirror),
        copies.remote(refs.gains, refs.gains_out.at[core], other),
    ]
    started = send_weights(refs, copies, 0, QKV)
    cotangent = copies.remote(refs.cotangent_rows.at[high], refs.cotangent_out.at[high], mirror)
    refs.tokens_out[0:HALF] = refs.token_rows[0:HALF]
    refs.cotangent_out[0:HALF] = refs.cotangent_rows[0:HALF]
    refs.gains_out[core] = refs.gains[...]
    keep_weights(refs, copies, started, {name: inward[name] for name in QKV})
    loads = []
    for name in QKV:
        wait_all(started[name])
        loads += load(
            copies, [(getattr(refs, name + ALL), getattr(refs, name + HERE))]
        )
    later = send_weights(refs, copies, 0, LATER)
    wait_all(rows)
    wait_all(loads)
    project(
        refs,
        refs.tokens_out[...].astype(WIDE),
        gain_row(refs.gains_out, 0),
        (refs.wq_here, refs.wk_here, refs.wv_here),
    )
    flying = gather_start(refs, copies)
    keep_weights(refs, copies, later, {name: inward[name] for name in LATER})
    gather_finish(refs, copies, flying)
    cotangent.wait()
    for name in LATER:
        wait_all(later[name])


def swap_partials(refs, copies):
    _, x, _, _ = coords()
    started = []
    for d in (1, 2, 3):
        peer = (x + d) % 4
        there = line_peer("x", d)
        started.append(copies.remote(refs.partial.at[peer], refs.partials.at[x], there))
        started.append(copies.remote(refs.logs.at[peer], refs.logs_all.at[x], there))
    refs.partials[x] = refs.partial[x]
    refs.logs_all[x] = refs.logs[x]
    return started


def merge_and_feed(refs, hidden, gain):
    logs = refs.logs_all[...]
    largest = jnp.max(logs, axis=0)
    shares = jnp.exp(logs - largest)
    total = jnp.sum(shares, axis=0)
    refs.lse[...] = largest + jnp.log(total)
    shares = shares / total
    for head in range(QUERY_HEADS):
        rows = slice(head * HEAD_SIZE, (head + 1) * HEAD_SIZE)
        outcome = jnp.zeros((HEAD_SIZE, 128), WIDE)
        for at in range(4):
            outcome += shares[at, head : head + 1, :] * refs.partials[at, rows, :].astype(WIDE)
        refs.outcome[rows, :] = outcome
    attended = refs.outcome[...].T.astype(LOW)
    put_halves(refs.attended, attended)
    middle = hidden + dot(attended, refs.wo_here[...])
    refs.middle[...] = middle
    normed_two = (middle * inverse_rms(middle) * gain).astype(LOW)
    put_halves(refs.normed_two, normed_two)
    gate = dot(normed_two, refs.wg_here[...])
    up = dot(normed_two, refs.wu_here[...])
    refs.gate[...] = gate
    refs.up[...] = up
    inner = (gate * jax.nn.sigmoid(gate) * up).astype(LOW)
    put_halves(refs.inner, inner)
    return middle + dot_t(inner, refs.wd_here[...])


FEED = dict(
    lse=((16, 128), WIDE),
    outcome=((576, 128), WIDE),
    attended=((2, 128, 288), LOW),
    middle=((128, 576), WIDE),
    normed_two=((2, 128, 288), LOW),
    gate=((128, 1536), WIDE),
    up=((128, 1536), WIDE),
    inner=((2, 128, 768), LOW),
)
PARTIALS = dict(partials=((4, 576, 128), LOW), logs_all=((4, 16, 128), WIDE))


def between_body(refs, copies):
    names = [*QKV, *LATER]
    loads = load(
        copies, [(getattr(refs, name + LOWER), getattr(refs, name + HERE)) for name in LATER]
    )
    inward = bring_weights(refs, copies, 1, names)
    greet([core_peer(), *line_peers("xzy")])
    started = send_weights(refs, copies, 1, names)
    attend(refs)
    swapped = swap_partials(refs, copies)
    keep_weights(refs, copies, started, inward)
    wait_all(loads)
    wait_all(swapped)
    hidden = merge_and_feed(refs, refs.tokens[...].astype(WIDE), gain_row(refs.gains, 2))
    refs.hidden[...] = hidden
    loads = []
    for name in QKV:
        wait_all(started[name])
        loads += load(
            copies, [(getattr(refs, name + ALL), getattr(refs, name + HERE))]
        )
    wait_all(loads)
    project(refs, hidden, gain_row(refs.gains, 1), (refs.wq_here, refs.wk_here, refs.wv_here))
    gather_finish(refs, copies, gather_start(refs, copies))
    for name in LATER:
        wait_all(started[name])


SWAPS = dict(
    normed=(2, 128, 288),
    attended=(2, 128, 288),
    normed_two=(2, 128, 288),
    inner=(2, 128, 768),
    branch=(128, 576),
    grad_gate=(128, 1536),
    grad_up=(128, 1536),
    grad_branch=(128, 576),
    grad_qkv=(128, 960),
)


def swap_cores(copies, own, pair, whole_array):
    core = lax.axis_index("shard")
    if whole_array:
        pair[core] = own[...]
        return copies.remote(own, pair.at[core], core_peer())
    pair[core] = own[core]
    return copies.remote(own.at[1 - core], pair.at[core], core_peer())


def pair_scratch(names):
    shapes = {}
    for name in names:
        shape = SWAPS[name]
        shapes[name + PAIR] = (shape if len(shape) == 3 else (2,) + shape, LOW)
    return shapes


def rows_of(ref):
    return ref[...].reshape(ref.shape[0] * ref.shape[1], ref.shape[2])


def split_wide(matrix):
    gap = jnp.zeros((144, 64), WIDE)
    tail = jnp.zeros((144, 320), WIDE)
    return jnp.concatenate([matrix[:144], gap, matrix[144:], tail], axis=1)


def put_gain(out, row, gains):
    out[row : row + 16, :] = jnp.zeros((16, 1536), LOW)
    out[row : row + 16, 0:384] = (gains[0] + gains[1]).astype(LOW)


def grads_b(out, normed, qkv, gains):
    grad = contract(rows_of(normed), rows_of(qkv), 0, 0)
    out[0:144, :] = split_wide(grad[:, 0:576]).astype(LOW)
    rest = grad[:, 576:960].astype(LOW)
    for at in range(3):
        out[144:240, at * 384 : (at + 1) * 384] = rest[at * 96 : (at + 1) * 96]
    out[144:240, 1152:1536] = jnp.zeros((96, 384), LOW)
    put_gain(out, 240, gains)


def feed_back(refs, copies, grad, gain):
    _, x, _, _ = coords()
    flying = SimpleNamespace()
    flying.normed = swap_cores(copies, refs.normed, refs.normed_pair, False)
    flying.attended = swap_cores(copies, refs.attended, refs.attended_pair, False)
    flying.normed_two = swap_cores(copies, refs.normed_two, refs.normed_two_pair, False)
    flying.inner = swap_cores(copies, refs.inner, refs.inner_pair, False)
    branch = grad.astype(LOW)
    refs.branch[...] = branch
    flying.branch = swap_cores(copies, refs.branch, refs.branch_pair, True)
    grad_inner = dot(branch, refs.wd_here[...])
    gate = refs.gate[...]
    sigma = jax.nn.sigmoid(gate)
    refs.grad_gate[...] = (
        grad_inner * refs.up[...] * sigma * (1.0 + gate * (1.0 - sigma))
    ).astype(LOW)
    refs.grad_up[...] = (grad_inner * gate * sigma).astype(LOW)
    flying.grad_gate = swap_cores(copies, refs.grad_gate, refs.grad_gate_pair, True)
    flying.grad_up = swap_cores(copies, refs.grad_up, refs.grad_up_pair, True)
    grad_normed = dot_t(refs.grad_gate[...], refs.wg_here[...]) + dot_t(
        refs.grad_up[...], refs.wu_here[...]
    )
    middle = refs.middle[...]
    inverse = inverse_rms(middle)
    put_gain_halves(refs.mlp_gain, jnp.sum(middle * inverse * grad_normed, axis=0, keepdims=True))
    flying.mlp_gain = swap_cores(copies, refs.mlp_gain, refs.mlp_gain_pair, False)
    grad_middle = grad + norm_back(grad_normed, middle, inverse, gain)
    refs.grad_middle[...] = grad_middle
    low = grad_middle.astype(LOW)
    refs.grad_branch[...] = low
    flying.grad_branch = swap_cores(copies, refs.grad_branch, refs.grad_branch_pair, True)
    refs.grad_attended[...] = dot_t(low, refs.wo_here[...]).astype(LOW)
    slot = refs.grads_all.at[x]
    started = [copies.remote(refs.grad_attended, slot, line_peer("x", d)) for d in (1, 2, 3)]
    started.append(copies.here(refs.grad_attended, slot))
    turned = dot_t(refs.wo_here[...], low).astype(LOW).astype(WIDE) * refs.outcome[...]
    refs.stats[0] = refs.lse[...]
    refs.stats[1, 9:16] = jnp.zeros((7, 128), WIDE)
    for head in range(QUERY_HEADS):
        refs.stats[1, head : head + 1] = jnp.sum(
            turned[head * HEAD_SIZE : (head + 1) * HEAD_SIZE], axis=0, keepdims=True
        )
    slot = refs.stats_all.at[x]
    started += [copies.remote(refs.stats, slot, line_peer("x", d)) for d in (1, 2, 3)]
    started.append(copies.here(refs.stats, slot))
    wait_all(
        [flying.inner, flying.branch, flying.normed_two, flying.grad_gate, flying.grad_up]
    )
    out = refs.grads_a
    two = rows_of(refs.normed_two_pair)
    out[0:288, :] = contract(two, rows_of(refs.grad_gate_pair), 0, 0).astype(LOW)
    out[288:576, :] = contract(two, rows_of(refs.grad_up_pair), 0, 0).astype(LOW)
    down = contract(rows_of(refs.branch_pair), rows_of(refs.inner_pair), 0, 0).astype(LOW)
    out[576:864, 0:768] = down[0:288]
    out[576:864, 768:1536] = down[288:576]
    flying.attended.wait()
    flying.grad_branch.wait()
    grad_out = contract(rows_of(refs.attended_pair), rows_of(refs.grad_branch_pair), 0, 0)
    out[864:1008, :] = split_wide(grad_out).astype(LOW)
    flying.mlp_gain.wait()
    put_gain(out, 1008, refs.mlp_gain_pair)
    flying.normed.wait()
    wait_all(started)


BACK_OUTS = dict(
    grads_all=((4, 128, 576), LOW, ANY),
    stats_all=((4, 2, 16, 128), WIDE, ANY),
    grads_a=((1024, 1536), LOW, VMEM),
    normed_pair=((2, 128, 288), LOW, VMEM),
    grad_middle=((128, 576), WIDE, VMEM),
)
BACK_SCRATCH = dict(
    branch=((128, 576), LOW),
    grad_gate=((128, 1536), LOW),
    grad_up=((128, 1536), LOW),
    grad_branch=((128, 576), LOW),
    grad_attended=((128, 576), LOW),
    stats=((2, 16, 128), WIDE),
    mlp_gain=((2, 16, 384), WIDE),
    mlp_gain_pair=((2, 16, 384), WIDE),
    **pair_scratch(
        ("attended", "normed_two", "inner", "branch", "grad_gate", "grad_up", "grad_branch")
    ),
)


def turn_body(refs, copies):
    loads = load(
        copies, [(getattr(refs, name + LOWER), getattr(refs, name + HERE)) for name in LATER]
    )
    greet([core_peer(), *line_peers("x")])
    attend(refs)
    swapped = swap_partials(refs, copies)
    wait_all(loads)
    wait_all(swapped)
    gain = gain_row(refs.gains, 3)
    rows = merge_and_feed(refs, refs.hidden[...], gain)
    refs.activations[...] = rows.astype(LOW)
    feed_back(refs, copies, refs.cotangent[...].astype(WIDE), gain)


SUMS = dict(
    dq_in=((3, MODEL_WIDTH, 128), LOW),
    first=((2, 3, 4, HALF, 384), LOW),
    midway=((2, 4, HALF, 384), LOW),
    second=((2, 3, HALF, 384), LOW),
    dkv_sum=((128, 384), WIDE),
    grad_qkv=((128, 960), LOW),
    grad_qkv_pair=((2, 128, 960), LOW),
    attn_gain=((2, 16, 384), WIDE),
    attn_gain_pair=((2, 16, 384), WIDE),
)


def sum_and_project_back(refs, copies, hidden, gain, first, second):
    _, x, z, y = coords()
    one, turned = [[], []], []
    for d in (1, 2, 3):
        one[0].append(
            copies.remote(
                refs.dkv.at[0, (z + d) % 4], refs.first.at[0, d - 1], line_peer("z", d)
            )
        )
        one[1].append(
            copies.remote(
                refs.dkv.at[1, (y + d) % 4], refs.first.at[1, d - 1], line_peer("y", d)
            )
        )
    for d in (1, 2, 3):
        turned.append(
            copies.remote(refs.dq.at[(x + d) % 4], refs.dq_in.at[d - 1], line_peer("x", d))
        )
    first()
    two = [[], []]
    for half, mine, axis, there in ((0, z, "y", y), (1, y, "z", z)):
        wait_all(one[half])
        total = refs.dkv[half, mine].astype(WIDE)
        for d in range(3):
            total = total + refs.first[half, d].astype(WIDE)
        refs.midway[half] = total.astype(LOW)
        for d in (1, 2, 3):
            two[half].append(
                copies.remote(
                    refs.midway.at[half, (there + d) % 4],
                    refs.second.at[half, d - 1],
                    line_peer(axis, d),
                )
            )
    second()
    wait_all(turned)
    total = refs.dq[x].astype(WIDE)
    for d in range(3):
        total = total + refs.dq_in[d].astype(WIDE)
    grad_queries = total.T
    for half, there in ((0, y), (1, z)):
        wait_all(two[half])
        total = refs.midway[half, there].astype(WIDE)
        for d in range(3):
            total = total + refs.second[half, d].astype(WIDE)
        refs.dkv_sum[half * HALF : (half + 1) * HALF, :] = total
    summed = refs.dkv_sum[...]
    keys = [summed[:, 128 * group : 128 * group + 64] for group in range(3)]
    values = [summed[:, 128 * group + 64 : 128 * group + 128] for group in range(3)]
    back = rotate(
        jnp.concatenate([grad_queries, *keys], axis=1), refs.cosine[...], -refs.sine[...]
    )
    joined = jnp.concatenate([back, *values], axis=1).astype(LOW)
    refs.grad_qkv[...] = joined
    sent = swap_cores(copies, refs.grad_qkv, refs.grad_qkv_pair, True)
    grad_normed = (
        dot_t(joined[:, 0:576], refs.wq_here[...])
        + dot_t(joined[:, 576:768], refs.wk_here[...])
        + dot_t(joined[:, 768:960], refs.wv_here[...])
    )
    inverse = inverse_rms(hidden)
    put_gain_halves(refs.attn_gain, jnp.sum(hidden * inverse * grad_normed, axis=0, keepdims=True))
    more = swap_cores(copies, refs.attn_gain, refs.attn_gain_pair, False)
    grad = refs.grad_before[...] + norm_back(grad_normed, hidden, inverse, gain)
    return grad, [sent, more]


def down_body(refs, copies):
    loads = load(
        copies,
        [
            (getattr(refs, name + LOWER), getattr(refs, name + HERE))
            for name in (*QKV, *LATER)
        ],
    )
    greet([core_peer(), *line_peers("xzy")])
    spread = Spread(copies, refs.red_above, refs.sum_a1)

    def first():
        spread.start()
        wait_all(loads)

    grad, sent = sum_and_project_back(
        refs, copies, refs.hidden[...], gain_row(refs.gains, 1), first, spread.second
    )
    feed_back(refs, copies, grad, gain_row(refs.gains, 2))
    spread.finish()
    wait_all(sent)
    grads_b(refs.grads_b, refs.normed_above, refs.grad_qkv_pair, refs.attn_gain_pair)


def last_body(refs, copies):
    loads = load(
        copies, [(getattr(refs, name + LOWER), getattr(refs, name + HERE)) for name in QKV]
    )
    mirror = mirror_peer()
    greet([core_peer(), mirror, *line_peers("xzy")])
    high = pl.ds(HALF, HALF)
    spreads = [
        Spread(copies, refs.red_a, refs.sum_a0),
        Spread(copies, refs.red_b, refs.sum_b1),
    ]

    def first():
        for spread in spreads:
            spread.start()
        wait_all(loads)

    def second():
        for spread in spreads:
            spread.second()

    grad, sent = sum_and_project_back(
        refs, copies, refs.tokens[...].astype(WIDE), gain_row(refs.gains, 0), first, second
    )
    wait_all(sent)
    grads_b(refs.grads_low, refs.normed_pair, refs.grad_qkv_pair, refs.attn_gain_pair)
    reduce = Reduce(
        copies, refs.grads_low, refs.one, refs.sum_one, refs.two, refs.three, refs.red
    )
    reduce.start()
    refs.grad[...] = grad
    refs.grad_out[0:HALF] = grad[0:HALF]
    refs.acts_out[0:HALF] = refs.acts[0:HALF]
    rows = [
        copies.remote(refs.grad.at[high], refs.grad_out.at[high], mirror),
        copies.remote(refs.acts.at[high], refs.acts_out.at[high], mirror),
    ]
    reduce.second()
    reduce.third()
    reduce.finish()
    last = Spread(copies, refs.red, refs.sum_b0)
    last.start()
    last.second()
    wait_all(rows)
    for spread in [*spreads, last]:
        spread.finish()


def results_kernel(
    acts, grads, a0, a1, b0, b1, acts_t, grads_t, ga, wq, wk, wv, wo, gm, wg, wu, wd
):
    wide = jnp.float32
    acts_t[...] = acts[...].astype(wide).T.astype(acts_t.dtype)
    grads_t[...] = grads[...].T
    for layer, (a, b) in enumerate(((a0, b0), (a1, b1))):
        wg[layer] = a[0:288, :].astype(wide)
        wu[layer] = a[288:576, :].astype(wide)
        wd[layer, 0:288] = a[576:864, 0:768].astype(wide)
        wd[layer, 288:576] = a[576:864, 768:1536].astype(wide)
        wo[layer, 0:144] = a[864:1008, 0:576].astype(wide)
        wo[layer, 144:288] = a[864:1008, 640:1216].astype(wide)
        gm[layer : layer + 1, :] = a[1008:1024, 0:288].astype(wide)[0:1]
        wq[layer, 0:144] = b[0:144, 0:576].astype(wide)
        wq[layer, 144:288] = b[0:144, 640:1216].astype(wide)
        for at in range(3):
            rows = slice(at * 96, at * 96 + 96)
            wk[layer, rows] = b[144:240, at * 384 : at * 384 + 192].astype(wide)
            wv[layer, rows] = b[144:240, at * 384 + 192 : at * 384 + 384].astype(wide)
        ga[layer : layer + 1, :] = b[240:256, 0:288].astype(wide)[0:1]


def results(*args):
    shapes = [
        (2, 288),
        (2, 288, 576),
        (2, 288, 192),
        (2, 288, 192),
        (2, 288, 576),
        (2, 288),
        (2, 288, 1536),
        (2, 288, 1536),
        (2, 576, 768),
    ]
    acts, grads, *gradients, down = pl.pallas_call(
        results_kernel,
        out_shape=[
            shape_of((MODEL_WIDTH, 128), jnp.bfloat16),
            shape_of((MODEL_WIDTH, 128), jnp.float32),
            *[shape_of(shape, jnp.float32) for shape in shapes],
        ],
        in_specs=[VMEM] * 6,
        out_specs=[VMEM] * 11,
        compiler_params=pltpu.CompilerParams(vmem_limit_bytes=56 << 20),
        name="results",
    )(*args)
    return (acts.T, grads.T, *gradients, down.transpose(0, 2, 1))


def attend_back_kernel(last, *refs):
    q_ref, kv_ref, do_ref, stats_ref, starts_ref, grads_a = refs[:6]
    if last:
        grads_b, dq_ref, dkv_ref, red_a, red_b = refs[6:11]
        rest = refs[11:]
    else:
        dq_ref, dkv_ref, red_a = refs[6:9]
        rest = refs[9:]
    copies = Copies(*rest[:3])
    bias, dq, dkv = rest[3:6]
    greet(line_peers("xzy"))
    sums = [Reduce(copies, grads_a, *rest[6:10], red_a)]
    if last:
        sums.append(Reduce(copies, grads_b, *rest[10:14], red_b))
    for item in sums:
        item.start()
    dq[...] = jnp.zeros(dq.shape, jnp.float32)
    dkv[...] = jnp.zeros(dkv.shape, jnp.float32)

    def step_body(step, carry):
        section, quarter = unit_places(step)
        bias[...] = unit_bias(section, quarter, starts_ref)
        lane = lax.broadcasted_iota(jnp.int32, (1, 128), 1)
        stats = jnp.where(lane < HALF, stats_ref[quarter], stats_ref[3 - quarter])
        for group in range(3):
            queries = head_rows(q_ref, quarter, group)
            grads = head_rows(do_ref, quarter, group)
            keys = kv_ref[section, :, group * 128 : group * 128 + 64]
            values = kv_ref[section, :, group * 128 + 64 : group * 128 + 128]
            heads = range(3 * group, 3 * group + 3)
            logs = jnp.concatenate([stats[0, h : h + 1, :] for h in heads], axis=1)
            delta = jnp.concatenate([stats[1, h : h + 1, :] for h in heads], axis=1)
            scores = contract(keys, queries, 1, 1)
            tile = bias[...]
            scores = scores + jnp.concatenate([tile, tile, tile], axis=1)
            weights = jnp.exp(scores - logs)
            grad_weights = contract(values, grads, 1, 1)
            grad_scores = (weights * (grad_weights - delta)).astype(jnp.bfloat16)
            grad_values = contract(weights.astype(jnp.bfloat16), grads, 1, 0)
            grad_keys = contract(grad_scores, queries, 1, 0)
            dkv[section, group] += jnp.concatenate([grad_keys, grad_values], axis=1)
            dq[quarter, group] += contract(keys, grad_scores, 0, 0)
        @pl.when(step == 2)
        def _():
            for item in sums:
                item.second()

        @pl.when(step == 3)
        def _():
            for item in sums:
                item.third()

        return carry

    lax.fori_loop(0, 5, step_body, 0)
    lane = lax.broadcasted_iota(jnp.int32, (1, 128), 1)
    for chunk in range(4):
        for head in range(QUERY_HEADS):
            group, part = head // 3, slice((head % 3) * 128, (head % 3) * 128 + 128)
            picked = jnp.where(
                lane < HALF, dq[chunk, group][:, part], dq[3 - chunk, group][:, part]
            )
            dq_ref[chunk, head * 64 : head * 64 + 64, :] = (picked * 0.125).astype(jnp.bfloat16)
    for section in range(2):
        for group in range(3):
            dkv_ref[section, :, group * 128 : group * 128 + 128] = dkv[section, group].astype(
                jnp.bfloat16
            )
    for item in sums:
        item.finish()


def attend_back(queries, kv, grads, stats, starts, jobs, cid):
    last = len(jobs) > 1
    outs = [
        shape_of((4, MODEL_WIDTH, 128), jnp.bfloat16),
        shape_of((2, 1024, 384), jnp.bfloat16),
        shape_of((3, ROWS_A // 4, 128), jnp.bfloat16),
    ]
    scratch = [
        pltpu.VMEM((1024, 128), jnp.float32),
        pltpu.VMEM((4, 3, 64, 384), jnp.float32),
        pltpu.VMEM((2, 3, 1024, 128), jnp.float32),
        *reduce_scratch(ROWS_A),
    ]
    if last:
        outs.append(shape_of((3, ROWS_B // 4, 128), jnp.bfloat16))
        scratch += reduce_scratch(ROWS_B)
    return comm_call(
        functools.partial(attend_back_kernel, last),
        f"attend_back_{cid}",
        cid,
        (queries, kv.reshape(2, 1024, 384), grads, stats, starts, *jobs),
        outs,
        [VMEM] * (5 + len(jobs)),
        [VMEM] * len(outs),
        54 if last else 27,
        1,
        scratch,
    )


def sequence_starts(lengths, rows):
    ends = jnp.cumsum(lengths)
    begins = ends - lengths
    segment = jnp.sum((rows[..., None] >= ends).astype(jnp.int32), axis=-1)
    labels = jnp.arange(lengths.shape[0], dtype=jnp.int32)
    return jnp.sum(jnp.where(segment[..., None] == labels, begins, 0), axis=-1)


def rope_tables(position):
    half = HEAD_SIZE // 2
    freqs = jnp.exp(jnp.arange(half, dtype=jnp.float32) * (-2.0 * math.log(10000.0) / HEAD_SIZE))
    angles = position.astype(jnp.float32)[:, None] * freqs[None, :]
    return jnp.cos(angles), jnp.sin(angles)


def per_device(
    tokens,
    seq_lengths,
    attn_gain,
    w_query,
    key_weight,
    value_weight,
    w_out,
    mlp_gain,
    w_gate,
    w_up,
    w_down,
    cotangent,
):
    lengths = seq_lengths[0]
    rep = lax.axis_index("rep")
    x, line = rep // 16, rep % 16
    inside = jnp.arange(128, dtype=jnp.int32)
    chunk = jnp.arange(4, dtype=jnp.int32)[:, None] * 16 + line
    rows_all = jnp.where(
        inside[None, :] < HALF,
        chunk * 128 + inside[None, :],
        (127 - 2 * chunk) * HALF + inside[None, :] - HALF,
    )
    starts = sequence_starts(lengths, rows_all)
    position = jnp.where(
        inside < HALF, rep * 128 + inside, (127 - 2 * rep) * HALF + inside - HALF
    ) - sequence_starts(
        lengths,
        jnp.where(inside < HALF, rep * 128 + inside, (127 - 2 * rep) * HALF + inside - HALF),
    )
    cosine, sine = rope_tables(position)
    cosine = jnp.concatenate([cosine] * 4, axis=1)
    sine = jnp.concatenate([-sine, sine] * 2, axis=1)
    tables = dict(cosine=(cosine, VMEM), sine=(sine, VMEM))
    gains = jnp.pad(jnp.concatenate([attn_gain, mlp_gain]), ((0, 12), (0, 96)))
    params = dict(zip(WEIGHTS, (w_query, key_weight, value_weight, w_out, w_gate, w_up, w_down.transpose(0, 2, 1))))
    raw = {name: (value, ANY) for name, value in params.items()}
    sources = dict(queries=((128, 576), LOW), kv=((128, 384), LOW))

    def kept_weights(result, names):
        return {name + LOWER: (getattr(result, name + ALL), ANY) for name in names}

    def kept_rows(result, names):
        return {name: (getattr(result, name), VMEM) for name in names}

    zero = named_call(
        start_body,
        "start",
        0,
        dict(
            tokens=(tokens.T, VMEM),
            cotangent=(cotangent.T, VMEM),
            gains=(gains, VMEM),
            **tables,
            **raw,
        ),
        dict(
            tokens_out=((128, 576), LOW, VMEM),
            cotangent_out=((128, 576), LOW, VMEM),
            gains_out=((2, 16, 384), LOW, VMEM),
            **gather_outs(),
            **weight_outs(),
        ),
        dict(
            **sources,
            **weight_stages(),
            **weight_loads(QKV),
            token_rows=((128, 576), LOW),
            cotangent_rows=((128, 576), LOW),
        ),
    )
    gains = (zero.gains_out, VMEM)
    tokens = (zero.tokens_out, VMEM)
    one = named_call(
        between_body,
        "between",
        1,
        dict(
            queries_in=(zero.queries_all, VMEM),
            kv_in=(zero.kv_all.reshape(2, 1024, 384), VMEM),
            starts=(starts, VMEM),
            tokens=tokens,
            gains=gains,
            **tables,
            **raw,
            **kept_weights(zero, LATER),
        ),
        dict(
            hidden=((128, 576), WIDE, VMEM),
            **{name: (*kind, VMEM) for name, kind in FEED.items()},
            **gather_outs(),
            **weight_outs(),
        ),
        {**sources, **ATTEND, **PARTIALS, **weight_stages(), **weight_loads([*QKV, *LATER])},
    )
    back_one = named_call(
        turn_body,
        "turn",
        2,
        dict(
            queries_in=(one.queries_all, VMEM),
            kv_in=(one.kv_all.reshape(2, 1024, 384), VMEM),
            starts=(starts, VMEM),
            hidden=(one.hidden, VMEM),
            cotangent=(zero.cotangent_out, VMEM),
            gains=gains,
            normed=(one.normed, VMEM),
            **kept_weights(one, LATER),
        ),
        dict(activations=((128, 576), LOW, VMEM), **BACK_OUTS),
        {**FEED, **ATTEND, **PARTIALS, **BACK_SCRATCH, **weight_loads(LATER)},
    )
    dq, dkv, red_a1 = attend_back(
        one.queries_all,
        one.kv_all,
        back_one.grads_all,
        back_one.stats_all,
        starts,
        (back_one.grads_a,),
        3,
    )
    back_zero = named_call(
        down_body,
        "down",
        4,
        dict(
            dq=(dq, VMEM),
            dkv=(dkv.reshape(2, 4, 4, HALF, 384), VMEM),
            hidden=(one.hidden, VMEM),
            grad_before=(back_one.grad_middle, VMEM),
            gains=gains,
            normed=(zero.normed, VMEM),
            normed_above=(back_one.normed_pair, VMEM),
            red_above=(red_a1, VMEM),
            **tables,
            **kept_rows(one, FEED),
            **kept_weights(one, QKV),
            **kept_weights(zero, LATER),
        ),
        dict(
            grads_b=((ROWS_B, 1536), LOW, VMEM),
            sum_a1=((ROWS_A, 1536), LOW, VMEM),
            **BACK_OUTS,
        ),
        {**SUMS, **BACK_SCRATCH, **weight_loads([*QKV, *LATER])},
    )
    dq, dkv, red_a0, red_b1 = attend_back(
        zero.queries_all,
        zero.kv_all,
        back_zero.grads_all,
        back_zero.stats_all,
        starts,
        (back_zero.grads_a, back_zero.grads_b),
        5,
    )
    end = named_call(
        last_body,
        "last",
        6,
        dict(
            dq=(dq, VMEM),
            dkv=(dkv.reshape(2, 4, 4, HALF, 384), VMEM),
            tokens=tokens,
            acts=(back_one.activations, VMEM),
            grad_before=(back_zero.grad_middle, VMEM),
            gains=gains,
            normed_pair=(back_zero.normed_pair, VMEM),
            red_a=(red_a0, VMEM),
            red_b=(red_b1, VMEM),
            **tables,
            **kept_weights(zero, QKV),
        ),
        dict(
            acts_out=((128, 576), LOW, VMEM),
            grad_out=((128, 576), WIDE, VMEM),
            sum_a0=((ROWS_A, 1536), LOW, VMEM),
            sum_b1=((ROWS_B, 1536), LOW, VMEM),
            sum_b0=((ROWS_B, 1536), LOW, VMEM),
        ),
        dict(
            **SUMS,
            **weight_loads(QKV),
            grad=((128, 576), WIDE),
            grads_low=((ROWS_B, 1536), LOW),
            one=((3, 3, ROWS_B, 128), LOW),
            sum_one=((3, ROWS_B, 128), LOW),
            two=((3, 3, ROWS_B // 4, 128), LOW),
            three=((3, 4, ROWS_B // 4, 128), LOW),
            red=((3, ROWS_B // 4, 128), LOW),
        ),
    )
    return results(
        end.acts_out, end.grad_out, end.sum_a0, back_zero.sum_a1, end.sum_b0, end.sum_b1
    )


def solution(mesh):
    rows = P(("shard", "rep"), None)
    gain, weight = P(None, "shard"), P(None, "shard", None)
    return jax.shard_map(
        per_device,
        mesh=mesh,
        in_specs=(
            rows,
            P("shard", None),
            gain,
            weight,
            weight,
            weight,
            weight,
            gain,
            weight,
            weight,
            weight,
            rows,
        ),
        out_specs=(
            rows,
            rows,
            gain,
            weight,
            weight,
            weight,
            weight,
            gain,
            weight,
            weight,
            weight,
        ),
        check_vma=False,
    )
```

```python
import functools
import math
from types import SimpleNamespace

import jax
import jax.numpy as jnp
from jax import lax
from jax.experimental import pallas as pl
from jax.experimental.pallas import tpu as pltpu
from jax.sharding import PartitionSpec as P

QUERY_HEADS = 9
KEY_VALUE_HEADS = 3
HEAD_SIZE = 64
DECODER_LAYERS = 2
MODEL_WIDTH = 576
HALF = 64
EPSILON = 1e-05
LOWEST = -1e30
FLOOR = -1e20

MESH = pl.DeviceIdType.MESH
ANY = pl.BlockSpec(memory_space=pl.ANY)
VMEM = pl.BlockSpec(memory_space=pltpu.VMEM)


def coords():
    rep = lax.axis_index("rep")
    return lax.axis_index("shard"), rep // 16, (rep // 4) % 4, rep % 4


def device(core, x, z, y):
    return (core, x * 16 + z * 4 + y)


def line_peer(axis, step):
    core, x, z, y = coords()
    if axis == "x":
        return device(core, (x + step) % 4, z, y)
    if axis == "z":
        return device(core, x, (z + step) % 4, y)
    return device(core, x, z, (y + step) % 4)


def core_peer():
    core, x, z, y = coords()
    return device(1 - core, x, z, y)


def mirror_peer():
    core, x, z, y = coords()
    return device(core, 3 - x, 3 - z, 3 - y)


def greet(peers):
    barrier = pltpu.get_barrier_semaphore()
    for peer in peers:
        pl.semaphore_signal(barrier, inc=1, device_id=peer, device_id_type=MESH)
    pl.semaphore_wait(barrier, len(peers))


def line_peers(axes):
    return [line_peer(axis, step) for axis in axes for step in (1, 2, 3)]


def named_call(body, name, cid, ins, outs, scratch):
    keys = [*ins, *outs, *scratch]

    def kernel(*refs):
        sems = refs[len(keys) :]
        body(SimpleNamespace(**dict(zip(keys, refs))), Copies(*sems))

    results = pl.pallas_call(
        kernel,
        out_shape=[shape_of(shape, dtype) for shape, dtype, _ in outs.values()],
        in_specs=[spec for _, spec in ins.values()],
        out_specs=[spec for _, _, spec in outs.values()],
        scratch_shapes=[
            *[pltpu.VMEM(shape, dtype) for shape, dtype in scratch.values()],
            pltpu.SemaphoreType.DMA((112,)),
            pltpu.SemaphoreType.DMA((112,)),
            pltpu.SemaphoreType.DMA((40,)),
        ],
        compiler_params=pltpu.CompilerParams(
            collective_id=cid, has_side_effects=True, vmem_limit_bytes=60 << 20
        ),
        name=name,
    )(*[array for array, _ in ins.values()])
    return SimpleNamespace(**dict(zip(outs, results)))


class Copies:
    def __init__(self, send, recv, local):
        self.send, self.recv, self.local = send, recv, local
        self.remotes, self.locals = 0, 0

    def reserve(self, count):
        first = self.remotes
        self.remotes += count
        return first

    def describe(self, src, dst, peer, at):
        return pltpu.make_async_remote_copy(
            src_ref=src,
            dst_ref=dst,
            send_sem=self.send.at[at],
            recv_sem=self.recv.at[at],
            device_id=peer,
            device_id_type=MESH,
        )

    def remote(self, src, dst, peer):
        copy = self.describe(src, dst, peer, self.reserve(1))
        copy.start()
        return copy

    def here(self, src, dst):
        copy = pltpu.make_async_copy(src, dst, self.local.at[self.locals])
        self.locals += 1
        copy.start()
        return copy


def comm_call(kernel, name, cid, args, outs, in_specs, out_specs, remotes, locals_, scratch=()):
    return pl.pallas_call(
        kernel,
        out_shape=outs,
        in_specs=in_specs,
        out_specs=out_specs,
        scratch_shapes=[
            pltpu.SemaphoreType.DMA((remotes,)),
            pltpu.SemaphoreType.DMA((remotes,)),
            pltpu.SemaphoreType.DMA((max(locals_, 1),)),
            *scratch,
        ],
        compiler_params=pltpu.CompilerParams(
            collective_id=cid, has_side_effects=True, vmem_limit_bytes=56 << 20
        ),
        name=name,
    )(*args)


def shape_of(shape, dtype):
    return jax.ShapeDtypeStruct(shape, dtype)


def unit_places(step):
    x = lax.axis_index("rep") // 16
    in_odd = step >= 4 - x
    section = jnp.where(in_odd, 1, 0)
    quarter = jnp.where(in_odd, step - 1, x + step)
    return section, quarter


def unit_bias(section, quarter, starts_ref):
    rep = lax.axis_index("rep")
    x, line = rep // 16, rep % 16
    row = lax.broadcasted_iota(jnp.int32, (1024, 128), 0)
    block, inside = row // HALF, row % HALF
    even_key = (16 * x + block) * 128 + inside
    odd_key = (127 - 2 * (16 * x + (block % 4) * 4 + block // 4)) * HALF + inside
    key = jnp.where(section == 1, odd_key, even_key)
    lane = lax.broadcasted_iota(jnp.int32, (1, 128), 1)
    even_query = (16 * quarter + line) * 128 + lane
    odd_query = (127 - 2 * (16 * (3 - quarter) + line)) * HALF + lane - HALF
    query = jnp.where(lane < HALF, even_query, odd_query)
    begin = jnp.where(
        lane < HALF, starts_ref[pl.ds(quarter, 1), :], starts_ref[pl.ds(3 - quarter, 1), :]
    )
    return jnp.where((key <= query) & (key >= begin), 0.0, LOWEST)


def head_rows(ref, quarter, group):
    parts = []
    for head in range(3 * group, 3 * group + 3):
        columns = slice(head * HEAD_SIZE, (head + 1) * HEAD_SIZE)
        parts.append(ref[quarter, 0:HALF, columns])
        parts.append(ref[3 - quarter, HALF : 2 * HALF, columns])
    return jnp.concatenate(parts, axis=0)


def contract(left, right, left_dim, right_dim):
    return lax.dot_general(
        left, right, (((left_dim,), (right_dim,)), ((), ())), preferred_element_type=jnp.float32
    )


def attend_kernel(q_ref, kv_ref, starts_ref, o_ref, lse_ref, bias, best, total, accum):
    best[...] = jnp.full(best.shape, FLOOR, jnp.float32)
    total[...] = jnp.zeros(total.shape, jnp.float32)
    accum[...] = jnp.zeros(accum.shape, jnp.float32)

    def unit(section, quarter):
        bias[...] = unit_bias(section, quarter, starts_ref)
        for group in range(3):
            queries = head_rows(q_ref, quarter, group)
            keys = kv_ref[section, :, group * 128 : group * 128 + 64]
            values = kv_ref[section, :, group * 128 + 64 : group * 128 + 128]
            scores = contract(keys, queries, 1, 1)
            tile = bias[...]
            scores = scores + jnp.concatenate([tile, tile, tile], axis=1)
            old = best[quarter, group]
            new = jnp.maximum(old, jnp.max(scores, axis=0, keepdims=True))
            expon = jnp.exp(scores - new)
            decay = jnp.exp(old - new)
            best[quarter, group] = new
            total[quarter, group] = total[quarter, group] * decay + jnp.sum(
                expon, axis=0, keepdims=True
            )
            accum[quarter, group] = accum[quarter, group] * decay + contract(
                values, expon.astype(jnp.bfloat16), 0, 0
            )

    def step_body(step, carry):
        section, quarter = unit_places(step)

        @pl.when(section == 0)
        def _():
            unit(0, quarter)

        @pl.when(section == 1)
        def _():
            unit(1, quarter)

        return carry

    lax.fori_loop(0, 5, step_body, 0)
    lane = lax.broadcasted_iota(jnp.int32, (1, 128), 1)
    results, logs = {}, {}
    for quarter in range(4):
        for group in range(3):
            summed = total[quarter, group]
            safe = jnp.where(summed > 0.0, summed, 1.0)
            results[quarter, group] = accum[quarter, group] / safe
            logs[quarter, group] = best[quarter, group] + jnp.log(safe)
    for chunk in range(4):
        rows = []
        for head in range(QUERY_HEADS):
            group, part = head // 3, slice((head % 3) * 128, (head % 3) * 128 + 128)
            o_ref[chunk, head * 64 : head * 64 + 64, :] = jnp.where(
                lane < HALF, results[chunk, group][:, part], results[3 - chunk, group][:, part]
            ).astype(jnp.bfloat16)
            rows.append(
                jnp.where(lane < HALF, logs[chunk, group][:, part], logs[3 - chunk, group][:, part])
            )
        rows.append(jnp.zeros((7, 128), jnp.float32))
        lse_ref[chunk] = jnp.concatenate(rows, axis=0)


ATTEND = dict(
    partial=((4, MODEL_WIDTH, 128), jnp.bfloat16),
    logs=((4, 16, 128), jnp.float32),
    bias=((1024, 128), jnp.float32),
    best=((4, 3, 1, 384), jnp.float32),
    total=((4, 3, 1, 384), jnp.float32),
    accum=((4, 3, 64, 384), jnp.float32),
)


def attend(refs):
    attend_kernel(
        refs.queries_in,
        refs.kv_in,
        refs.starts,
        refs.partial,
        refs.logs,
        refs.bias,
        refs.best,
        refs.total,
        refs.accum,
    )


ORDERS = ("xzy", "zyx", "yxz")


def part_columns(part, at):
    return pl.ds(pl.multiple_of(part * 512 + at * 128, 128), 128)


def piece_rows(piece, at):
    return pl.ds(pl.multiple_of(at * piece, 16), piece)


def places():
    _, x, z, y = coords()
    return dict(x=x, z=z, y=y)


def reduce_scratch(rows):
    return [
        pltpu.VMEM((3, 3, rows, 128), jnp.bfloat16),
        pltpu.VMEM((3, rows, 128), jnp.bfloat16),
        pltpu.VMEM((3, 3, rows // 4, 128), jnp.bfloat16),
        pltpu.VMEM((3, 4, rows // 4, 128), jnp.bfloat16),
    ]


class Reduce:
    def __init__(self, copies, source, one, sum_one, two, three, target):
        self.copies, self.source, self.target = copies, source, target
        self.one, self.sum_one, self.two, self.three = one, sum_one, two, three
        self.piece = source.shape[0] // 4
        self.place = places()
        self.first = copies.reserve(27)

    def legs(self, stage, part):
        axis = ORDERS[part][stage]
        here = self.place[axis]
        made = []
        for d in (1, 2, 3):
            there = (here + d) % 4
            if stage == 0:
                src = self.source.at[:, part_columns(part, there)]
                dst = self.one.at[part, d - 1]
            elif stage == 1:
                src = self.sum_one.at[part, piece_rows(self.piece, there)]
                dst = self.two.at[part, d - 1]
            else:
                src = dst = self.three.at[part, here]
            at = self.first + stage * 9 + part * 3 + d - 1
            made.append(self.copies.describe(src, dst, line_peer(axis, d), at))
        return made

    def go(self, stage, part):
        for copy in self.legs(stage, part):
            copy.start()

    def arrive(self, stage, part):
        for copy in self.legs(stage, part):
            copy.wait()

    def start(self):
        for part in range(3):
            self.go(0, part)

    def second(self):
        for part, order in enumerate(ORDERS):
            self.arrive(0, part)
            total = self.source[:, part_columns(part, self.place[order[0]])].astype(jnp.float32)
            for d in range(3):
                total = total + self.one[part, d].astype(jnp.float32)
            self.sum_one[part] = total.astype(jnp.bfloat16)
            self.go(1, part)

    def third(self):
        for part, order in enumerate(ORDERS):
            self.arrive(1, part)
            mine = piece_rows(self.piece, self.place[order[1]])
            total = self.sum_one[part, mine].astype(jnp.float32)
            for d in range(3):
                total = total + self.two[part, d].astype(jnp.float32)
            self.three[part, self.place[order[2]]] = total.astype(jnp.bfloat16)
            self.go(2, part)

    def finish(self):
        for part in range(3):
            self.arrive(2, part)
            total = self.three[part, 0].astype(jnp.float32)
            for at in (1, 2, 3):
                total = total + self.three[part, at].astype(jnp.float32)
            self.target[part] = total.astype(jnp.bfloat16)


class Spread:
    def __init__(self, copies, pieces, target):
        self.copies, self.pieces, self.target = copies, pieces, target
        self.piece = target.shape[0] // 4
        self.place = places()
        self.first = copies.reserve(18)

    def window(self, stage, part):
        order = ORDERS[part]
        columns = part_columns(part, self.place[order[0]])
        if stage == 0:
            return piece_rows(self.piece, self.place[order[1]]), columns
        return slice(None), columns

    def legs(self, stage, part):
        axis = ORDERS[part][1 - stage]
        block = self.target.at[self.window(stage, part)]
        at = self.first + stage * 9 + part * 3
        return [
            self.copies.describe(block, block, line_peer(axis, d), at + d - 1) for d in (1, 2, 3)
        ]

    def start(self):
        for part in range(3):
            self.target[self.window(0, part)] = self.pieces[part]
            for copy in self.legs(0, part):
                copy.start()

    def second(self):
        for part in range(3):
            for copy in self.legs(0, part):
                copy.wait()
            for copy in self.legs(1, part):
                copy.start()

    def finish(self):
        for part in range(3):
            for copy in self.legs(1, part):
                copy.wait()


ROWS_A, ROWS_B = 1024, 256


def split_wide(matrix):
    gap = jnp.zeros((144, 64), jnp.float32)
    tail = jnp.zeros((144, 320), jnp.float32)
    return jnp.concatenate([matrix[:144], gap, matrix[144:], tail], axis=1)


def rows_of(ref):
    return ref[...].reshape(ref.shape[0] * ref.shape[1], ref.shape[2])


def put_gain(out, row, gains):
    out[row : row + 16, :] = jnp.zeros((16, 1536), jnp.bfloat16)
    out[row : row + 16, 0:384] = (gains[0] + gains[1]).astype(jnp.bfloat16)


WEIGHTS = dict(wq=576, wk=192, wv=192, wo=576, wg=1536, wu=1536, wd=1536)
TAIL_A, TAIL_B = "_a", "_b"
ALL, STAGE, HERE, LOWER, PAIR = "_all", "_stage", "_here", "_low", "_pair"
WIDE = jnp.float32
LOW = jnp.bfloat16


def dot(left, right):
    return contract(left, right, 1, 0)


def dot_t(left, right):
    return contract(left, right, 1, 1)


def inverse_rms(rows):
    return lax.rsqrt(jnp.mean(rows * rows, axis=-1, keepdims=True) + EPSILON)


def norm_back(grad, rows, inverse, gain):
    scaled = grad * gain
    return inverse * scaled - rows * inverse**3 * jnp.mean(scaled * rows, axis=-1, keepdims=True)


def gain_row(gains, row):
    both = gains[...].astype(WIDE)
    return jnp.concatenate(
        [both[0, row : row + 1, 0:288], both[1, row : row + 1, 0:288]], axis=1
    )


def rotate(rows, cosine, sine):
    lane = lax.broadcasted_iota(jnp.int32, (128, 128), 1) % HEAD_SIZE
    tiles = []
    for at in range(0, rows.shape[1], 128):
        tile = rows[:, at : at + 128]
        swapped = jnp.where(lane < 32, pltpu.roll(tile, 96, 1), pltpu.roll(tile, 32, 1))
        tiles.append(tile * cosine + swapped * sine)
    return jnp.concatenate(tiles, axis=1)


def put_halves(ref, rows):
    width = rows.shape[1] // 2
    ref[0] = rows[:, :width].astype(ref.dtype)
    ref[1] = rows[:, width:].astype(ref.dtype)


def get_halves(ref):
    return jnp.concatenate([ref[0], ref[1]], axis=1)


def put_gain_halves(ref, gain):
    ref[...] = jnp.zeros(ref.shape, WIDE)
    ref[0, 0:1, 0:288] = gain[:, 0:288]
    ref[1, 0:1, 0:288] = gain[:, 288:576]


def project(refs, hidden, gain, weights):
    normed = (hidden * inverse_rms(hidden) * gain).astype(LOW)
    put_halves(refs.normed, normed)
    wq, wk, wv = [weight[...] for weight in weights]
    turned = rotate(
        jnp.concatenate([dot(normed, wq), dot(normed, wk)], axis=1), refs.cosine[...], refs.sine[...]
    )
    refs.queries[...] = (turned[:, 0:576] * 0.125).astype(LOW)
    values = dot(normed, wv)
    parts = []
    for group in range(3):
        parts.append(turned[:, 576 + 64 * group : 640 + 64 * group])
        parts.append(values[:, 64 * group : 64 * group + 64])
    refs.kv[...] = jnp.concatenate(parts, axis=1).astype(LOW)


def own_part(refs, name, core):
    whole = getattr(refs, name + ALL)
    if name == "wd":
        return whole.at[:, pl.ds(pl.multiple_of(core * 768, 128), 768)]
    return whole.at[pl.ds(pl.multiple_of(core * 288, 16), 288)]


def whole_shape(name):
    return (MODEL_WIDTH, WEIGHTS[name])


def half_shape(name):
    return (576, 768) if name == "wd" else (288, WEIGHTS[name])


def send_weights(refs, copies, layer, names):
    core = lax.axis_index("shard")
    started = {}
    for name in names:
        own = getattr(refs, name).at[layer]
        started[name] = [copies.remote(own, own_part(refs, name, core), core_peer())]
    return started


def bring_weights(refs, copies, layer, names):
    return {
        name: copies.here(getattr(refs, name).at[layer], getattr(refs, name + STAGE))
        for name in names
    }


def keep_weights(refs, copies, started, inward):
    core = lax.axis_index("shard")
    for name, copy in inward.items():
        copy.wait()
        stage = getattr(refs, name + STAGE)
        started[name].append(copies.here(stage, own_part(refs, name, core)))


def load(copies, pairs):
    return [copies.here(source, target) for source, target in pairs]


def wait_all(started):
    for copy in started:
        copy.wait()


def gather_start(refs, copies):
    _, x, z, y = coords()
    even, odd = refs.kv.at[pl.ds(0, HALF)], refs.kv.at[pl.ds(HALF, HALF)]
    even_slot, odd_slot = refs.kv_all.at[0, z, y], refs.kv_all.at[1, y, z]
    first_even = [copies.remote(even, even_slot, line_peer("y", d)) for d in (1, 2, 3)]
    first_odd = [copies.remote(odd, odd_slot, line_peer("z", d)) for d in (1, 2, 3)]
    first_even.append(copies.here(even, even_slot))
    first_odd.append(copies.here(odd, odd_slot))
    slot = refs.queries_all.at[x]
    rest = [copies.remote(refs.queries, slot, line_peer("x", d)) for d in (1, 2, 3)]
    rest.append(copies.here(refs.queries, slot))
    return first_even, first_odd, rest


def gather_finish(refs, copies, flying):
    _, _, z, y = coords()
    first_even, first_odd, rest = flying
    wait_all(first_even)
    block = refs.kv_all.at[0, z]
    rest += [copies.remote(block, block, line_peer("z", d)) for d in (1, 2, 3)]
    wait_all(first_odd)
    block = refs.kv_all.at[1, y]
    rest += [copies.remote(block, block, line_peer("y", d)) for d in (1, 2, 3)]
    wait_all(rest)


def gather_outs():
    return dict(
        queries_all=((4, 128, 576), LOW, ANY),
        kv_all=((2, 4, 4, HALF, 384), LOW, ANY),
        normed=((2, 128, 288), LOW, VMEM),
    )


def weight_outs():
    return {
        name + ALL: (whole_shape(name), LOW, ANY)
        for name in WEIGHTS
    }


def weight_stages():
    return {
        name + STAGE: (half_shape(name), LOW)
        for name in WEIGHTS
    }


def weight_loads(names):
    return {
        name + HERE: (whole_shape(name), LOW) for name in names
    }


QKV, LATER = ("wq", "wk", "wv"), ("wo", "wg", "wu", "wd")


def start_body(refs, copies):
    other, mirror = core_peer(), mirror_peer()
    core = lax.axis_index("shard")
    inward = bring_weights(refs, copies, 0, [*QKV, *LATER])
    refs.token_rows[...] = refs.tokens[...].astype(WIDE).T.astype(LOW)
    refs.cotangent_rows[...] = refs.cotangent[...].astype(WIDE).T.astype(LOW)
    greet([other, mirror, *line_peers("xzy")])
    high = pl.ds(HALF, HALF)
    rows = [
        copies.remote(refs.token_rows.at[high], refs.tokens_out.at[high], mirror),
        copies.remote(refs.gains, refs.gains_out.at[core], other),
    ]
    started = send_weights(refs, copies, 0, QKV)
    cotangent = copies.remote(refs.cotangent_rows.at[high], refs.cotangent_out.at[high], mirror)
    refs.tokens_out[0:HALF] = refs.token_rows[0:HALF]
    refs.cotangent_out[0:HALF] = refs.cotangent_rows[0:HALF]
    refs.gains_out[core] = refs.gains[...]
    keep_weights(refs, copies, started, {name: inward[name] for name in QKV})
    loads = []
    for name in QKV:
        wait_all(started[name])
        loads += load(
            copies, [(getattr(refs, name + ALL), getattr(refs, name + HERE))]
        )
    later = send_weights(refs, copies, 0, LATER)
    wait_all(rows)
    wait_all(loads)
    project(
        refs,
        refs.tokens_out[...].astype(WIDE),
        gain_row(refs.gains_out, 0),
        (refs.wq_here, refs.wk_here, refs.wv_here),
    )
    flying = gather_start(refs, copies)
    keep_weights(refs, copies, later, {name: inward[name] for name in LATER})
    gather_finish(refs, copies, flying)
    cotangent.wait()
    for name in LATER:
        wait_all(later[name])


def swap_partials(refs, copies):
    _, x, _, _ = coords()
    started = []
    for d in (1, 2, 3):
        peer = (x + d) % 4
        there = line_peer("x", d)
        started.append(copies.remote(refs.partial.at[peer], refs.partials.at[x], there))
        started.append(copies.remote(refs.logs.at[peer], refs.logs_all.at[x], there))
    refs.partials[x] = refs.partial[x]
    refs.logs_all[x] = refs.logs[x]
    return started


def merge_and_feed(refs, hidden, gain):
    logs = refs.logs_all[...]
    largest = jnp.max(logs, axis=0)
    shares = jnp.exp(logs - largest)
    total = jnp.sum(shares, axis=0)
    refs.lse[...] = largest + jnp.log(total)
    shares = shares / total
    for head in range(QUERY_HEADS):
        rows = slice(head * HEAD_SIZE, (head + 1) * HEAD_SIZE)
        outcome = jnp.zeros((HEAD_SIZE, 128), WIDE)
        for at in range(4):
            outcome += shares[at, head : head + 1, :] * refs.partials[at, rows, :].astype(WIDE)
        refs.outcome[rows, :] = outcome
    attended = refs.outcome[...].T.astype(LOW)
    put_halves(refs.attended, attended)
    middle = hidden + dot(attended, refs.wo_here[...])
    refs.middle[...] = middle
    normed_two = (middle * inverse_rms(middle) * gain).astype(LOW)
    put_halves(refs.normed_two, normed_two)
    gate = dot(normed_two, refs.wg_here[...])
    up = dot(normed_two, refs.wu_here[...])
    refs.gate[...] = gate
    refs.up[...] = up
    inner = (gate * jax.nn.sigmoid(gate) * up).astype(LOW)
    put_halves(refs.inner, inner)
    return middle + dot_t(inner, refs.wd_here[...])


FEED = dict(
    lse=((16, 128), WIDE),
    outcome=((576, 128), WIDE),
    attended=((2, 128, 288), LOW),
    middle=((128, 576), WIDE),
    normed_two=((2, 128, 288), LOW),
    gate=((128, 1536), WIDE),
    up=((128, 1536), WIDE),
    inner=((2, 128, 768), LOW),
)
PARTIALS = dict(partials=((4, 576, 128), LOW), logs_all=((4, 16, 128), WIDE))


def between_body(refs, copies):
    names = [*QKV, *LATER]
    loads = load(
        copies, [(getattr(refs, name + LOWER), getattr(refs, name + HERE)) for name in LATER]
    )
    inward = bring_weights(refs, copies, 1, names)
    greet([core_peer(), *line_peers("xzy")])
    started = send_weights(refs, copies, 1, names)
    attend(refs)
    swapped = swap_partials(refs, copies)
    keep_weights(refs, copies, started, inward)
    wait_all(loads)
    wait_all(swapped)
    hidden = merge_and_feed(refs, refs.tokens[...].astype(WIDE), gain_row(refs.gains, 2))
    refs.hidden[...] = hidden
    loads = []
    for name in QKV:
        wait_all(started[name])
        loads += load(
            copies, [(getattr(refs, name + ALL), getattr(refs, name + HERE))]
        )
    wait_all(loads)
    project(refs, hidden, gain_row(refs.gains, 1), (refs.wq_here, refs.wk_here, refs.wv_here))
    gather_finish(refs, copies, gather_start(refs, copies))
    for name in LATER:
        wait_all(started[name])


SWAPS = dict(
    normed=(2, 128, 288),
    attended=(2, 128, 288),
    normed_two=(2, 128, 288),
    inner=(2, 128, 768),
    branch=(128, 576),
    grad_gate=(128, 1536),
    grad_up=(128, 1536),
    grad_branch=(128, 576),
    grad_qkv=(128, 960),
)


def swap_cores(copies, own, pair, whole_array):
    core = lax.axis_index("shard")
    if whole_array:
        pair[core] = own[...]
        return copies.remote(own, pair.at[core], core_peer())
    pair[core] = own[core]
    return copies.remote(own.at[1 - core], pair.at[core], core_peer())


def pair_scratch(names):
    shapes = {}
    for name in names:
        shape = SWAPS[name]
        shapes[name + PAIR] = (shape if len(shape) == 3 else (2,) + shape, LOW)
    return shapes


def rows_of(ref):
    return ref[...].reshape(ref.shape[0] * ref.shape[1], ref.shape[2])


def split_wide(matrix):
    gap = jnp.zeros((144, 64), WIDE)
    tail = jnp.zeros((144, 320), WIDE)
    return jnp.concatenate([matrix[:144], gap, matrix[144:], tail], axis=1)


def put_gain(out, row, gains):
    out[row : row + 16, :] = jnp.zeros((16, 1536), LOW)
    out[row : row + 16, 0:384] = (gains[0] + gains[1]).astype(LOW)


def grads_b(out, normed, qkv, gains):
    grad = contract(rows_of(normed), rows_of(qkv), 0, 0)
    out[0:144, :] = split_wide(grad[:, 0:576]).astype(LOW)
    rest = grad[:, 576:960].astype(LOW)
    for at in range(3):
        out[144:240, at * 384 : (at + 1) * 384] = rest[at * 96 : (at + 1) * 96]
    out[144:240, 1152:1536] = jnp.zeros((96, 384), LOW)
    put_gain(out, 240, gains)


def feed_back(refs, copies, grad, gain, sums, beside):
    _, x, _, _ = coords()
    flying = SimpleNamespace()
    flying.normed = swap_cores(copies, refs.normed, refs.normed_pair, False)
    flying.attended = swap_cores(copies, refs.attended, refs.attended_pair, False)
    flying.normed_two = swap_cores(copies, refs.normed_two, refs.normed_two_pair, False)
    flying.inner = swap_cores(copies, refs.inner, refs.inner_pair, False)
    branch = grad.astype(LOW)
    refs.branch[...] = branch
    flying.branch = swap_cores(copies, refs.branch, refs.branch_pair, True)
    grad_inner = dot(branch, refs.wd_here[...])
    gate = refs.gate[...]
    sigma = jax.nn.sigmoid(gate)
    refs.grad_gate[...] = (
        grad_inner * refs.up[...] * sigma * (1.0 + gate * (1.0 - sigma))
    ).astype(LOW)
    refs.grad_up[...] = (grad_inner * gate * sigma).astype(LOW)
    flying.grad_gate = swap_cores(copies, refs.grad_gate, refs.grad_gate_pair, True)
    flying.grad_up = swap_cores(copies, refs.grad_up, refs.grad_up_pair, True)
    grad_normed = dot_t(refs.grad_gate[...], refs.wg_here[...]) + dot_t(
        refs.grad_up[...], refs.wu_here[...]
    )
    middle = refs.middle[...]
    inverse = inverse_rms(middle)
    put_gain_halves(refs.mlp_gain, jnp.sum(middle * inverse * grad_normed, axis=0, keepdims=True))
    flying.mlp_gain = swap_cores(copies, refs.mlp_gain, refs.mlp_gain_pair, False)
    grad_middle = grad + norm_back(grad_normed, middle, inverse, gain)
    refs.grad_middle[...] = grad_middle
    low = grad_middle.astype(LOW)
    refs.grad_branch[...] = low
    flying.grad_branch = swap_cores(copies, refs.grad_branch, refs.grad_branch_pair, True)
    refs.grad_attended[...] = dot_t(low, refs.wo_here[...]).astype(LOW)
    slot = refs.grads_all.at[x]
    started = [copies.remote(refs.grad_attended, slot, line_peer("x", d)) for d in (1, 2, 3)]
    refs.grads_all[x] = refs.grad_attended[...]
    turned = dot_t(refs.wo_here[...], low).astype(LOW).astype(WIDE) * refs.outcome[...]
    refs.stats[0] = refs.lse[...]
    refs.stats[1, 9:16] = jnp.zeros((7, 128), WIDE)
    for head in range(QUERY_HEADS):
        refs.stats[1, head : head + 1] = jnp.sum(
            turned[head * HEAD_SIZE : (head + 1) * HEAD_SIZE], axis=0, keepdims=True
        )
    slot = refs.stats_all.at[x]
    started += [copies.remote(refs.stats, slot, line_peer("x", d)) for d in (1, 2, 3)]
    refs.stats_all[x] = refs.stats[...]
    wait_all(
        [flying.inner, flying.branch, flying.normed_two, flying.grad_gate, flying.grad_up]
    )
    out = refs.grads_a
    two = rows_of(refs.normed_two_pair)
    out[0:288, :] = contract(two, rows_of(refs.grad_gate_pair), 0, 0).astype(LOW)
    out[288:576, :] = contract(two, rows_of(refs.grad_up_pair), 0, 0).astype(LOW)
    down = contract(rows_of(refs.branch_pair), rows_of(refs.inner_pair), 0, 0).astype(LOW)
    out[576:864, 0:768] = down[0:288]
    out[576:864, 768:1536] = down[288:576]
    flying.attended.wait()
    flying.grad_branch.wait()
    grad_out = contract(rows_of(refs.attended_pair), rows_of(refs.grad_branch_pair), 0, 0)
    out[864:1008, :] = split_wide(grad_out).astype(LOW)
    flying.mlp_gain.wait()
    put_gain(out, 1008, refs.mlp_gain_pair)
    sums[0].start()
    beside()
    for item in sums[1:]:
        item.start()
    flying.normed.wait()
    wait_all(started)


BACK_OUTS = dict(
    dq_out=((4, MODEL_WIDTH, 128), LOW, VMEM),
    dkv_out=((2, 1024, 384), LOW, VMEM),
    red_a=((3, ROWS_A // 4, 128), LOW, VMEM),
    normed_pair=((2, 128, 288), LOW, VMEM),
    grad_middle=((128, 576), WIDE, VMEM),
)
BACK_SCRATCH = dict(
    grads_all=((4, 128, 576), LOW),
    stats_all=((4, 2, 16, 128), WIDE),
    grads_a=((ROWS_A, 1536), LOW),
    bias_back=((1024, 128), WIDE),
    dq_total=((4, 3, 64, 384), WIDE),
    dkv_total=((2, 3, 1024, 128), WIDE),
    branch=((128, 576), LOW),
    grad_gate=((128, 1536), LOW),
    grad_up=((128, 1536), LOW),
    grad_branch=((128, 576), LOW),
    grad_attended=((128, 576), LOW),
    stats=((2, 16, 128), WIDE),
    mlp_gain=((2, 16, 384), WIDE),
    mlp_gain_pair=((2, 16, 384), WIDE),
    **pair_scratch(
        ("attended", "normed_two", "inner", "branch", "grad_gate", "grad_up", "grad_branch")
    ),
)


def turn_body(refs, copies):
    loads = load(
        copies, [(getattr(refs, name + LOWER), getattr(refs, name + HERE)) for name in LATER]
    )
    greet([core_peer(), *line_peers("xzy")])
    attend(refs)
    swapped = swap_partials(refs, copies)
    wait_all(loads)
    wait_all(swapped)
    gain = gain_row(refs.gains, 3)
    rows = merge_and_feed(refs, refs.hidden[...], gain)
    refs.activations[...] = rows.astype(LOW)
    sums = [reduce_of(refs, copies, refs.grads_a, refs.red_a, TAIL_A)]
    feed_back(refs, copies, refs.cotangent[...].astype(WIDE), gain, sums, lambda: None)
    attend_back(refs, sums)


SUMS = dict(
    dq_in=((3, MODEL_WIDTH, 128), LOW),
    first=((2, 3, 4, HALF, 384), LOW),
    midway=((2, 4, HALF, 384), LOW),
    second=((2, 3, HALF, 384), LOW),
    dkv_sum=((128, 384), WIDE),
    grad_qkv=((128, 960), LOW),
    grad_qkv_pair=((2, 128, 960), LOW),
    attn_gain=((2, 16, 384), WIDE),
    attn_gain_pair=((2, 16, 384), WIDE),
)


def sum_and_project_back(refs, copies, hidden, gain, first, second):
    _, x, z, y = coords()
    one, turned = [[], []], []
    for d in (1, 2, 3):
        one[0].append(
            copies.remote(
                refs.dkv.at[0, (z + d) % 4], refs.first.at[0, d - 1], line_peer("z", d)
            )
        )
        one[1].append(
            copies.remote(
                refs.dkv.at[1, (y + d) % 4], refs.first.at[1, d - 1], line_peer("y", d)
            )
        )
    for d in (1, 2, 3):
        turned.append(
            copies.remote(refs.dq.at[(x + d) % 4], refs.dq_in.at[d - 1], line_peer("x", d))
        )
    first()
    two = [[], []]
    for half, mine, axis, there in ((0, z, "y", y), (1, y, "z", z)):
        wait_all(one[half])
        total = refs.dkv[half, mine].astype(WIDE)
        for d in range(3):
            total = total + refs.first[half, d].astype(WIDE)
        refs.midway[half] = total.astype(LOW)
        for d in (1, 2, 3):
            two[half].append(
                copies.remote(
                    refs.midway.at[half, (there + d) % 4],
                    refs.second.at[half, d - 1],
                    line_peer(axis, d),
                )
            )
    second()
    wait_all(turned)
    total = refs.dq[x].astype(WIDE)
    for d in range(3):
        total = total + refs.dq_in[d].astype(WIDE)
    grad_queries = total.T
    for half, there in ((0, y), (1, z)):
        wait_all(two[half])
        total = refs.midway[half, there].astype(WIDE)
        for d in range(3):
            total = total + refs.second[half, d].astype(WIDE)
        refs.dkv_sum[half * HALF : (half + 1) * HALF, :] = total
    summed = refs.dkv_sum[...]
    keys = [summed[:, 128 * group : 128 * group + 64] for group in range(3)]
    values = [summed[:, 128 * group + 64 : 128 * group + 128] for group in range(3)]
    back = rotate(
        jnp.concatenate([grad_queries, *keys], axis=1), refs.cosine[...], -refs.sine[...]
    )
    joined = jnp.concatenate([back, *values], axis=1).astype(LOW)
    refs.grad_qkv[...] = joined
    sent = swap_cores(copies, refs.grad_qkv, refs.grad_qkv_pair, True)
    grad_normed = (
        dot_t(joined[:, 0:576], refs.wq_here[...])
        + dot_t(joined[:, 576:768], refs.wk_here[...])
        + dot_t(joined[:, 768:960], refs.wv_here[...])
    )
    inverse = inverse_rms(hidden)
    put_gain_halves(refs.attn_gain, jnp.sum(hidden * inverse * grad_normed, axis=0, keepdims=True))
    more = swap_cores(copies, refs.attn_gain, refs.attn_gain_pair, False)
    grad = refs.grad_before[...] + norm_back(grad_normed, hidden, inverse, gain)
    return grad, [sent, more]


def down_body(refs, copies):
    loads = load(
        copies,
        [
            (getattr(refs, name + LOWER), getattr(refs, name + HERE))
            for name in (*QKV, *LATER)
        ],
    )
    greet([core_peer(), *line_peers("xzy")])
    spread = Spread(copies, refs.red_above, refs.sum_a1)

    def first():
        spread.start()
        wait_all(loads)

    grad, sent = sum_and_project_back(
        refs, copies, refs.hidden[...], gain_row(refs.gains, 1), first, spread.second
    )

    def beside():
        wait_all(sent)
        grads_b(refs.grads_b, refs.normed_above, refs.grad_qkv_pair, refs.attn_gain_pair)

    sums = [
        reduce_of(refs, copies, refs.grads_a, refs.red_a, TAIL_A),
        reduce_of(refs, copies, refs.grads_b, refs.red_b, TAIL_B),
    ]
    feed_back(refs, copies, grad, gain_row(refs.gains, 2), sums, beside)
    spread.finish()
    attend_back(refs, sums)


def last_body(refs, copies):
    loads = load(
        copies, [(getattr(refs, name + LOWER), getattr(refs, name + HERE)) for name in QKV]
    )
    mirror = mirror_peer()
    greet([core_peer(), mirror, *line_peers("xzy")])
    high = pl.ds(HALF, HALF)
    spreads = [
        Spread(copies, refs.red_a, refs.sum_a0),
        Spread(copies, refs.red_b, refs.sum_b1),
    ]

    def first():
        for spread in spreads:
            spread.start()
        wait_all(loads)

    def second():
        for spread in spreads:
            spread.second()

    grad, sent = sum_and_project_back(
        refs, copies, refs.tokens[...].astype(WIDE), gain_row(refs.gains, 0), first, second
    )
    wait_all(sent)
    grads_b(refs.grads_low, refs.normed_pair, refs.grad_qkv_pair, refs.attn_gain_pair)
    reduce = Reduce(
        copies, refs.grads_low, refs.one, refs.sum_one, refs.two, refs.three, refs.red
    )
    reduce.start()
    refs.grad[...] = grad
    refs.grad_out[0:HALF] = grad[0:HALF]
    refs.acts_out[0:HALF] = refs.acts[0:HALF]
    rows = [
        copies.remote(refs.grad.at[high], refs.grad_out.at[high], mirror),
        copies.remote(refs.acts.at[high], refs.acts_out.at[high], mirror),
    ]
    reduce.second()
    reduce.third()
    reduce.finish()
    last = Spread(copies, refs.red, refs.sum_b0)
    last.start()
    last.second()
    wait_all(rows)
    for spread in [*spreads, last]:
        spread.finish()


def results_kernel(
    acts, grads, a0, a1, b0, b1, acts_t, grads_t, ga, wq, wk, wv, wo, gm, wg, wu, wd
):
    wide = jnp.float32
    acts_t[...] = acts[...].astype(wide).T.astype(acts_t.dtype)
    grads_t[...] = grads[...].T
    for layer, (a, b) in enumerate(((a0, b0), (a1, b1))):
        wg[layer] = a[0:288, :].astype(wide)
        wu[layer] = a[288:576, :].astype(wide)
        wd[layer, 0:288] = a[576:864, 0:768].astype(wide)
        wd[layer, 288:576] = a[576:864, 768:1536].astype(wide)
        wo[layer, 0:144] = a[864:1008, 0:576].astype(wide)
        wo[layer, 144:288] = a[864:1008, 640:1216].astype(wide)
        gm[layer : layer + 1, :] = a[1008:1024, 0:288].astype(wide)[0:1]
        wq[layer, 0:144] = b[0:144, 0:576].astype(wide)
        wq[layer, 144:288] = b[0:144, 640:1216].astype(wide)
        for at in range(3):
            rows = slice(at * 96, at * 96 + 96)
            wk[layer, rows] = b[144:240, at * 384 : at * 384 + 192].astype(wide)
            wv[layer, rows] = b[144:240, at * 384 + 192 : at * 384 + 384].astype(wide)
        ga[layer : layer + 1, :] = b[240:256, 0:288].astype(wide)[0:1]


def results(*args):
    shapes = [
        (2, 288),
        (2, 288, 576),
        (2, 288, 192),
        (2, 288, 192),
        (2, 288, 576),
        (2, 288),
        (2, 288, 1536),
        (2, 288, 1536),
        (2, 576, 768),
    ]
    acts, grads, *gradients, down = pl.pallas_call(
        results_kernel,
        out_shape=[
            shape_of((MODEL_WIDTH, 128), jnp.bfloat16),
            shape_of((MODEL_WIDTH, 128), jnp.float32),
            *[shape_of(shape, jnp.float32) for shape in shapes],
        ],
        in_specs=[VMEM] * 6,
        out_specs=[VMEM] * 11,
        compiler_params=pltpu.CompilerParams(vmem_limit_bytes=56 << 20),
        name="results",
    )(*args)
    return (acts.T, grads.T, *gradients, down.transpose(0, 2, 1))


def attend_back(refs, sums):
    q_ref, kv_ref, do_ref = refs.queries_in, refs.kv_in, refs.grads_all
    stats_ref, starts_ref, bias = refs.stats_all, refs.starts, refs.bias_back
    dq, dkv = refs.dq_total, refs.dkv_total
    dq[...] = jnp.zeros(dq.shape, jnp.float32)
    dkv[...] = jnp.zeros(dkv.shape, jnp.float32)

    def step_body(step, carry):
        section, quarter = unit_places(step)
        bias[...] = unit_bias(section, quarter, starts_ref)
        lane = lax.broadcasted_iota(jnp.int32, (1, 128), 1)
        stats = jnp.where(lane < HALF, stats_ref[quarter], stats_ref[3 - quarter])
        for group in range(3):
            queries = head_rows(q_ref, quarter, group)
            grads = head_rows(do_ref, quarter, group)
            keys = kv_ref[section, :, group * 128 : group * 128 + 64]
            values = kv_ref[section, :, group * 128 + 64 : group * 128 + 128]
            heads = range(3 * group, 3 * group + 3)
            logs = jnp.concatenate([stats[0, h : h + 1, :] for h in heads], axis=1)
            delta = jnp.concatenate([stats[1, h : h + 1, :] for h in heads], axis=1)
            scores = contract(keys, queries, 1, 1)
            tile = bias[...]
            scores = scores + jnp.concatenate([tile, tile, tile], axis=1)
            weights = jnp.exp(scores - logs)
            grad_weights = contract(values, grads, 1, 1)
            grad_scores = (weights * (grad_weights - delta)).astype(jnp.bfloat16)
            grad_values = contract(weights.astype(jnp.bfloat16), grads, 1, 0)
            grad_keys = contract(grad_scores, queries, 1, 0)
            dkv[section, group] += jnp.concatenate([grad_keys, grad_values], axis=1)
            dq[quarter, group] += contract(keys, grad_scores, 0, 0)
        @pl.when(step == 2)
        def _():
            for item in sums:
                item.second()

        @pl.when(step == 3)
        def _():
            for item in sums:
                item.third()

        return carry

    lax.fori_loop(0, 5, step_body, 0)
    lane = lax.broadcasted_iota(jnp.int32, (1, 128), 1)
    for chunk in range(4):
        for head in range(QUERY_HEADS):
            group, part = head // 3, slice((head % 3) * 128, (head % 3) * 128 + 128)
            picked = jnp.where(
                lane < HALF, dq[chunk, group][:, part], dq[3 - chunk, group][:, part]
            )
            refs.dq_out[chunk, head * 64 : head * 64 + 64, :] = (picked * 0.125).astype(jnp.bfloat16)
    for section in range(2):
        for group in range(3):
            refs.dkv_out[section, :, group * 128 : group * 128 + 128] = dkv[section, group].astype(
                jnp.bfloat16
            )
    for item in sums:
        item.finish()


SUM_SCRATCH = ("one", "sum_one", "two", "three")


def reduce_refs(rows, tail):
    names = [name + tail for name in SUM_SCRATCH]
    shapes = [(3, 3, rows, 128), (3, rows, 128), (3, 3, rows // 4, 128), (3, 4, rows // 4, 128)]
    return {name: (shape, jnp.bfloat16) for name, shape in zip(names, shapes)}


def reduce_of(refs, copies, source, target, tail):
    return Reduce(
        copies, source, *[getattr(refs, name + tail) for name in SUM_SCRATCH], target
    )


def sequence_starts(lengths, rows):
    ends = jnp.cumsum(lengths)
    begins = ends - lengths
    segment = jnp.sum((rows[..., None] >= ends).astype(jnp.int32), axis=-1)
    labels = jnp.arange(lengths.shape[0], dtype=jnp.int32)
    return jnp.sum(jnp.where(segment[..., None] == labels, begins, 0), axis=-1)


def rope_tables(position):
    half = HEAD_SIZE // 2
    freqs = jnp.exp(jnp.arange(half, dtype=jnp.float32) * (-2.0 * math.log(10000.0) / HEAD_SIZE))
    angles = position.astype(jnp.float32)[:, None] * freqs[None, :]
    return jnp.cos(angles), jnp.sin(angles)


def per_device(
    tokens,
    seq_lengths,
    attn_gain,
    w_query,
    key_weight,
    value_weight,
    w_out,
    mlp_gain,
    w_gate,
    w_up,
    w_down,
    cotangent,
):
    lengths = seq_lengths[0]
    rep = lax.axis_index("rep")
    x, line = rep // 16, rep % 16
    inside = jnp.arange(128, dtype=jnp.int32)
    chunk = jnp.arange(4, dtype=jnp.int32)[:, None] * 16 + line
    rows_all = jnp.where(
        inside[None, :] < HALF,
        chunk * 128 + inside[None, :],
        (127 - 2 * chunk) * HALF + inside[None, :] - HALF,
    )
    starts = sequence_starts(lengths, rows_all)
    position = jnp.where(
        inside < HALF, rep * 128 + inside, (127 - 2 * rep) * HALF + inside - HALF
    ) - sequence_starts(
        lengths,
        jnp.where(inside < HALF, rep * 128 + inside, (127 - 2 * rep) * HALF + inside - HALF),
    )
    cosine, sine = rope_tables(position)
    cosine = jnp.concatenate([cosine] * 4, axis=1)
    sine = jnp.concatenate([-sine, sine] * 2, axis=1)
    tables = dict(cosine=(cosine, VMEM), sine=(sine, VMEM))
    gains = jnp.pad(jnp.concatenate([attn_gain, mlp_gain]), ((0, 12), (0, 96)))
    params = dict(zip(WEIGHTS, (w_query, key_weight, value_weight, w_out, w_gate, w_up, w_down.transpose(0, 2, 1))))
    raw = {name: (value, ANY) for name, value in params.items()}
    sources = dict(queries=((128, 576), LOW), kv=((128, 384), LOW))

    def kept_weights(result, names):
        return {name + LOWER: (getattr(result, name + ALL), ANY) for name in names}

    def kept_rows(result, names):
        return {name: (getattr(result, name), VMEM) for name in names}

    zero = named_call(
        start_body,
        "start",
        0,
        dict(
            tokens=(tokens.T, VMEM),
            cotangent=(cotangent.T, VMEM),
            gains=(gains, VMEM),
            **tables,
            **raw,
        ),
        dict(
            tokens_out=((128, 576), LOW, VMEM),
            cotangent_out=((128, 576), LOW, VMEM),
            gains_out=((2, 16, 384), LOW, VMEM),
            **gather_outs(),
            **weight_outs(),
        ),
        dict(
            **sources,
            **weight_stages(),
            **weight_loads(QKV),
            token_rows=((128, 576), LOW),
            cotangent_rows=((128, 576), LOW),
        ),
    )
    gains = (zero.gains_out, VMEM)
    tokens = (zero.tokens_out, VMEM)
    one = named_call(
        between_body,
        "between",
        1,
        dict(
            queries_in=(zero.queries_all, VMEM),
            kv_in=(zero.kv_all.reshape(2, 1024, 384), VMEM),
            starts=(starts, VMEM),
            tokens=tokens,
            gains=gains,
            **tables,
            **raw,
            **kept_weights(zero, LATER),
        ),
        dict(
            hidden=((128, 576), WIDE, VMEM),
            **{name: (*kind, VMEM) for name, kind in FEED.items()},
            **gather_outs(),
            **weight_outs(),
        ),
        {**sources, **ATTEND, **PARTIALS, **weight_stages(), **weight_loads([*QKV, *LATER])},
    )
    back_one = named_call(
        turn_body,
        "turn",
        2,
        dict(
            queries_in=(one.queries_all, VMEM),
            kv_in=(one.kv_all.reshape(2, 1024, 384), VMEM),
            starts=(starts, VMEM),
            hidden=(one.hidden, VMEM),
            cotangent=(zero.cotangent_out, VMEM),
            gains=gains,
            normed=(one.normed, VMEM),
            **kept_weights(one, LATER),
        ),
        dict(activations=((128, 576), LOW, VMEM), **BACK_OUTS),
        {**FEED, **ATTEND, **PARTIALS, **BACK_SCRATCH, **reduce_refs(ROWS_A, TAIL_A), **weight_loads(LATER)},
    )
    back_zero = named_call(
        down_body,
        "down",
        3,
        dict(
            dq=(back_one.dq_out, VMEM),
            dkv=(back_one.dkv_out.reshape(2, 4, 4, HALF, 384), VMEM),
            queries_in=(zero.queries_all, VMEM),
            kv_in=(zero.kv_all.reshape(2, 1024, 384), VMEM),
            starts=(starts, VMEM),
            hidden=(one.hidden, VMEM),
            grad_before=(back_one.grad_middle, VMEM),
            gains=gains,
            normed=(zero.normed, VMEM),
            normed_above=(back_one.normed_pair, VMEM),
            red_above=(back_one.red_a, VMEM),
            **tables,
            **kept_rows(one, FEED),
            **kept_weights(one, QKV),
            **kept_weights(zero, LATER),
        ),
        dict(
            red_b=((3, ROWS_B // 4, 128), LOW, VMEM),
            sum_a1=((ROWS_A, 1536), LOW, VMEM),
            **BACK_OUTS,
        ),
        dict(
            **SUMS,
            **BACK_SCRATCH,
            **reduce_refs(ROWS_A, TAIL_A),
            **reduce_refs(ROWS_B, TAIL_B),
            grads_b=((ROWS_B, 1536), LOW),
            **weight_loads([*QKV, *LATER]),
        ),
    )
    end = named_call(
        last_body,
        "last",
        4,
        dict(
            dq=(back_zero.dq_out, VMEM),
            dkv=(back_zero.dkv_out.reshape(2, 4, 4, HALF, 384), VMEM),
            tokens=tokens,
            acts=(back_one.activations, VMEM),
            grad_before=(back_zero.grad_middle, VMEM),
            gains=gains,
            normed_pair=(back_zero.normed_pair, VMEM),
            red_a=(back_zero.red_a, VMEM),
            red_b=(back_zero.red_b, VMEM),
            **tables,
            **kept_weights(zero, QKV),
        ),
        dict(
            acts_out=((128, 576), LOW, VMEM),
            grad_out=((128, 576), WIDE, VMEM),
            sum_a0=((ROWS_A, 1536), LOW, VMEM),
            sum_b1=((ROWS_B, 1536), LOW, VMEM),
            sum_b0=((ROWS_B, 1536), LOW, VMEM),
        ),
        dict(
            **SUMS,
            **weight_loads(QKV),
            grad=((128, 576), WIDE),
            grads_low=((ROWS_B, 1536), LOW),
            one=((3, 3, ROWS_B, 128), LOW),
            sum_one=((3, ROWS_B, 128), LOW),
            two=((3, 3, ROWS_B // 4, 128), LOW),
            three=((3, 4, ROWS_B // 4, 128), LOW),
            red=((3, ROWS_B // 4, 128), LOW),
        ),
    )
    return results(
        end.acts_out, end.grad_out, end.sum_a0, back_zero.sum_a1, end.sum_b0, end.sum_b1
    )


def solution(mesh):
    rows = P(("shard", "rep"), None)
    gain, weight = P(None, "shard"), P(None, "shard", None)
    return jax.shard_map(
        per_device,
        mesh=mesh,
        in_specs=(
            rows,
            P("shard", None),
            gain,
            weight,
            weight,
            weight,
            weight,
            gain,
            weight,
            weight,
            weight,
            rows,
        ),
        out_specs=(
            rows,
            rows,
            gain,
            weight,
            weight,
            weight,
            weight,
            gain,
            weight,
            weight,
            weight,
        ),
        check_vma=False,
    )
```

```python
import functools
import math
from types import SimpleNamespace

import jax
import jax.numpy as jnp
from jax import lax
from jax.experimental import pallas as pl
from jax.experimental.pallas import tpu as pltpu
from jax.sharding import PartitionSpec as P

QUERY_HEADS = 9
KEY_VALUE_HEADS = 3
HEAD_SIZE = 64
DECODER_LAYERS = 2
MODEL_WIDTH = 576
HALF = 64
EPSILON = 1e-05
LOWEST = -1e30
FLOOR = -1e20

MESH = pl.DeviceIdType.MESH
ANY = pl.BlockSpec(memory_space=pl.ANY)
VMEM = pl.BlockSpec(memory_space=pltpu.VMEM)


def coords():
    rep = lax.axis_index("rep")
    return lax.axis_index("shard"), rep // 16, (rep // 4) % 4, rep % 4


def device(core, x, z, y):
    return (core, x * 16 + z * 4 + y)


def line_peer(axis, step):
    core, x, z, y = coords()
    if axis == "x":
        return device(core, (x + step) % 4, z, y)
    if axis == "z":
        return device(core, x, (z + step) % 4, y)
    return device(core, x, z, (y + step) % 4)


def core_peer():
    core, x, z, y = coords()
    return device(1 - core, x, z, y)


def mirror_peer():
    core, x, z, y = coords()
    return device(core, 3 - x, 3 - z, 3 - y)


def greet(peers):
    barrier = pltpu.get_barrier_semaphore()
    for peer in peers:
        pl.semaphore_signal(barrier, inc=1, device_id=peer, device_id_type=MESH)
    pl.semaphore_wait(barrier, len(peers))


def line_peers(axes):
    return [line_peer(axis, step) for axis in axes for step in (1, 2, 3)]


def named_call(body, name, cid, ins, outs, scratch):
    keys = [*ins, *outs, *scratch]

    def kernel(*refs):
        sems = refs[len(keys) :]
        body(SimpleNamespace(**dict(zip(keys, refs))), Copies(*sems))

    results = pl.pallas_call(
        kernel,
        out_shape=[shape_of(shape, dtype) for shape, dtype, _ in outs.values()],
        in_specs=[spec for _, spec in ins.values()],
        out_specs=[spec for _, _, spec in outs.values()],
        scratch_shapes=[
            *[pltpu.VMEM(shape, dtype) for shape, dtype in scratch.values()],
            pltpu.SemaphoreType.DMA((224,)),
            pltpu.SemaphoreType.DMA((224,)),
            pltpu.SemaphoreType.DMA((40,)),
        ],
        compiler_params=pltpu.CompilerParams(
            collective_id=cid, has_side_effects=True, vmem_limit_bytes=60 << 20
        ),
        name=name,
    )(*[array for array, _ in ins.values()])
    return SimpleNamespace(**dict(zip(outs, results)))


class Copies:
    def __init__(self, send, recv, local):
        self.send, self.recv, self.local = send, recv, local
        self.remotes, self.locals = 0, 0

    def reserve(self, count):
        first = self.remotes
        self.remotes += count
        return first

    def describe(self, src, dst, peer, at):
        return pltpu.make_async_remote_copy(
            src_ref=src,
            dst_ref=dst,
            send_sem=self.send.at[at],
            recv_sem=self.recv.at[at],
            device_id=peer,
            device_id_type=MESH,
        )

    def remote(self, src, dst, peer):
        copy = self.describe(src, dst, peer, self.reserve(1))
        copy.start()
        return copy

    def here(self, src, dst):
        copy = pltpu.make_async_copy(src, dst, self.local.at[self.locals])
        self.locals += 1
        copy.start()
        return copy


def comm_call(kernel, name, cid, args, outs, in_specs, out_specs, remotes, locals_, scratch=()):
    return pl.pallas_call(
        kernel,
        out_shape=outs,
        in_specs=in_specs,
        out_specs=out_specs,
        scratch_shapes=[
            pltpu.SemaphoreType.DMA((remotes,)),
            pltpu.SemaphoreType.DMA((remotes,)),
            pltpu.SemaphoreType.DMA((max(locals_, 1),)),
            *scratch,
        ],
        compiler_params=pltpu.CompilerParams(
            collective_id=cid, has_side_effects=True, vmem_limit_bytes=56 << 20
        ),
        name=name,
    )(*args)


def shape_of(shape, dtype):
    return jax.ShapeDtypeStruct(shape, dtype)


def unit_places(step):
    x = lax.axis_index("rep") // 16
    in_odd = step >= 4 - x
    section = jnp.where(in_odd, 1, 0)
    quarter = jnp.where(in_odd, step - 1, x + step)
    return section, quarter


def unit_bias(section, quarter, starts_ref):
    rep = lax.axis_index("rep")
    x, line = rep // 16, rep % 16
    row = lax.broadcasted_iota(jnp.int32, (1024, 128), 0)
    block, inside = row // HALF, row % HALF
    even_key = (16 * x + block) * 128 + inside
    odd_key = (127 - 2 * (16 * x + (block % 4) * 4 + block // 4)) * HALF + inside
    key = jnp.where(section == 1, odd_key, even_key)
    lane = lax.broadcasted_iota(jnp.int32, (1, 128), 1)
    even_query = (16 * quarter + line) * 128 + lane
    odd_query = (127 - 2 * (16 * (3 - quarter) + line)) * HALF + lane - HALF
    query = jnp.where(lane < HALF, even_query, odd_query)
    begin = jnp.where(
        lane < HALF, starts_ref[pl.ds(quarter, 1), :], starts_ref[pl.ds(3 - quarter, 1), :]
    )
    return jnp.where((key <= query) & (key >= begin), 0.0, LOWEST)


def head_rows(ref, quarter, group):
    parts = []
    for head in range(3 * group, 3 * group + 3):
        columns = slice(head * HEAD_SIZE, (head + 1) * HEAD_SIZE)
        parts.append(ref[quarter, 0:HALF, columns])
        parts.append(ref[3 - quarter, HALF : 2 * HALF, columns])
    return jnp.concatenate(parts, axis=0)


def contract(left, right, left_dim, right_dim):
    return lax.dot_general(
        left, right, (((left_dim,), (right_dim,)), ((), ())), preferred_element_type=jnp.float32
    )


def attend_kernel(q_ref, kv_ref, starts_ref, o_ref, lse_ref, bias, best, total, accum):
    best[...] = jnp.full(best.shape, FLOOR, jnp.float32)
    total[...] = jnp.zeros(total.shape, jnp.float32)
    accum[...] = jnp.zeros(accum.shape, jnp.float32)

    def unit(section, quarter):
        bias[...] = unit_bias(section, quarter, starts_ref)
        for group in range(3):
            queries = head_rows(q_ref, quarter, group)
            keys = kv_ref[section, :, group * 128 : group * 128 + 64]
            values = kv_ref[section, :, group * 128 + 64 : group * 128 + 128]
            scores = contract(keys, queries, 1, 1)
            tile = bias[...]
            scores = scores + jnp.concatenate([tile, tile, tile], axis=1)
            old = best[quarter, group]
            new = jnp.maximum(old, jnp.max(scores, axis=0, keepdims=True))
            expon = jnp.exp(scores - new)
            decay = jnp.exp(old - new)
            best[quarter, group] = new
            total[quarter, group] = total[quarter, group] * decay + jnp.sum(
                expon, axis=0, keepdims=True
            )
            accum[quarter, group] = accum[quarter, group] * decay + contract(
                values, expon.astype(jnp.bfloat16), 0, 0
            )

    def step_body(step, carry):
        section, quarter = unit_places(step)

        @pl.when(section == 0)
        def _():
            unit(0, quarter)

        @pl.when(section == 1)
        def _():
            unit(1, quarter)

        return carry

    lax.fori_loop(0, 5, step_body, 0)
    lane = lax.broadcasted_iota(jnp.int32, (1, 128), 1)
    results, logs = {}, {}
    for quarter in range(4):
        for group in range(3):
            summed = total[quarter, group]
            safe = jnp.where(summed > 0.0, summed, 1.0)
            results[quarter, group] = accum[quarter, group] / safe
            logs[quarter, group] = best[quarter, group] + jnp.log(safe)
    for chunk in range(4):
        rows = []
        for head in range(QUERY_HEADS):
            group, part = head // 3, slice((head % 3) * 128, (head % 3) * 128 + 128)
            o_ref[chunk, head * 64 : head * 64 + 64, :] = jnp.where(
                lane < HALF, results[chunk, group][:, part], results[3 - chunk, group][:, part]
            ).astype(jnp.bfloat16)
            rows.append(
                jnp.where(lane < HALF, logs[chunk, group][:, part], logs[3 - chunk, group][:, part])
            )
        rows.append(jnp.zeros((7, 128), jnp.float32))
        lse_ref[chunk] = jnp.concatenate(rows, axis=0)


ATTEND = dict(
    partial=((4, MODEL_WIDTH, 128), jnp.bfloat16),
    logs=((4, 16, 128), jnp.float32),
    bias=((1024, 128), jnp.float32),
    best=((4, 3, 1, 384), jnp.float32),
    total=((4, 3, 1, 384), jnp.float32),
    accum=((4, 3, 64, 384), jnp.float32),
)


def attend(refs):
    attend_kernel(
        refs.queries_in,
        refs.kv_in,
        refs.starts,
        refs.partial,
        refs.logs,
        refs.bias,
        refs.best,
        refs.total,
        refs.accum,
    )


ORDERS = ("xzy", "zyx", "yxz")


def part_columns(part, at):
    return pl.ds(pl.multiple_of(part * 512 + at * 128, 128), 128)


def piece_rows(piece, at):
    return pl.ds(pl.multiple_of(at * piece, 16), piece)


def places():
    _, x, z, y = coords()
    return dict(x=x, z=z, y=y)


def reduce_scratch(rows):
    return [
        pltpu.VMEM((3, 3, rows, 128), jnp.bfloat16),
        pltpu.VMEM((3, rows, 128), jnp.bfloat16),
        pltpu.VMEM((3, 3, rows // 4, 128), jnp.bfloat16),
        pltpu.VMEM((3, 4, rows // 4, 128), jnp.bfloat16),
    ]


class Reduce:
    def __init__(self, copies, source, one, sum_one, two, three, target):
        self.copies, self.source, self.target = copies, source, target
        self.one, self.sum_one, self.two, self.three = one, sum_one, two, three
        self.piece = source.shape[0] // 4
        self.place = places()
        self.first = copies.reserve(27)

    def legs(self, stage, part):
        axis = ORDERS[part][stage]
        here = self.place[axis]
        made = []
        for d in (1, 2, 3):
            there = (here + d) % 4
            if stage == 0:
                src = self.source.at[:, part_columns(part, there)]
                dst = self.one.at[part, d - 1]
            elif stage == 1:
                src = self.sum_one.at[part, piece_rows(self.piece, there)]
                dst = self.two.at[part, d - 1]
            else:
                src = dst = self.three.at[part, here]
            at = self.first + stage * 9 + part * 3 + d - 1
            made.append(self.copies.describe(src, dst, line_peer(axis, d), at))
        return made

    def go(self, stage, part):
        for copy in self.legs(stage, part):
            copy.start()

    def arrive(self, stage, part):
        for copy in self.legs(stage, part):
            copy.wait()

    def start(self):
        for part in range(3):
            self.go(0, part)

    def second(self):
        for part, order in enumerate(ORDERS):
            self.arrive(0, part)
            total = self.source[:, part_columns(part, self.place[order[0]])].astype(jnp.float32)
            for d in range(3):
                total = total + self.one[part, d].astype(jnp.float32)
            self.sum_one[part] = total.astype(jnp.bfloat16)
            self.go(1, part)

    def third(self):
        for part, order in enumerate(ORDERS):
            self.arrive(1, part)
            mine = piece_rows(self.piece, self.place[order[1]])
            total = self.sum_one[part, mine].astype(jnp.float32)
            for d in range(3):
                total = total + self.two[part, d].astype(jnp.float32)
            self.three[part, self.place[order[2]]] = total.astype(jnp.bfloat16)
            self.go(2, part)

    def finish(self):
        for part in range(3):
            self.arrive(2, part)
            total = self.three[part, 0].astype(jnp.float32)
            for at in (1, 2, 3):
                total = total + self.three[part, at].astype(jnp.float32)
            self.target[part] = total.astype(jnp.bfloat16)


class Spread:
    def __init__(self, copies, pieces, target):
        self.copies, self.pieces, self.target = copies, pieces, target
        self.piece = target.shape[0] // 4
        self.place = places()
        self.first = copies.reserve(18)

    def window(self, stage, part):
        order = ORDERS[part]
        columns = part_columns(part, self.place[order[0]])
        if stage == 0:
            return piece_rows(self.piece, self.place[order[1]]), columns
        return slice(None), columns

    def legs(self, stage, part):
        axis = ORDERS[part][1 - stage]
        block = self.target.at[self.window(stage, part)]
        at = self.first + stage * 9 + part * 3
        return [
            self.copies.describe(block, block, line_peer(axis, d), at + d - 1) for d in (1, 2, 3)
        ]

    def start(self):
        for part in range(3):
            self.target[self.window(0, part)] = self.pieces[part]
            for copy in self.legs(0, part):
                copy.start()

    def second(self):
        for part in range(3):
            for copy in self.legs(0, part):
                copy.wait()
            for copy in self.legs(1, part):
                copy.start()

    def finish(self):
        for part in range(3):
            for copy in self.legs(1, part):
                copy.wait()


ROWS_A, ROWS_B = 1024, 256


def split_wide(matrix):
    gap = jnp.zeros((144, 64), jnp.float32)
    tail = jnp.zeros((144, 320), jnp.float32)
    return jnp.concatenate([matrix[:144], gap, matrix[144:], tail], axis=1)


def rows_of(ref):
    return ref[...].reshape(ref.shape[0] * ref.shape[1], ref.shape[2])


def put_gain(out, row, gains):
    out[row : row + 16, :] = jnp.zeros((16, 1536), jnp.bfloat16)
    out[row : row + 16, 0:384] = (gains[0] + gains[1]).astype(jnp.bfloat16)


WEIGHTS = dict(wq=576, wk=192, wv=192, wo=576, wg=1536, wu=1536, wd=1536)
TAIL_A, TAIL_B, END, HERE_END = "_a", "_b", "_end", "_here_end"
ALL, STAGE, HERE, LOWER, PAIR = "_all", "_stage", "_here", "_low", "_pair"
WIDE = jnp.float32
LOW = jnp.bfloat16


def dot(left, right):
    return contract(left, right, 1, 0)


def dot_t(left, right):
    return contract(left, right, 1, 1)


def inverse_rms(rows):
    return lax.rsqrt(jnp.mean(rows * rows, axis=-1, keepdims=True) + EPSILON)


def norm_back(grad, rows, inverse, gain):
    scaled = grad * gain
    return inverse * scaled - rows * inverse**3 * jnp.mean(scaled * rows, axis=-1, keepdims=True)


def gain_row(gains, row):
    both = gains[...].astype(WIDE)
    return jnp.concatenate(
        [both[0, row : row + 1, 0:288], both[1, row : row + 1, 0:288]], axis=1
    )


def rotate(rows, cosine, sine):
    lane = lax.broadcasted_iota(jnp.int32, (128, 128), 1) % HEAD_SIZE
    tiles = []
    for at in range(0, rows.shape[1], 128):
        tile = rows[:, at : at + 128]
        swapped = jnp.where(lane < 32, pltpu.roll(tile, 96, 1), pltpu.roll(tile, 32, 1))
        tiles.append(tile * cosine + swapped * sine)
    return jnp.concatenate(tiles, axis=1)


def put_halves(ref, rows):
    width = rows.shape[1] // 2
    ref[0] = rows[:, :width].astype(ref.dtype)
    ref[1] = rows[:, width:].astype(ref.dtype)


def get_halves(ref):
    return jnp.concatenate([ref[0], ref[1]], axis=1)


def put_gain_halves(ref, gain):
    ref[...] = jnp.zeros(ref.shape, WIDE)
    ref[0, 0:1, 0:288] = gain[:, 0:288]
    ref[1, 0:1, 0:288] = gain[:, 288:576]


def project(refs, hidden, gain, weights):
    normed = (hidden * inverse_rms(hidden) * gain).astype(LOW)
    put_halves(refs.normed, normed)
    wq, wk, wv = [weight[...] for weight in weights]
    turned = rotate(
        jnp.concatenate([dot(normed, wq), dot(normed, wk)], axis=1), refs.cosine[...], refs.sine[...]
    )
    refs.queries[...] = (turned[:, 0:576] * 0.125).astype(LOW)
    values = dot(normed, wv)
    parts = []
    for group in range(3):
        parts.append(turned[:, 576 + 64 * group : 640 + 64 * group])
        parts.append(values[:, 64 * group : 64 * group + 64])
    refs.kv[...] = jnp.concatenate(parts, axis=1).astype(LOW)


def own_part(refs, name, core):
    whole = getattr(refs, name + ALL)
    if name == "wd":
        return whole.at[:, pl.ds(pl.multiple_of(core * 768, 128), 768)]
    return whole.at[pl.ds(pl.multiple_of(core * 288, 16), 288)]


def whole_shape(name):
    return (MODEL_WIDTH, WEIGHTS[name])


def half_shape(name):
    return (576, 768) if name == "wd" else (288, WEIGHTS[name])


def send_weights(refs, copies, layer, names):
    core = lax.axis_index("shard")
    started = {}
    for name in names:
        own = getattr(refs, name).at[layer]
        started[name] = [copies.remote(own, own_part(refs, name, core), core_peer())]
    return started


def bring_weights(refs, copies, layer, names):
    return {
        name: copies.here(getattr(refs, name).at[layer], getattr(refs, name + STAGE))
        for name in names
    }


def keep_weights(refs, copies, started, inward):
    core = lax.axis_index("shard")
    for name, copy in inward.items():
        copy.wait()
        stage = getattr(refs, name + STAGE)
        started[name].append(copies.here(stage, own_part(refs, name, core)))


def load(copies, pairs):
    return [copies.here(source, target) for source, target in pairs]


def wait_all(started):
    for copy in started:
        copy.wait()


def gather_start(refs, copies):
    _, x, z, y = coords()
    even, odd = refs.kv.at[pl.ds(0, HALF)], refs.kv.at[pl.ds(HALF, HALF)]
    even_slot, odd_slot = refs.kv_all.at[0, z, y], refs.kv_all.at[1, y, z]
    first_even = [copies.remote(even, even_slot, line_peer("y", d)) for d in (1, 2, 3)]
    first_odd = [copies.remote(odd, odd_slot, line_peer("z", d)) for d in (1, 2, 3)]
    first_even.append(copies.here(even, even_slot))
    first_odd.append(copies.here(odd, odd_slot))
    slot = refs.queries_all.at[x]
    rest = [copies.remote(refs.queries, slot, line_peer("x", d)) for d in (1, 2, 3)]
    rest.append(copies.here(refs.queries, slot))
    return first_even, first_odd, rest


def gather_finish(refs, copies, flying):
    _, _, z, y = coords()
    first_even, first_odd, rest = flying
    wait_all(first_even)
    block = refs.kv_all.at[0, z]
    rest += [copies.remote(block, block, line_peer("z", d)) for d in (1, 2, 3)]
    wait_all(first_odd)
    block = refs.kv_all.at[1, y]
    rest += [copies.remote(block, block, line_peer("y", d)) for d in (1, 2, 3)]
    wait_all(rest)


def gather_outs():
    return dict(
        queries_all=((4, 128, 576), LOW, ANY),
        kv_all=((2, 4, 4, HALF, 384), LOW, ANY),
        normed=((2, 128, 288), LOW, VMEM),
    )


def weight_outs():
    return {
        name + ALL: (whole_shape(name), LOW, ANY)
        for name in WEIGHTS
    }


def weight_stages():
    return {
        name + STAGE: (half_shape(name), LOW)
        for name in WEIGHTS
    }


def weight_loads(names):
    return {
        name + HERE: (whole_shape(name), LOW) for name in names
    }


QKV, LATER = ("wq", "wk", "wv"), ("wo", "wg", "wu", "wd")


def start_body(refs, copies):
    other, mirror = core_peer(), mirror_peer()
    core = lax.axis_index("shard")
    inward = bring_weights(refs, copies, 0, [*QKV, *LATER])
    refs.token_rows[...] = refs.tokens[...].astype(WIDE).T.astype(LOW)
    refs.cotangent_rows[...] = refs.cotangent[...].astype(WIDE).T.astype(LOW)
    greet([other, mirror, *line_peers("xzy")])
    high = pl.ds(HALF, HALF)
    rows = [
        copies.remote(refs.token_rows.at[high], refs.tokens_out.at[high], mirror),
        copies.remote(refs.gains, refs.gains_out.at[core], other),
    ]
    started = send_weights(refs, copies, 0, QKV)
    cotangent = copies.remote(refs.cotangent_rows.at[high], refs.cotangent_out.at[high], mirror)
    refs.tokens_out[0:HALF] = refs.token_rows[0:HALF]
    refs.cotangent_out[0:HALF] = refs.cotangent_rows[0:HALF]
    refs.gains_out[core] = refs.gains[...]
    keep_weights(refs, copies, started, {name: inward[name] for name in QKV})
    loads = []
    for name in QKV:
        wait_all(started[name])
        loads += load(
            copies, [(getattr(refs, name + ALL), getattr(refs, name + HERE))]
        )
    later = send_weights(refs, copies, 0, LATER)
    wait_all(rows)
    wait_all(loads)
    project(
        refs,
        refs.tokens_out[...].astype(WIDE),
        gain_row(refs.gains_out, 0),
        (refs.wq_here, refs.wk_here, refs.wv_here),
    )
    flying = gather_start(refs, copies)
    keep_weights(refs, copies, later, {name: inward[name] for name in LATER})
    gather_finish(refs, copies, flying)
    cotangent.wait()
    for name in LATER:
        wait_all(later[name])


def swap_partials(refs, copies):
    _, x, _, _ = coords()
    started = []
    for d in (1, 2, 3):
        peer = (x + d) % 4
        there = line_peer("x", d)
        started.append(copies.remote(refs.partial.at[peer], refs.partials.at[x], there))
        started.append(copies.remote(refs.logs.at[peer], refs.logs_all.at[x], there))
    refs.partials[x] = refs.partial[x]
    refs.logs_all[x] = refs.logs[x]
    return started


def merge_and_feed(refs, hidden, gain):
    logs = refs.logs_all[...]
    largest = jnp.max(logs, axis=0)
    shares = jnp.exp(logs - largest)
    total = jnp.sum(shares, axis=0)
    refs.lse[...] = largest + jnp.log(total)
    shares = shares / total
    for head in range(QUERY_HEADS):
        rows = slice(head * HEAD_SIZE, (head + 1) * HEAD_SIZE)
        outcome = jnp.zeros((HEAD_SIZE, 128), WIDE)
        for at in range(4):
            outcome += shares[at, head : head + 1, :] * refs.partials[at, rows, :].astype(WIDE)
        refs.outcome[rows, :] = outcome
    attended = refs.outcome[...].T.astype(LOW)
    put_halves(refs.attended, attended)
    middle = hidden + dot(attended, refs.wo_here[...])
    refs.middle[...] = middle
    normed_two = (middle * inverse_rms(middle) * gain).astype(LOW)
    put_halves(refs.normed_two, normed_two)
    gate = dot(normed_two, refs.wg_here[...])
    up = dot(normed_two, refs.wu_here[...])
    refs.gate[...] = gate
    refs.up[...] = up
    inner = (gate * jax.nn.sigmoid(gate) * up).astype(LOW)
    put_halves(refs.inner, inner)
    return middle + dot_t(inner, refs.wd_here[...])


FEED = dict(
    lse=((16, 128), WIDE),
    outcome=((576, 128), WIDE),
    attended=((2, 128, 288), LOW),
    middle=((128, 576), WIDE),
    normed_two=((2, 128, 288), LOW),
    gate=((128, 1536), WIDE),
    up=((128, 1536), WIDE),
    inner=((2, 128, 768), LOW),
)
PARTIALS = dict(partials=((4, 576, 128), LOW), logs_all=((4, 16, 128), WIDE))


def between_body(refs, copies):
    names = [*QKV, *LATER]
    loads = load(
        copies, [(getattr(refs, name + LOWER), getattr(refs, name + HERE)) for name in LATER]
    )
    inward = bring_weights(refs, copies, 1, names)
    greet([core_peer(), *line_peers("xzy")])
    started = send_weights(refs, copies, 1, names)
    attend(refs)
    swapped = swap_partials(refs, copies)
    keep_weights(refs, copies, started, inward)
    wait_all(loads)
    wait_all(swapped)
    hidden = merge_and_feed(refs, refs.tokens[...].astype(WIDE), gain_row(refs.gains, 2))
    refs.hidden[...] = hidden
    loads = []
    for name in QKV:
        wait_all(started[name])
        loads += load(
            copies, [(getattr(refs, name + ALL), getattr(refs, name + HERE))]
        )
    wait_all(loads)
    project(refs, hidden, gain_row(refs.gains, 1), (refs.wq_here, refs.wk_here, refs.wv_here))
    gather_finish(refs, copies, gather_start(refs, copies))
    for name in LATER:
        wait_all(started[name])


SWAPS = dict(
    normed=(2, 128, 288),
    attended=(2, 128, 288),
    normed_two=(2, 128, 288),
    inner=(2, 128, 768),
    branch=(128, 576),
    grad_gate=(128, 1536),
    grad_up=(128, 1536),
    grad_branch=(128, 576),
    grad_qkv=(128, 960),
)


def swap_cores(copies, own, pair, whole_array):
    core = lax.axis_index("shard")
    if whole_array:
        pair[core] = own[...]
        return copies.remote(own, pair.at[core], core_peer())
    pair[core] = own[core]
    return copies.remote(own.at[1 - core], pair.at[core], core_peer())


def pair_scratch(names):
    shapes = {}
    for name in names:
        shape = SWAPS[name]
        shapes[name + PAIR] = (shape if len(shape) == 3 else (2,) + shape, LOW)
    return shapes


def rows_of(ref):
    return ref[...].reshape(ref.shape[0] * ref.shape[1], ref.shape[2])


def split_wide(matrix):
    gap = jnp.zeros((144, 64), WIDE)
    tail = jnp.zeros((144, 320), WIDE)
    return jnp.concatenate([matrix[:144], gap, matrix[144:], tail], axis=1)


def put_gain(out, row, gains):
    out[row : row + 16, :] = jnp.zeros((16, 1536), LOW)
    out[row : row + 16, 0:384] = (gains[0] + gains[1]).astype(LOW)


def grads_b(out, normed, qkv, gains):
    grad = contract(rows_of(normed), rows_of(qkv), 0, 0)
    out[0:144, :] = split_wide(grad[:, 0:576]).astype(LOW)
    rest = grad[:, 576:960].astype(LOW)
    for at in range(3):
        out[144:240, at * 384 : (at + 1) * 384] = rest[at * 96 : (at + 1) * 96]
    out[144:240, 1152:1536] = jnp.zeros((96, 384), LOW)
    put_gain(out, 240, gains)


def feed_back(refs, copies, grad, gain, sums, beside):
    _, x, _, _ = coords()
    flying = SimpleNamespace()
    flying.normed = swap_cores(copies, refs.normed, refs.normed_pair, False)
    flying.attended = swap_cores(copies, refs.attended, refs.attended_pair, False)
    flying.normed_two = swap_cores(copies, refs.normed_two, refs.normed_two_pair, False)
    flying.inner = swap_cores(copies, refs.inner, refs.inner_pair, False)
    branch = grad.astype(LOW)
    refs.branch[...] = branch
    flying.branch = swap_cores(copies, refs.branch, refs.branch_pair, True)
    grad_inner = dot(branch, refs.wd_here[...])
    gate = refs.gate[...]
    sigma = jax.nn.sigmoid(gate)
    refs.grad_gate[...] = (
        grad_inner * refs.up[...] * sigma * (1.0 + gate * (1.0 - sigma))
    ).astype(LOW)
    refs.grad_up[...] = (grad_inner * gate * sigma).astype(LOW)
    flying.grad_gate = swap_cores(copies, refs.grad_gate, refs.grad_gate_pair, True)
    flying.grad_up = swap_cores(copies, refs.grad_up, refs.grad_up_pair, True)
    grad_normed = dot_t(refs.grad_gate[...], refs.wg_here[...]) + dot_t(
        refs.grad_up[...], refs.wu_here[...]
    )
    middle = refs.middle[...]
    inverse = inverse_rms(middle)
    put_gain_halves(refs.mlp_gain, jnp.sum(middle * inverse * grad_normed, axis=0, keepdims=True))
    flying.mlp_gain = swap_cores(copies, refs.mlp_gain, refs.mlp_gain_pair, False)
    grad_middle = grad + norm_back(grad_normed, middle, inverse, gain)
    refs.grad_middle[...] = grad_middle
    low = grad_middle.astype(LOW)
    refs.grad_branch[...] = low
    flying.grad_branch = swap_cores(copies, refs.grad_branch, refs.grad_branch_pair, True)
    refs.grad_attended[...] = dot_t(low, refs.wo_here[...]).astype(LOW)
    slot = refs.grads_all.at[x]
    started = [copies.remote(refs.grad_attended, slot, line_peer("x", d)) for d in (1, 2, 3)]
    refs.grads_all[x] = refs.grad_attended[...]
    turned = dot_t(refs.wo_here[...], low).astype(LOW).astype(WIDE) * refs.outcome[...]
    refs.stats[0] = refs.lse[...]
    refs.stats[1, 9:16] = jnp.zeros((7, 128), WIDE)
    for head in range(QUERY_HEADS):
        refs.stats[1, head : head + 1] = jnp.sum(
            turned[head * HEAD_SIZE : (head + 1) * HEAD_SIZE], axis=0, keepdims=True
        )
    slot = refs.stats_all.at[x]
    started += [copies.remote(refs.stats, slot, line_peer("x", d)) for d in (1, 2, 3)]
    refs.stats_all[x] = refs.stats[...]
    wait_all(
        [flying.inner, flying.branch, flying.normed_two, flying.grad_gate, flying.grad_up]
    )
    out = refs.grads_a
    two = rows_of(refs.normed_two_pair)
    out[0:288, :] = contract(two, rows_of(refs.grad_gate_pair), 0, 0).astype(LOW)
    out[288:576, :] = contract(two, rows_of(refs.grad_up_pair), 0, 0).astype(LOW)
    down = contract(rows_of(refs.branch_pair), rows_of(refs.inner_pair), 0, 0).astype(LOW)
    out[576:864, 0:768] = down[0:288]
    out[576:864, 768:1536] = down[288:576]
    flying.attended.wait()
    flying.grad_branch.wait()
    grad_out = contract(rows_of(refs.attended_pair), rows_of(refs.grad_branch_pair), 0, 0)
    out[864:1008, :] = split_wide(grad_out).astype(LOW)
    flying.mlp_gain.wait()
    put_gain(out, 1008, refs.mlp_gain_pair)
    sums[0].start()
    beside()
    for item in sums[1:]:
        item.start()
    flying.normed.wait()
    wait_all(started)


BACK_OUTS = dict(
    dq_out=((4, MODEL_WIDTH, 128), LOW, VMEM),
    dkv_out=((2, 4, 4, HALF, 384), LOW, VMEM),
    red_a=((3, ROWS_A // 4, 128), LOW, VMEM),
    normed_pair=((2, 128, 288), LOW, VMEM),
    grad_middle=((128, 576), WIDE, VMEM),
)
BACK_SCRATCH = dict(
    grads_all=((4, 128, 576), LOW),
    stats_all=((4, 2, 16, 128), WIDE),
    grads_a=((ROWS_A, 1536), LOW),
    bias_back=((1024, 128), WIDE),
    dq_total=((4, 3, 64, 384), WIDE),
    dkv_total=((2, 3, 1024, 128), WIDE),
    branch=((128, 576), LOW),
    grad_gate=((128, 1536), LOW),
    grad_up=((128, 1536), LOW),
    grad_branch=((128, 576), LOW),
    grad_attended=((128, 576), LOW),
    stats=((2, 16, 128), WIDE),
    mlp_gain=((2, 16, 384), WIDE),
    mlp_gain_pair=((2, 16, 384), WIDE),
    **pair_scratch(
        ("attended", "normed_two", "inner", "branch", "grad_gate", "grad_up", "grad_branch")
    ),
)


def turn_body(refs, copies):
    loads = load(
        copies, [(getattr(refs, name + LOWER), getattr(refs, name + HERE)) for name in LATER]
    )
    greet([core_peer(), *line_peers("xzy")])
    attend(refs)
    swapped = swap_partials(refs, copies)
    wait_all(loads)
    wait_all(swapped)
    gain = gain_row(refs.gains, 3)
    rows = merge_and_feed(refs, refs.hidden[...], gain)
    refs.activations[...] = rows.astype(LOW)
    sums = [reduce_of(refs, copies, refs.grads_a, refs.red_a, TAIL_A)]
    feed_back(refs, copies, refs.cotangent[...].astype(WIDE), gain, sums, lambda: None)
    attend_back(refs, sums)


SUMS = dict(
    dq_in=((3, MODEL_WIDTH, 128), LOW),
    first=((2, 3, 4, HALF, 384), LOW),
    midway=((2, 4, HALF, 384), LOW),
    second=((2, 3, HALF, 384), LOW),
    dkv_sum=((128, 384), WIDE),
    grad_qkv=((128, 960), LOW),
    grad_qkv_pair=((2, 128, 960), LOW),
    attn_gain=((2, 16, 384), WIDE),
    attn_gain_pair=((2, 16, 384), WIDE),
)


def sum_and_project_back(refs, copies, hidden, gain, first, second):
    _, x, z, y = coords()
    one, turned = [[], []], []
    for d in (1, 2, 3):
        one[0].append(
            copies.remote(
                refs.dkv.at[0, (z + d) % 4], refs.first.at[0, d - 1], line_peer("z", d)
            )
        )
        one[1].append(
            copies.remote(
                refs.dkv.at[1, (y + d) % 4], refs.first.at[1, d - 1], line_peer("y", d)
            )
        )
    for d in (1, 2, 3):
        turned.append(
            copies.remote(refs.dq.at[(x + d) % 4], refs.dq_in.at[d - 1], line_peer("x", d))
        )
    first()
    two = [[], []]
    for half, mine, axis, there in ((0, z, "y", y), (1, y, "z", z)):
        wait_all(one[half])
        total = refs.dkv[half, mine].astype(WIDE)
        for d in range(3):
            total = total + refs.first[half, d].astype(WIDE)
        refs.midway[half] = total.astype(LOW)
        for d in (1, 2, 3):
            two[half].append(
                copies.remote(
                    refs.midway.at[half, (there + d) % 4],
                    refs.second.at[half, d - 1],
                    line_peer(axis, d),
                )
            )
    second()
    wait_all(turned)
    total = refs.dq[x].astype(WIDE)
    for d in range(3):
        total = total + refs.dq_in[d].astype(WIDE)
    grad_queries = total.T
    for half, there in ((0, y), (1, z)):
        wait_all(two[half])
        total = refs.midway[half, there].astype(WIDE)
        for d in range(3):
            total = total + refs.second[half, d].astype(WIDE)
        refs.dkv_sum[half * HALF : (half + 1) * HALF, :] = total
    summed = refs.dkv_sum[...]
    keys = [summed[:, 128 * group : 128 * group + 64] for group in range(3)]
    values = [summed[:, 128 * group + 64 : 128 * group + 128] for group in range(3)]
    back = rotate(
        jnp.concatenate([grad_queries, *keys], axis=1), refs.cosine[...], -refs.sine[...]
    )
    joined = jnp.concatenate([back, *values], axis=1).astype(LOW)
    refs.grad_qkv[...] = joined
    sent = swap_cores(copies, refs.grad_qkv, refs.grad_qkv_pair, True)
    grad_normed = (
        dot_t(joined[:, 0:576], refs.wq_here[...])
        + dot_t(joined[:, 576:768], refs.wk_here[...])
        + dot_t(joined[:, 768:960], refs.wv_here[...])
    )
    inverse = inverse_rms(hidden)
    put_gain_halves(refs.attn_gain, jnp.sum(hidden * inverse * grad_normed, axis=0, keepdims=True))
    more = swap_cores(copies, refs.attn_gain, refs.attn_gain_pair, False)
    grad = refs.grad_before[...] + norm_back(grad_normed, hidden, inverse, gain)
    return grad, [sent, more]


def down_body(refs, copies):
    loads = load(
        copies,
        [
            (getattr(refs, name + LOWER), getattr(refs, name + HERE))
            for name in (*QKV, *LATER)
        ],
    )
    loads += load(copies, [(getattr(refs, name + END), getattr(refs, name + HERE_END)) for name in QKV])
    greet([core_peer(), mirror_peer(), *line_peers("xzy")])
    spread = Spread(copies, refs.red_above, refs.sum_a1)

    def first():
        spread.start()
        wait_all(loads)

    grad, sent = sum_and_project_back(
        refs, copies, refs.hidden[...], gain_row(refs.gains, 1), first, spread.second
    )

    def beside():
        wait_all(sent)
        grads_b(refs.grads_b, refs.normed_above, refs.grad_qkv_pair, refs.attn_gain_pair)

    sums = [
        reduce_of(refs, copies, refs.grads_a, refs.red_a, TAIL_A),
        reduce_of(refs, copies, refs.grads_b, refs.red_b, TAIL_B),
    ]
    feed_back(refs, copies, grad, gain_row(refs.gains, 2), sums, beside)
    spread.finish()
    attend_back(refs, sums)
    names = dict(vars(refs), dq=refs.dq_out, dkv=refs.dkv_out, grad_before=refs.grad_middle)
    for name in SUMS:
        names[name] = getattr(refs, name + END)
    for name in QKV:
        names[name + HERE] = getattr(refs, name + HERE_END)
    last_part(SimpleNamespace(**names), copies)


def last_part(refs, copies):
    mirror = mirror_peer()
    high = pl.ds(HALF, HALF)
    spreads = [
        Spread(copies, refs.red_a, refs.sum_a0),
        Spread(copies, refs.red_b, refs.sum_b1),
    ]

    def first():
        for spread in spreads:
            spread.start()

    def second():
        for spread in spreads:
            spread.second()

    grad, sent = sum_and_project_back(
        refs, copies, refs.tokens[...].astype(WIDE), gain_row(refs.gains, 0), first, second
    )
    wait_all(sent)
    grads_b(refs.grads_low, refs.normed_pair, refs.grad_qkv_pair, refs.attn_gain_pair)
    reduce = Reduce(
        copies, refs.grads_low, refs.one, refs.sum_one, refs.two, refs.three, refs.red
    )
    reduce.start()
    refs.grad[...] = grad
    refs.grad_out[0:HALF] = grad[0:HALF]
    refs.acts_out[0:HALF] = refs.acts[0:HALF]
    rows = [
        copies.remote(refs.grad.at[high], refs.grad_out.at[high], mirror),
        copies.remote(refs.acts.at[high], refs.acts_out.at[high], mirror),
    ]
    reduce.second()
    reduce.third()
    reduce.finish()
    last = Spread(copies, refs.red, refs.sum_b0)
    last.start()
    last.second()
    wait_all(rows)
    for spread in [*spreads, last]:
        spread.finish()


def results_kernel(
    acts, grads, a0, a1, b0, b1, acts_t, grads_t, ga, wq, wk, wv, wo, gm, wg, wu, wd
):
    wide = jnp.float32
    acts_t[...] = acts[...].astype(wide).T.astype(acts_t.dtype)
    grads_t[...] = grads[...].T
    for layer, (a, b) in enumerate(((a0, b0), (a1, b1))):
        wg[layer] = a[0:288, :].astype(wide)
        wu[layer] = a[288:576, :].astype(wide)
        wd[layer, 0:288] = a[576:864, 0:768].astype(wide)
        wd[layer, 288:576] = a[576:864, 768:1536].astype(wide)
        wo[layer, 0:144] = a[864:1008, 0:576].astype(wide)
        wo[layer, 144:288] = a[864:1008, 640:1216].astype(wide)
        gm[layer : layer + 1, :] = a[1008:1024, 0:288].astype(wide)[0:1]
        wq[layer, 0:144] = b[0:144, 0:576].astype(wide)
        wq[layer, 144:288] = b[0:144, 640:1216].astype(wide)
        for at in range(3):
            rows = slice(at * 96, at * 96 + 96)
            wk[layer, rows] = b[144:240, at * 384 : at * 384 + 192].astype(wide)
            wv[layer, rows] = b[144:240, at * 384 + 192 : at * 384 + 384].astype(wide)
        ga[layer : layer + 1, :] = b[240:256, 0:288].astype(wide)[0:1]


def results(*args):
    shapes = [
        (2, 288),
        (2, 288, 576),
        (2, 288, 192),
        (2, 288, 192),
        (2, 288, 576),
        (2, 288),
        (2, 288, 1536),
        (2, 288, 1536),
        (2, 576, 768),
    ]
    acts, grads, *gradients, down = pl.pallas_call(
        results_kernel,
        out_shape=[
            shape_of((MODEL_WIDTH, 128), jnp.bfloat16),
            shape_of((MODEL_WIDTH, 128), jnp.float32),
            *[shape_of(shape, jnp.float32) for shape in shapes],
        ],
        in_specs=[VMEM] * 6,
        out_specs=[VMEM] * 11,
        compiler_params=pltpu.CompilerParams(vmem_limit_bytes=56 << 20),
        name="results",
    )(*args)
    return (acts.T, grads.T, *gradients, down.transpose(0, 2, 1))


def attend_back(refs, sums):
    q_ref, kv_ref, do_ref = refs.queries_in, refs.kv_in, refs.grads_all
    stats_ref, starts_ref, bias = refs.stats_all, refs.starts, refs.bias_back
    dq, dkv = refs.dq_total, refs.dkv_total
    dq[...] = jnp.zeros(dq.shape, jnp.float32)
    dkv[...] = jnp.zeros(dkv.shape, jnp.float32)

    def step_body(step, carry):
        section, quarter = unit_places(step)
        bias[...] = unit_bias(section, quarter, starts_ref)
        lane = lax.broadcasted_iota(jnp.int32, (1, 128), 1)
        stats = jnp.where(lane < HALF, stats_ref[quarter], stats_ref[3 - quarter])
        for group in range(3):
            queries = head_rows(q_ref, quarter, group)
            grads = head_rows(do_ref, quarter, group)
            keys = kv_ref[section, :, group * 128 : group * 128 + 64]
            values = kv_ref[section, :, group * 128 + 64 : group * 128 + 128]
            heads = range(3 * group, 3 * group + 3)
            logs = jnp.concatenate([stats[0, h : h + 1, :] for h in heads], axis=1)
            delta = jnp.concatenate([stats[1, h : h + 1, :] for h in heads], axis=1)
            scores = contract(keys, queries, 1, 1)
            tile = bias[...]
            scores = scores + jnp.concatenate([tile, tile, tile], axis=1)
            weights = jnp.exp(scores - logs)
            grad_weights = contract(values, grads, 1, 1)
            grad_scores = (weights * (grad_weights - delta)).astype(jnp.bfloat16)
            grad_values = contract(weights.astype(jnp.bfloat16), grads, 1, 0)
            grad_keys = contract(grad_scores, queries, 1, 0)
            dkv[section, group] += jnp.concatenate([grad_keys, grad_values], axis=1)
            dq[quarter, group] += contract(keys, grad_scores, 0, 0)
        @pl.when(step == 2)
        def _():
            for item in sums:
                item.second()

        @pl.when(step == 3)
        def _():
            for item in sums:
                item.third()

        return carry

    lax.fori_loop(0, 5, step_body, 0)
    lane = lax.broadcasted_iota(jnp.int32, (1, 128), 1)
    for chunk in range(4):
        for head in range(QUERY_HEADS):
            group, part = head // 3, slice((head % 3) * 128, (head % 3) * 128 + 128)
            picked = jnp.where(
                lane < HALF, dq[chunk, group][:, part], dq[3 - chunk, group][:, part]
            )
            refs.dq_out[chunk, head * 64 : head * 64 + 64, :] = (picked * 0.125).astype(jnp.bfloat16)
    for section in range(2):
        for group in range(3):
            refs.dkv_out[section, :, :, :, group * 128 : group * 128 + 128] = (
                dkv[section, group].astype(jnp.bfloat16).reshape(4, 4, HALF, 128)
            )
    for item in sums:
        item.finish()


SUM_SCRATCH = ("one", "sum_one", "two", "three")


def reduce_refs(rows, tail):
    names = [name + tail for name in SUM_SCRATCH]
    shapes = [(3, 3, rows, 128), (3, rows, 128), (3, 3, rows // 4, 128), (3, 4, rows // 4, 128)]
    return {name: (shape, jnp.bfloat16) for name, shape in zip(names, shapes)}


def reduce_of(refs, copies, source, target, tail):
    return Reduce(
        copies, source, *[getattr(refs, name + tail) for name in SUM_SCRATCH], target
    )


def sequence_starts(lengths, rows):
    ends = jnp.cumsum(lengths)
    begins = ends - lengths
    segment = jnp.sum((rows[..., None] >= ends).astype(jnp.int32), axis=-1)
    labels = jnp.arange(lengths.shape[0], dtype=jnp.int32)
    return jnp.sum(jnp.where(segment[..., None] == labels, begins, 0), axis=-1)


def rope_tables(position):
    half = HEAD_SIZE // 2
    freqs = jnp.exp(jnp.arange(half, dtype=jnp.float32) * (-2.0 * math.log(10000.0) / HEAD_SIZE))
    angles = position.astype(jnp.float32)[:, None] * freqs[None, :]
    return jnp.cos(angles), jnp.sin(angles)


def per_device(
    tokens,
    seq_lengths,
    attn_gain,
    w_query,
    key_weight,
    value_weight,
    w_out,
    mlp_gain,
    w_gate,
    w_up,
    w_down,
    cotangent,
):
    lengths = seq_lengths[0]
    rep = lax.axis_index("rep")
    x, line = rep // 16, rep % 16
    inside = jnp.arange(128, dtype=jnp.int32)
    chunk = jnp.arange(4, dtype=jnp.int32)[:, None] * 16 + line
    rows_all = jnp.where(
        inside[None, :] < HALF,
        chunk * 128 + inside[None, :],
        (127 - 2 * chunk) * HALF + inside[None, :] - HALF,
    )
    starts = sequence_starts(lengths, rows_all)
    position = jnp.where(
        inside < HALF, rep * 128 + inside, (127 - 2 * rep) * HALF + inside - HALF
    ) - sequence_starts(
        lengths,
        jnp.where(inside < HALF, rep * 128 + inside, (127 - 2 * rep) * HALF + inside - HALF),
    )
    cosine, sine = rope_tables(position)
    cosine = jnp.concatenate([cosine] * 4, axis=1)
    sine = jnp.concatenate([-sine, sine] * 2, axis=1)
    tables = dict(cosine=(cosine, VMEM), sine=(sine, VMEM))
    gains = jnp.pad(jnp.concatenate([attn_gain, mlp_gain]), ((0, 12), (0, 96)))
    params = dict(zip(WEIGHTS, (w_query, key_weight, value_weight, w_out, w_gate, w_up, w_down.transpose(0, 2, 1))))
    raw = {name: (value, ANY) for name, value in params.items()}
    sources = dict(queries=((128, 576), LOW), kv=((128, 384), LOW))

    def kept_weights(result, names):
        return {name + LOWER: (getattr(result, name + ALL), ANY) for name in names}

    def kept_rows(result, names):
        return {name: (getattr(result, name), VMEM) for name in names}

    zero = named_call(
        start_body,
        "start",
        0,
        dict(
            tokens=(tokens.T, VMEM),
            cotangent=(cotangent.T, VMEM),
            gains=(gains, VMEM),
            **tables,
            **raw,
        ),
        dict(
            tokens_out=((128, 576), LOW, VMEM),
            cotangent_out=((128, 576), LOW, VMEM),
            gains_out=((2, 16, 384), LOW, VMEM),
            **gather_outs(),
            **weight_outs(),
        ),
        dict(
            **sources,
            **weight_stages(),
            **weight_loads(QKV),
            token_rows=((128, 576), LOW),
            cotangent_rows=((128, 576), LOW),
        ),
    )
    gains = (zero.gains_out, VMEM)
    tokens = (zero.tokens_out, VMEM)
    one = named_call(
        between_body,
        "between",
        1,
        dict(
            queries_in=(zero.queries_all, VMEM),
            kv_in=(zero.kv_all.reshape(2, 1024, 384), VMEM),
            starts=(starts, VMEM),
            tokens=tokens,
            gains=gains,
            **tables,
            **raw,
            **kept_weights(zero, LATER),
        ),
        dict(
            hidden=((128, 576), WIDE, VMEM),
            **{name: (*kind, VMEM) for name, kind in FEED.items()},
            **gather_outs(),
            **weight_outs(),
        ),
        {**sources, **ATTEND, **PARTIALS, **weight_stages(), **weight_loads([*QKV, *LATER])},
    )
    back_one = named_call(
        turn_body,
        "turn",
        2,
        dict(
            queries_in=(one.queries_all, VMEM),
            kv_in=(one.kv_all.reshape(2, 1024, 384), VMEM),
            starts=(starts, VMEM),
            hidden=(one.hidden, VMEM),
            cotangent=(zero.cotangent_out, VMEM),
            gains=gains,
            normed=(one.normed, VMEM),
            **kept_weights(one, LATER),
        ),
        dict(activations=((128, 576), LOW, VMEM), **BACK_OUTS),
        {**FEED, **ATTEND, **PARTIALS, **BACK_SCRATCH, **reduce_refs(ROWS_A, TAIL_A), **weight_loads(LATER)},
    )
    end = named_call(
        down_body,
        "down",
        3,
        dict(
            dq=(back_one.dq_out, VMEM),
            dkv=(back_one.dkv_out, VMEM),
            queries_in=(zero.queries_all, VMEM),
            kv_in=(zero.kv_all.reshape(2, 1024, 384), VMEM),
            starts=(starts, VMEM),
            hidden=(one.hidden, VMEM),
            grad_before=(back_one.grad_middle, VMEM),
            gains=gains,
            normed=(zero.normed, VMEM),
            normed_above=(back_one.normed_pair, VMEM),
            red_above=(back_one.red_a, VMEM),
            tokens=tokens,
            acts=(back_one.activations, VMEM),
            **tables,
            **kept_rows(one, FEED),
            **kept_weights(one, QKV),
            **kept_weights(zero, LATER),
            **{name + END: (getattr(zero, name + ALL), ANY) for name in QKV},
        ),
        dict(
            sum_a1=((ROWS_A, 1536), LOW, VMEM),
            acts_out=((128, 576), LOW, VMEM),
            grad_out=((128, 576), WIDE, VMEM),
            sum_a0=((ROWS_A, 1536), LOW, VMEM),
            sum_b1=((ROWS_B, 1536), LOW, VMEM),
            sum_b0=((ROWS_B, 1536), LOW, VMEM),
        ),
        dict(
            **SUMS,
            **{name + END: kind for name, kind in SUMS.items()},
            **{name: kind[:2] for name, kind in BACK_OUTS.items()},
            **BACK_SCRATCH,
            **reduce_refs(ROWS_A, TAIL_A),
            **reduce_refs(ROWS_B, TAIL_B),
            **weight_loads([*QKV, *LATER]),
            **{name + HERE_END: (whole_shape(name), LOW) for name in QKV},
            grads_b=((ROWS_B, 1536), LOW),
            red_b=((3, ROWS_B // 4, 128), LOW),
            grad=((128, 576), WIDE),
            grads_low=((ROWS_B, 1536), LOW),
            one=((3, 3, ROWS_B, 128), LOW),
            sum_one=((3, ROWS_B, 128), LOW),
            two=((3, 3, ROWS_B // 4, 128), LOW),
            three=((3, 4, ROWS_B // 4, 128), LOW),
            red=((3, ROWS_B // 4, 128), LOW),
        ),
    )
    return results(
        end.acts_out, end.grad_out, end.sum_a0, end.sum_a1, end.sum_b0, end.sum_b1
    )


def solution(mesh):
    rows = P(("shard", "rep"), None)
    gain, weight = P(None, "shard"), P(None, "shard", None)
    return jax.shard_map(
        per_device,
        mesh=mesh,
        in_specs=(
            rows,
            P("shard", None),
            gain,
            weight,
            weight,
            weight,
            weight,
            gain,
            weight,
            weight,
            weight,
            rows,
        ),
        out_specs=(
            rows,
            rows,
            gain,
            weight,
            weight,
            weight,
            weight,
            gain,
            weight,
            weight,
            weight,
        ),
        check_vma=False,
    )
```
